256 devices in a mesh: dp: 4 (over z_hi, core), seq: 64 (over x, z_lo, y).
Axes of the slice: x: 4, y: 4, z: 8 (z_hi: 2, z_lo: 4; z = z_hi * 4 + z_lo), core: 2. Of those that a mesh axis runs over, the one named last changes fastest.
Arguments:
- inputs: bfloat16 [4, 8192, 1536], P('dp', 'seq'), may hold values from -16 to 16
- out_grad: bfloat16 [4, 8192, 1536], P('dp', 'seq'), may hold values from -16 to 16
- conv_weight: bfloat16 [3, 1536, 768], P(None, 'dp'), may hold values from -0.09375 to 0.09375
- point_weight: bfloat16 [768, 1536], P('dp'), may hold values from -0.21875 to 0.21875
Outputs:
- in_grad: bfloat16 [4, 8192, 1536], P('dp', 'seq')
- conv_grad: float32 [3, 1536, 768], P(None, ('dp', 'seq'))
- point_grad: float32 [768, 1536], P(('dp', 'seq'))
The draws below stay inside these ranges and needn't reach their ends.
All inputs are finite; a program needn't handle non-finite values.
Results may differ from the reference program's by a relative error of at most 0.0065.
Values may be sent and summed in bfloat16 or wider, within the bound.
No kernel may reach another device: no remote copies, remote signals or barrier semaphores. Data moves between devices by JAX's collectives and lax.ppermute only.
A program may use at most 64 MiB of HBM per device.

```python
import jax
import jax.numpy as jnp
from jax import lax

C = 1536
H = 768
DILATION_STEP = 1024
LENGTH = 8192
BATCH = 4


def raised(entries, own_key, source, target, parts, factor):
    owner, partner = [(jnp.arange(entries.shape[axis_at]) // (entries.shape[axis_at] // parts)).reshape([-1 if axis == axis_at else 1 for axis in range(entries.ndim)]) for axis_at in (source, target)]
    chosen = jax.random.permutation(own_key, parts)[partner]
    strong = (owner == chosen) | (owner == (partner + parts // 2) % parts)
    return jnp.where(strong, factor * entries, entries)


def shard_levels(own_key, extent, cuts, smallest, largest):
    level = 1.0
    for dim, blocks in cuts:
        heights = jax.random.uniform(jax.random.fold_in(jax.random.fold_in(own_key, 6), dim), (blocks,), jnp.float32, smallest / len(cuts), largest / len(cuts))
        level = level * jnp.repeat(jnp.exp(heights), extent[dim] // blocks).reshape((-1,) + (1,) * (len(extent) - 1 - dim))
    return level


def noise(own_key, dims, spread, most, cuts=(), kind=jnp.bfloat16):
    result = spread * jax.random.normal(own_key, dims, jnp.float32)
    if cuts:
        result = result * shard_levels(own_key, dims, cuts, -0.22, 0.18)
    return jnp.clip(result, -most, most).astype(kind)


def noise_with(own_key, dims, deviation, reach, shards, heavy, kind=jnp.bfloat16):
    drawn = deviation * jax.random.normal(own_key, dims, jnp.float32)
    if shards:
        drawn = drawn * shard_levels(own_key, dims, shards, -0.22, 0.18)
    return jnp.clip(raised(drawn, jax.random.fold_in(own_key, 3), *heavy), -reach, reach).astype(kind)


def setup_inputs(seed: int = 0) -> dict:
    seeds = jax.random.split(jax.random.key(seed), 5)
    inputs = noise_with(seeds[0], (BATCH, LENGTH, C), 1.0, 16.0, ((0, 4), (1, 64)), (1, 2, 64, 4.0))
    out_grad = noise_with(seeds[1], (BATCH, LENGTH, C), 1.0, 16.0, ((0, 4), (1, 64)), (1, 2, 64, 4.0))
    conv_weight = noise(seeds[2], (3, C, H), (3 * C) ** -0.5, 0.09375, ((1, 4),))
    point_weight = noise(seeds[3], (H, C), H ** -0.5, 0.21875, ((0, 4),))
    return {"inputs": inputs, "out_grad": out_grad, "conv_weight": conv_weight, "point_weight": point_weight}


def shifted_pair(position_rows):
    zero_padding = jnp.zeros((DILATION_STEP, position_rows.shape[1]), position_rows.dtype)
    preceding_rows = jnp.concatenate([zero_padding, position_rows[:-DILATION_STEP]], axis=0)
    following_rows = jnp.concatenate([position_rows[DILATION_STEP:], zero_padding], axis=0)
    return (preceding_rows, following_rows)

def one_sequence(inputs_row, grad_row, conv_weight, point_weight):
    preceding_rows, following_rows = shifted_pair(inputs_row)
    pre = jnp.dot(preceding_rows, conv_weight[0], preferred_element_type=jnp.float32)
    pre = pre + jnp.dot(inputs_row, conv_weight[1], preferred_element_type=jnp.float32)
    pre = pre + jnp.dot(following_rows, conv_weight[2], preferred_element_type=jnp.float32)
    gelu_out, pull = jax.vjp(jax.nn.gelu, pre)
    hidden = gelu_out.astype(jnp.bfloat16)
    hidden_input = jnp.dot(grad_row, point_weight.T, preferred_element_type=jnp.float32)
    hidden_grad = pull(hidden_input)[0].astype(jnp.bfloat16)
    grad_earlier, grad_later = shifted_pair(hidden_grad)
    total = grad_row.astype(jnp.float32)
    total = total + jnp.dot(grad_later, conv_weight[0].T, preferred_element_type=jnp.float32)
    total = total + jnp.dot(hidden_grad, conv_weight[1].T, preferred_element_type=jnp.float32)
    total = total + jnp.dot(grad_earlier, conv_weight[2].T, preferred_element_type=jnp.float32)
    in_grad = total.astype(jnp.bfloat16)
    conv_grad = jnp.stack([jnp.dot(part.T, hidden_grad, preferred_element_type=jnp.float32) for part in (preceding_rows, inputs_row, following_rows)])
    point_grad = jnp.dot(hidden.T, grad_row, preferred_element_type=jnp.float32)
    return (in_grad, conv_grad, point_grad)

def reference(inputs, out_grad, conv_weight, point_weight):

    def step(carry, pair):
        in_grad, conv_grad, point_grad = one_sequence(pair[0], pair[1], conv_weight, point_weight)
        return ((carry[0] + conv_grad, carry[1] + point_grad), in_grad)
    start = (jnp.zeros((3, C, H), jnp.float32), jnp.zeros((H, C), jnp.float32))
    sums, in_grad = lax.scan(step, start, (inputs, out_grad))
    return (in_grad, sums[0], sums[1])
```

```python
import jax
import jax.numpy as jnp
from jax import lax
from jax.sharding import PartitionSpec as P

DILATION_STEP = 1024
BF16 = jnp.bfloat16
F32 = jnp.float32


def coords(index):
    dp, seq = divmod(index, 64)
    return seq // 16, seq % 4, (dp // 2) * 4 + (seq // 4) % 4, dp % 2


def index_of(x, y, z, core):
    return ((z % 8) // 4 * 2 + core % 2) * 64 + (x % 4) * 16 + (z % 4) * 4 + y % 4


def send(value, target):
    pairs = [(device, index_of(*target(*coords(device)))) for device in range(256)]
    return lax.ppermute(value, ("dp", "seq"), pairs)


def send_core(value):
    return send(value, lambda x, y, z, c: (x, y, z, 1 - c))


def send_z(value, steps):
    return send(value, lambda x, y, z, c: (x, y, z + steps, c))


def send_a(value, steps):
    return send(value, lambda x, y, z, c: (x + steps * (1 - c), y + steps * c, z, c))


def send_b(value, steps):
    return send(value, lambda x, y, z, c: (x + steps * c, y + steps * (1 - c), z, c))


def shifted(value, steps):
    first, last = (max(0, -steps), min(64, 64 - steps))
    return lax.ppermute(value, "seq", [(source, source + steps) for source in range(first, last)])


def dot(left, right, dims):
    return lax.dot_general(left, right, ((dims[:1], dims[1:]), ((), ())), preferred_element_type=F32)


def pick(value, axis, index):
    return lax.dynamic_index_in_dim(value, index, axis, keepdims=False)


def gather_ring(piece, mover, place):
    whole = jnp.zeros((4,) + piece.shape, piece.dtype)
    parts = [(place, piece)] + [((place + k) % 4, mover(piece, -k)) for k in (1, 2, 3)]
    for at, part in parts:
        whole = lax.dynamic_update_index_in_dim(whole, part, at, 0)
    return whole


def order_matrix(width, span, core):
    unit = span // 64
    new = jnp.arange(width)
    block, inner = new // span, new % span
    a, b, zl, j = inner // (16 * unit), inner // (4 * unit) % 4, inner // unit % 4, inner % unit
    x, y = jnp.where(core == 0, a, b), jnp.where(core == 0, b, a)
    old = block * span + x * (16 * unit) + zl * (4 * unit) + y * unit + j
    return (jnp.arange(width)[:, None] == old[None, :]).astype(BF16)


def local(inputs, out_grad, conv_weight, point_weight):
    x, og = inputs[0], out_grad[0]
    rows, C = x.shape
    H = conv_weight.shape[2]
    Cq, Hq, Hh = C // 4, H // 4, H // 2
    hops = DILATION_STEP // rows
    dp, seq = lax.axis_index("dp"), lax.axis_index("seq")
    zh, core = dp // 2, dp % 2
    xi, zl, yi = seq // 16, seq // 4 % 4, seq % 4
    z = zh * 4 + zl
    a, b = jnp.where(core == 0, xi, yi), jnp.where(core == 0, yi, xi)

    def columns(c):
        return jnp.concatenate(
            [lax.dynamic_slice_in_dim(conv_weight, half * 2 * Hq + c * Hq, Hq, 2) for half in (0, 1)], axis=2
        )

    mine, theirs = columns(core), columns(1 - core)
    got = send_core(theirs)
    near = jnp.where(core == 0, jnp.stack([mine, got], 1), jnp.stack([got, mine], 1)).reshape(3, 2 * Cq, Hh)
    at = a * 4 + b
    conv_piece = pick(near.reshape(3, 16, Cq // 8, Hh), 1, at).reshape(-1, Hh)
    point_piece = pick(point_weight.reshape(16, Hq // 16, C), 0, at).reshape(-1, Hh)
    n_conv = conv_piece.shape[0]
    far = send_z(jnp.concatenate([conv_piece, point_piece]), 4)
    far = gather_ring(far, send_a, a)
    far = gather_ring(far, send_b, b)
    far_conv = far[:, :, :n_conv].reshape(4, 4, 3, Cq // 8, Hh).transpose(2, 1, 0, 3, 4).reshape(3, 2 * Cq, Hh)
    far_point = far[:, :, n_conv:].reshape(4, 4, Hq // 16, C).transpose(1, 0, 2, 3).reshape(Hq, C)

    def halves(first, second, axis):
        return jnp.where(zh == 0, jnp.concatenate([first, second], axis), jnp.concatenate([second, first], axis))

    W = halves(near, far_conv, 1)
    PW = halves(point_weight, far_point, 0)

    x_taps = jnp.stack([shifted(x, hops), x, shifted(x, -hops)])
    x_taps = jnp.concatenate([x_taps, jnp.stack([send_core(x_taps[k]) for k in range(3)])], 1)
    og2 = jnp.concatenate([og, send_core(og)])

    pre = sum(dot(x_taps[k], W[k], (1, 0)) for k in (1, 0, 2))
    gelu_out, pull = jax.vjp(jax.nn.gelu, pre)
    hidden = gelu_out.astype(BF16)
    hg = pull(dot(og2, PW, (1, 1)))[0].astype(BF16)
    later, earlier = shifted(hg, -hops), shifted(hg, hops)

    x_flat = jnp.concatenate([x_taps[0], x_taps[1], x_taps[2]], 0)
    x_flat = dot(x_flat, order_matrix(C, Cq, core), (1, 0)).astype(BF16).reshape(3, 2 * rows, C)
    hidden = dot(hidden, order_matrix(Hh, Hq, core), (1, 0)).astype(BF16)
    conv = jnp.stack([dot(x_flat[k], hg, (0, 0)) for k in range(3)]).reshape(3, 4, 4, Cq // 4, Hh)
    point = dot(hidden, og2, (0, 0)).reshape(2, 4, Hq // 4, C // Hh, Hh).transpose(3, 0, 1, 2, 4)

    def reduce_ring(conv, point, mover, place):
        def chunk(k):
            at = (place + k) % 4
            return jnp.concatenate([pick(conv, 2, at).reshape(-1, Hh), pick(point, 2, at).reshape(-1, Hh)])

        total = chunk(0)
        for k in (1, 2, 3):
            total = total + mover(chunk(k).astype(BF16), k).astype(F32)
        return total

    total = reduce_ring(conv, point, send_a, a)
    n = 12 * (Cq // 4)
    conv = total[:n].reshape(3, 4, 4, Cq // 16, Hh)
    point = total[n:].reshape(C // Hh, 2, 4, Hq // 16, Hh)
    total = reduce_ring(conv, point, send_b, b)
    n = 12 * (Cq // 16)
    conv = total[:n].reshape(3, 2, 2, 4, Cq // 64, Hh).transpose(1, 3, 0, 2, 4, 5).reshape(8, -1, Hh)
    point = total[n:].reshape(C // Hh, 2, 4, Hq // 64, Hh).transpose(1, 2, 0, 3, 4).reshape(8, -1, Hh)
    by_z = jnp.concatenate([conv, point], 1)
    last = pick(by_z, 0, z)
    for k in range(1, 8):
        last = last + send_z(pick(by_z, 0, (z + k) % 8).astype(BF16), k).astype(F32)
    n = conv.shape[1]
    conv = last[:n].reshape(3, 2, Cq // 64, Hh)
    point_mine = last[n:].reshape(C // Hh, Hq // 64, Hh).transpose(1, 0, 2).reshape(Hq // 64, C)
    kept, swapped = pick(conv, 1, core), send_core(pick(conv, 1, 1 - core))
    kept, swapped = (part.reshape(3, Cq // 64, 2, 1, Hq) for part in (kept, swapped))
    conv_mine = jnp.where(
        core == 0, jnp.concatenate([kept, swapped], 3), jnp.concatenate([swapped, kept], 3)
    ).reshape(3, Cq // 64, H)

    partial = dot(hg, W[1], (1, 1)) + dot(later, W[0], (1, 1)) + dot(earlier, W[2], (1, 1))
    total = og.astype(F32) + partial[:rows] + send_core(partial[rows:])
    return total.astype(BF16)[None], conv_mine, point_mine


def solution(mesh):
    placed = (P("dp", "seq", None), P("dp", "seq", None), P(None, "dp", None), P("dp", None))
    return jax.shard_map(
        local,
        mesh=mesh,
        in_specs=placed,
        out_specs=(P("dp", "seq", None), P(None, ("dp", "seq"), None), P(("dp", "seq"), None)),
        check_vma=False,
    )
```

```python
import jax
import jax.numpy as jnp
from jax import lax
from jax.experimental import pallas as pl
from jax.experimental.pallas import tpu as pltpu
from jax.sharding import PartitionSpec as P

DILATION_STEP = 1024
BF16 = jnp.bfloat16
F32 = jnp.float32


def coords(index):
    dp, seq = divmod(index, 64)
    return seq // 16, seq % 4, (dp // 2) * 4 + (seq // 4) % 4, dp % 2


def index_of(x, y, z, core):
    return ((z % 8) // 4 * 2 + core % 2) * 64 + (x % 4) * 16 + (z % 4) * 4 + y % 4


def send(value, target, sources=range(256)):
    pairs = [(device, index_of(*target(*coords(device)))) for device in sources]
    return lax.ppermute(value, ("dp", "seq"), pairs)


def send_a(value, steps):
    return send(value, lambda x, y, z, c: (x + steps * (1 - c), y + steps * c, z, c))


def send_b(value, steps):
    return send(value, lambda x, y, z, c: (x + steps * c, y + steps * (1 - c), z, c))


def shifted(value, steps):
    first, last = (max(0, -steps), min(64, 64 - steps))
    return lax.ppermute(value, "seq", [(source, source + steps) for source in range(first, last)])


def dot(left, right, dims):
    return lax.dot_general(left, right, ((dims[:1], dims[1:]), ((), ())), preferred_element_type=F32)


def pick(value, axis, index):
    return lax.dynamic_index_in_dim(value, index, axis, keepdims=False)


def run(kernel, scalars, arrays, outs, scratch=(), flops=0):
    vmem = pl.BlockSpec(memory_space=pltpu.VMEM)
    held = sum(v.size * v.dtype.itemsize for v in arrays)
    made = sum(o.size * o.dtype.itemsize for o in outs)
    return pl.pallas_call(
        kernel,
        out_shape=outs,
        in_specs=[pl.BlockSpec(memory_space=pltpu.SMEM)] + [vmem] * len(arrays),
        out_specs=[vmem] * len(outs),
        scratch_shapes=scratch,
        compiler_params=pltpu.CompilerParams(vmem_limit_bytes=48 * 1024 * 1024),
        cost_estimate=pl.CostEstimate(flops=flops, bytes_accessed=held + made, transcendentals=0),
    )(scalars, *arrays)


def shape(dims, dtype):
    return jax.ShapeDtypeStruct(tuple(dims), dtype)


def lanes(start, size):
    return pl.ds(pl.multiple_of(start * size, size), size)


def forward_kernel(meta, x0, x0o, x1, x1o, x2, x2o, og, ogo, mine, got, pw, far0, far1, far2, far3, order,
                   hg, hidden_t, taps, ogs, wfar, pws):
    core, zh, a, b = (meta[i] for i in range(4))
    rows = x0.shape[0]
    for k, (own, other) in enumerate(((x0, x0o), (x1, x1o), (x2, x2o))):
        taps[k, :rows] = own[...]
        taps[k, rows:] = other[...]
    ogs[:rows] = og[...]
    ogs[rows:] = ogo[...]
    piece, width = far0.shape[2:]
    for y in range(4):
        pws[y, zh] = pw[:, y * width:(y + 1) * width].reshape(4, piece, width)
    for j, far in enumerate((far0, far1, far2, far3)):
        for k in range(4):
            ak, bj = lax.rem(a + k, 4), lax.rem(b + j, 4)
            x, y = jnp.where(core == 0, ak, bj), jnp.where(core == 0, bj, ak)
            for t in range(3):
                wfar[t, x * 4 + y] = far[k, t]
            pws[y, 1 - zh, x] = far[k, 3]
    quarter = mine.shape[1]
    d = zh * 2 + core
    pre = jnp.zeros((2 * rows, width), F32)
    for t in range(3):
        pre += dot(taps[t, :, lanes(d, quarter)], mine[t], (1, 0))
        pre += dot(taps[t, :, lanes(zh * 2 + 1 - core, quarter)], got[t], (1, 0))
        pre += dot(taps[t, :, lanes(1 - zh, 2 * quarter)], wfar[t].reshape(2 * quarter, width), (1, 0))
    arriving = jnp.zeros((2 * rows, width), F32)
    for y in range(4):
        arriving += dot(ogs[:, y * width:(y + 1) * width], pws[y].reshape(width, width), (1, 1))
    scale, cubic = 0.7978845608028654, 0.044715
    square = pre * pre
    tanh = jnp.tanh(scale * (pre + cubic * (square * pre)))
    half = 0.5 * (1.0 + tanh)
    slope = half + 0.5 * pre * (1.0 - tanh * tanh) * (scale * (1.0 + 3.0 * cubic * square))
    hg[...] = (arriving * slope).astype(BF16)
    hidden_t[...] = dot(order[...], (pre * half).astype(BF16), (1, 1)).astype(BF16)


def gradient_kernel(meta, taps, ogs, hg, hidden_t, order, own, send1, send2, send3):
    core, zh = meta[0], meta[1]
    outs = (own, send1, send2, send3)
    both, width = hg.shape
    quarter = order.shape[0]
    unit, piece = quarter // 4, quarter // 16
    grads = hg[...]
    for u in range(2):
        moved = []
        for v in range(2):
            d = lax.rem(zh + u, 2) * 2 + lax.rem(core + v, 2)
            block = taps[:, :, lanes(d, quarter)].reshape(3 * both, quarter)
            moved.append(dot(order[...], block, (1, 1)).astype(BF16))
        for t in range(3):
            parts = [dot(m[:, t * both:(t + 1) * both], grads, (1, 0)) for m in moved]
            for r in range(4):
                for q in range(4):
                    at = r * unit + q * piece
                    pair = jnp.concatenate([p[at:at + piece] for p in parts], 0)
                    first = (t * 2 + u) * 2 * piece
                    outs[r][q, first:first + 2 * piece] = pair.astype(outs[r].dtype)
    unit = hidden_t.shape[0] // 4
    small = unit // 4
    base = 12 * piece
    for h in range(ogs.shape[1] // (2 * width)):
        parts = [dot(hidden_t[...], ogs[:, (2 * h + p) * width:(2 * h + p + 1) * width], (1, 0)) for p in range(2)]
        for r in range(4):
            for q in range(4):
                at = r * unit + q * small
                pair = jnp.concatenate([p[at:at + small] for p in parts], 0)
                first = base + h * 2 * small
                outs[r][q, first:first + 2 * small] = pair.astype(outs[r].dtype)


def reduce_kernel(meta, own, got1, got2, got3, kept, send1, send2, send3):
    for q, out in enumerate((kept, send1, send2, send3)):
        total = own[q] + got1[q].astype(F32) + got2[q].astype(F32) + got3[q].astype(F32)
        out[...] = total.astype(out.dtype)


def input_kernel(meta, hg, later, earlier, mine, got, wfar, kept, other):
    core, zh = meta[0], meta[1]
    quarter = mine.shape[1]
    rows = kept.shape[0]
    grads = (later[...], hg[...], earlier[...])
    for weights, at, size in ((mine, zh * 2 + core, quarter), (got, zh * 2 + 1 - core, quarter), (wfar, 1 - zh, 2 * quarter)):
        total = sum(dot(grads[t], weights[t], (1, 1)) for t in range(3))
        kept[:, lanes(at, size)] = total[:rows]
        other[:, lanes(at, size)] = total[rows:]


def local(inputs, out_grad, conv_weight, point_weight):
    x, og = inputs[0], out_grad[0]
    rows, C = x.shape
    H = conv_weight.shape[2]
    Cq, Hq, Hh = C // 4, H // 4, H // 2
    piece = C // 32
    hops = DILATION_STEP // rows
    dp, seq = lax.axis_index("dp"), lax.axis_index("seq")
    zh, core = dp // 2, dp % 2
    xi, zl, yi = seq // 16, seq // 4 % 4, seq % 4
    a, b = jnp.where(core == 0, xi, yi), jnp.where(core == 0, yi, xi)
    meta = jnp.stack([core, zh, a, b]).astype(jnp.int32)

    def columns(value, c):
        return jnp.concatenate(
            [lax.dynamic_slice_in_dim(value, half * 2 * Hq + c * Hq, Hq, 2) for half in (0, 1)], axis=2
        )

    at = xi * 4 + yi
    conv_piece = lax.dynamic_slice_in_dim(conv_weight, at % 8 * piece, piece, 1)
    point_piece = lax.dynamic_slice(point_weight, (xi * (Hq // 4), yi * Hh), (Hq // 4, Hh))
    holders = [d for d in range(256) if coords(d)[3] == coords(d)[0] // 2]

    def mirror(x, y, z, c):
        return x, y, 7 - z, c

    def partner(x, y, z, c):
        return x, y, z, 1 - c

    conv_piece = send(conv_piece, mirror, holders)
    point_piece = send(point_piece, mirror)
    prev, following = shifted(x, hops), shifted(x, -hops)
    conv_piece, point_piece, conv_weight, x_swap, og_swap = lax.optimization_barrier(
        (conv_piece, point_piece, conv_weight, x, og)
    )
    handed = send(columns(conv_piece, 1 - core), partner, holders)
    conv_piece = jnp.where(core == xi // 2, columns(conv_piece, core), handed)
    far = jnp.concatenate([conv_piece, point_piece[None]])
    far = jnp.stack([far] + [send_a(far, -k) for k in (1, 2, 3)])
    fars = [far] + [send_b(far, -k) for k in (1, 2, 3)]

    mine = columns(conv_weight, core)
    got = send(columns(conv_weight, 1 - core), partner)
    x_other, og_other = send(x_swap, partner), send(og_swap, partner)
    prev, following, fars[1] = lax.optimization_barrier((prev, following, fars[1]))
    prev_other, following_other = send(prev, partner), send(following, partner)

    def order(width, unit, count):
        new = jnp.arange(width)
        inner = new % (4 * unit)
        u = new // (4 * unit) % count
        r, q = new // (16 * unit * count), new // (4 * unit * count) % 4
        an, bn = (a + r) % 4, (b + q) % 4
        xn, yn = jnp.where(core == 0, an, bn), jnp.where(core == 0, bn, an)
        half = (zh + u) % 2 if count == 2 else 0
        old = half * (64 * unit) + xn * (16 * unit) + (zl + inner // unit) % 4 * (4 * unit) + yn * unit + inner % unit
        return (old[:, None] == jnp.arange(width)[None, :]).astype(BF16)

    hg, hidden_t, taps, ogs, wfar = run(
        forward_kernel,
        meta,
        [prev, prev_other, x, x_other, following, following_other, og, og_other, mine, got, point_weight, *fars,
         order(Hh, Hq // 64, 2)],
        [shape((2 * rows, Hh), BF16), shape((Hh, 2 * rows), BF16), shape((3, 2 * rows, C), BF16),
         shape((2 * rows, C), BF16), shape((3, 16, piece, Hh), BF16)],
        [pltpu.VMEM((4, 2, 4, Hq // 4, Hh), BF16)],
        flops=4 * 2 * 2 * rows * C * Hh,
    )
    later, earlier = shifted(hg, -hops), shifted(hg, hops)
    big = (4, 16 * piece // 2, Hh)
    own, *sends = run(
        gradient_kernel, meta, [taps, ogs, hg, hidden_t, order(Cq, Cq // 64, 1)],
        [shape(big, F32)] + [shape(big, BF16)] * 3,
        flops=4 * 2 * 2 * rows * C * Hh,
    )
    got_a = [send_a(part, k + 1) for k, part in enumerate(sends)]

    kept, other = run(
        input_kernel, meta, [hg, later, earlier, mine, got, wfar.reshape(3, 2 * Cq, Hh)],
        [shape((rows, C), F32)] * 2,
        flops=3 * 2 * 2 * rows * C * Hh,
    )
    in_grad = (og.astype(F32) + kept + send(other, partner)).astype(BF16)
    in_grad, *got_a = lax.optimization_barrier((in_grad, *got_a))

    own, *sends = run(reduce_kernel, meta, [own, *got_a], [shape(big[1:], F32)] + [shape(big[1:], BF16)] * 3)
    total = own
    for k, part in enumerate(sends):
        total = total + send_b(part, k + 1).astype(F32)
    n = 12 * (Cq // 16)
    conv = total[:n].reshape(3, 2, 2, 4, Cq // 64, Hh).transpose(3, 1, 0, 2, 4, 5).reshape(4, 2, -1, Hh)
    point = total[n:].reshape(C // Hh, 2, 4, Hq // 64, Hh).transpose(2, 1, 0, 3, 4).reshape(4, 2, -1, Hh)
    by_z = jnp.concatenate([conv, point], 2)
    last = by_z[0]
    for t in (1, 2, 3):
        got_z = send(by_z[t].astype(BF16), lambda x, y, z, c: (x, y, z // 4 * 4 + (z + t) % 4, c))
        last = last + got_z.astype(F32)
    last = last[0] + send(last[1].astype(BF16), lambda x, y, z, c: (x, y, z + 4, c)).astype(F32)
    n = conv.shape[2]
    conv = last[:n].reshape(3, 2, Cq // 64, Hh)
    point_mine = last[n:].reshape(C // Hh, Hq // 64, Hh).transpose(1, 0, 2).reshape(Hq // 64, C)
    kept, swapped = conv[:, 0], send(conv[:, 1], partner)
    kept, swapped = (part.reshape(3, Cq // 64, 2, 1, Hq) for part in (kept, swapped))
    conv_mine = jnp.where(
        core == 0, jnp.concatenate([kept, swapped], 3), jnp.concatenate([swapped, kept], 3)
    ).reshape(3, Cq // 64, H)
    return in_grad[None], conv_mine, point_mine


def solution(mesh):
    placed = (P("dp", "seq", None), P("dp", "seq", None), P(None, "dp", None), P("dp", None))
    return jax.shard_map(
        local,
        mesh=mesh,
        in_specs=placed,
        out_specs=(P("dp", "seq", None), P(None, ("dp", "seq"), None), P(("dp", "seq"), None)),
        check_vma=False,
    )
```

```python
import jax
import jax.numpy as jnp
from jax import lax
from jax.experimental import pallas as pl
from jax.experimental.pallas import tpu as pltpu
from jax.sharding import PartitionSpec as P

DILATION_STEP = 1024
BF16 = jnp.bfloat16
F32 = jnp.float32


def coords(index):
    dp, seq = divmod(index, 64)
    return seq // 16, seq % 4, (dp // 2) * 4 + (seq // 4) % 4, dp % 2


def index_of(x, y, z, core):
    return ((z % 8) // 4 * 2 + core % 2) * 64 + (x % 4) * 16 + (z % 4) * 4 + y % 4


def send(value, target, sources=range(256)):
    pairs = [(device, index_of(*target(*coords(device)))) for device in sources]
    return lax.ppermute(value, ("dp", "seq"), pairs)


def send_a(value, steps):
    return send(value, lambda x, y, z, c: (x + steps * (1 - c), y + steps * c, z, c))


def send_b(value, steps):
    return send(value, lambda x, y, z, c: (x + steps * c, y + steps * (1 - c), z, c))


def shifted(value, steps):
    first, last = (max(0, -steps), min(64, 64 - steps))
    return lax.ppermute(value, "seq", [(source, source + steps) for source in range(first, last)])


def dot(left, right, dims):
    return lax.dot_general(left, right, ((dims[:1], dims[1:]), ((), ())), preferred_element_type=F32)


def pick(value, axis, index):
    return lax.dynamic_index_in_dim(value, index, axis, keepdims=False)


def run(kernel, scalars, arrays, outs, scratch=()):
    vmem = pl.BlockSpec(memory_space=pltpu.VMEM)
    return pl.pallas_call(
        kernel,
        out_shape=outs,
        in_specs=[pl.BlockSpec(memory_space=pltpu.SMEM)] + [vmem] * len(arrays),
        out_specs=[vmem] * len(outs),
        scratch_shapes=scratch,
        compiler_params=pltpu.CompilerParams(vmem_limit_bytes=48 * 1024 * 1024),
        cost_estimate=pl.CostEstimate(flops=1, bytes_accessed=1, transcendentals=0),
    )(scalars, *arrays)


def shape(dims, dtype):
    return jax.ShapeDtypeStruct(tuple(dims), dtype)


def lanes(start, size):
    return pl.ds(pl.multiple_of(start * size, size), size)


def near_kernel(meta, x0, x0o, x1, x1o, og, ogo, mine, got, taps, ogs, pre):
    core, zh = meta[0], meta[1]
    rows, quarter = x0.shape[0], mine.shape[1]
    ogs[:rows] = og[...]
    ogs[rows:] = ogo[...]
    total = jnp.zeros(pre.shape, F32)
    for k, (own, other) in enumerate(((x0, x0o), (x1, x1o))):
        taps[k, :rows] = own[...]
        taps[k, rows:] = other[...]
        total += dot(taps[k, :, lanes(zh * 2 + core, quarter)], mine[k], (1, 0))
        total += dot(taps[k, :, lanes(zh * 2 + 1 - core, quarter)], got[k], (1, 0))
    pre[...] = total


def spread_block(meta, block, order, outs, first):
    core, zh = meta[0], meta[1]
    quarter = order.shape[0]
    unit = quarter // 4
    for u in range(2):
        for v in range(2):
            columns = lanes(lax.rem(zh + u, 2) * 2 + lax.rem(core + v, 2), quarter)
            moved = dot(order[...], block[:, columns], (1, 1)).astype(BF16)
            at = first + (u * 2 + v) * unit
            for r, out in enumerate(outs):
                out[at:at + unit] = moved[r * unit:(r + 1) * unit]


def centre_kernel(meta, x, xo, order, own, send1, send2, send3, both):
    rows = x.shape[0]
    both[:rows] = x[...]
    both[rows:] = xo[...]
    spread_block(meta, both, order, (own, send1, send2, send3), 0)


def spread_kernel(meta, taps, x2, x2o, order, tap2, own, send1, send2, send3):
    rows = x2.shape[0]
    tap2[:rows] = x2[...]
    tap2[rows:] = x2o[...]
    outs = (own, send1, send2, send3)
    spread_block(meta, taps.at[0], order, outs, 0)
    spread_block(meta, tap2, order, outs, own.shape[0] // 2)


def forward_kernel(meta, taps, tap2, ogs, near, mine, got, pw, far0, far1, far2, far3, order,
                   x0, x1, x2, x3, hg, hidden_t, wfar, m0, m1, m2, m3, pws):
    core, zh, a, b = (meta[i] for i in range(4))
    piece, width = far0.shape[2:]
    quarter = mine.shape[1]
    for y in range(4):
        pws[y, zh] = pw[:, y * width:(y + 1) * width].reshape(4, piece, width)
    for j, far in enumerate((far0, far1, far2, far3)):
        for k in range(4):
            ak, bj = lax.rem(a + k, 4), lax.rem(b + j, 4)
            x, y = jnp.where(core == 0, ak, bj), jnp.where(core == 0, bj, ak)
            for t in range(3):
                wfar[t, x * 4 + y] = far[k, t]
            pws[y, 1 - zh, x] = far[k, 3]
    pre = near[...]
    pre += dot(tap2[:, lanes(zh * 2 + core, quarter)], mine[2], (1, 0))
    pre += dot(tap2[:, lanes(zh * 2 + 1 - core, quarter)], got[2], (1, 0))
    for t in range(3):
        columns = lanes(1 - zh, 2 * quarter)
        block = tap2[:, columns] if t == 2 else taps[t, :, columns]
        pre += dot(block, wfar[t].reshape(2 * quarter, width), (1, 0))
    arriving = jnp.zeros(pre.shape, F32)
    for y in range(4):
        arriving += dot(ogs[:, y * width:(y + 1) * width], pws[y].reshape(width, width), (1, 1))
    scale, cubic = 0.7978845608028654, 0.044715
    square = pre * pre
    tanh = jnp.tanh(scale * (pre + cubic * (square * pre)))
    half = 0.5 * (1.0 + tanh)
    slope = half + 0.5 * pre * (1.0 - tanh * tanh) * (scale * (1.0 + 3.0 * cubic * square))
    grads = (arriving * slope).astype(BF16)
    hg[...] = grads
    count = x0.shape[0]
    place = [lax.broadcasted_iota(jnp.int32, (width, width), axis) for axis in (0, 1)]
    turned = dot((place[0] == place[1]).astype(BF16), grads, (1, 1)).astype(BF16)
    for x, message in ((x0, m0), (x1, m1), (x2, m2), (x3, m3)):
        message[:count] = x[...]
        message[count:] = turned
    hidden_t[...] = dot(order[...], (pre * half).astype(BF16), (1, 1)).astype(BF16)


def point_kernel(meta, ogs, hidden_t, own, send1, send2, send3):
    width = own.shape[2]
    unit = hidden_t.shape[0] // 4
    small = unit // 4
    for h in range(ogs.shape[1] // (2 * width)):
        parts = [dot(hidden_t[...], ogs[:, (2 * h + p) * width:(2 * h + p + 1) * width], (1, 0)) for p in range(2)]
        for r, out in enumerate((own, send1, send2, send3)):
            for q in range(4):
                at = r * unit + q * small
                pair = jnp.concatenate([p[at:at + small] for p in parts], 0)
                out[q, h * 2 * small:(h + 1) * 2 * small] = pair.astype(out.dtype)


def gradient_kernel(meta, x0, x1, x2, x3, m0, m1, m2, m3, conv):
    tap = x0.shape[0]
    total = [jnp.zeros((size, conv.shape[1]), F32) for size in (tap, 2 * tap)]
    for x, m in ((x0, m0), (x1, m1), (x2, m2), (x3, m3)):
        turned = m[2 * tap:]
        total[0] += dot(x[...], turned, (1, 1))
        total[1] += dot(m[:2 * tap], turned, (1, 1))
    conv[:tap] = total[1][:tap]
    conv[tap:2 * tap] = total[0]
    conv[2 * tap:] = total[1][tap:]


def pack_kernel(meta, conv, p0, p1, p2, p3, own, send1, send2, send3):
    unit = conv.shape[0] // 12
    piece = unit // 4
    for q, out in enumerate((own, send1, send2, send3)):
        for g in range(6):
            at = 2 * g * unit + q * piece
            pair = jnp.concatenate([conv[at:at + piece], conv[at + unit:at + unit + piece]], 0)
            out[g * 2 * piece:(g + 1) * 2 * piece] = pair.astype(out.dtype)
        point = p0[q] + p1[q].astype(F32) + p2[q].astype(F32) + p3[q].astype(F32)
        out[12 * piece:] = point.astype(out.dtype)


def input_kernel(meta, hg, later, earlier, mine, got, wfar, kept, other):
    core, zh = meta[0], meta[1]
    quarter = mine.shape[1]
    rows = kept.shape[0]
    grads = (later[...], hg[...], earlier[...])
    for weights, at, size in ((mine, zh * 2 + core, quarter), (got, zh * 2 + 1 - core, quarter), (wfar, 1 - zh, 2 * quarter)):
        total = sum(dot(grads[t], weights[t], (1, 1)) for t in range(3))
        kept[:, lanes(at, size)] = total[:rows]
        other[:, lanes(at, size)] = total[rows:]


def local(inputs, out_grad, conv_weight, point_weight):
    x, og = inputs[0], out_grad[0]
    rows, C = x.shape
    H = conv_weight.shape[2]
    Cq, Hq, Hh = C // 4, H // 4, H // 2
    piece = C // 32
    hops = DILATION_STEP // rows
    dp, seq = lax.axis_index("dp"), lax.axis_index("seq")
    zh, core = dp // 2, dp % 2
    xi, zl, yi = seq // 16, seq // 4 % 4, seq % 4
    a, b = jnp.where(core == 0, xi, yi), jnp.where(core == 0, yi, xi)
    meta = jnp.stack([core, zh, a, b]).astype(jnp.int32)

    def columns(value, c):
        return jnp.concatenate(
            [lax.dynamic_slice_in_dim(value, half * 2 * Hq + c * Hq, Hq, 2) for half in (0, 1)], axis=2
        )

    def order(width, unit, count):
        new = jnp.arange(width)
        inner = new % (4 * unit)
        u = new // (4 * unit) % count
        r, q = new // (16 * unit * count), new // (4 * unit * count) % 4
        an, bn = (a + r) % 4, (b + q) % 4
        xn, yn = jnp.where(core == 0, an, bn), jnp.where(core == 0, bn, an)
        half = (zh + u) % 2 if count == 2 else 0
        old = half * (64 * unit) + xn * (16 * unit) + (zl + inner // unit) % 4 * (4 * unit) + yn * unit + inner % unit
        return (old[:, None] == jnp.arange(width)[None, :]).astype(BF16)

    def mirror(x, y, z, c):
        return x, y, 7 - z, c

    def partner(x, y, z, c):
        return x, y, z, 1 - c

    def beside(first, second, axis):
        return jnp.where(core == 0, jnp.concatenate([first, second], axis), jnp.concatenate([second, first], axis))

    conv_piece = lax.dynamic_slice_in_dim(conv_weight, (xi * 4 + yi) % 8 * piece, piece, 1)
    point_piece = lax.dynamic_slice(point_weight, (xi * (Hq // 4), yi * Hh), (Hq // 4, Hh))
    holders = [d for d in range(256) if coords(d)[3] == coords(d)[0] // 2]
    point_piece = beside(point_piece, send(point_piece, partner), 1)
    far = send(jnp.concatenate([conv_piece, point_piece[None]]), mirror, holders)
    prev = shifted(x, hops)
    x_other = send(x, partner)
    spread = (Cq, 2 * rows)
    centre, *sends = run(
        centre_kernel, meta, [x, x_other, order(Cq, Cq // 64, 1)], [shape(spread, BF16)] * 4,
        [pltpu.VMEM((2 * rows, C), BF16)],
    )
    centres = [centre] + [send_a(part, k + 1) for k, part in enumerate(sends)]
    far, prev, conv_weight, x_late, og_late, *centres = lax.optimization_barrier(
        (far, prev, conv_weight, x, og, *centres)
    )

    def halves(c):
        return jnp.concatenate([columns(far[:3], c), lax.dynamic_slice_in_dim(far[3:], c * Hh, Hh, 2)])

    far = jnp.where(core == xi // 2, halves(core), send(halves(1 - core), partner, holders))
    mine = columns(conv_weight, core)
    got = send(columns(conv_weight, 1 - core), partner)
    prev_other, og_other = send(prev, partner), send(og_late, partner)
    following = shifted(x_late, -hops)
    fars = [send_a(far, -k) for k in (1, 2, 3)]
    far, prev_other, og_other, got, *fars = lax.optimization_barrier((far, prev_other, og_other, got, *fars))
    far = jnp.stack([far, *fars])
    fars = [far] + [send_b(far, -k) for k in (1, 2, 3)]
    taps, ogs, near = run(
        near_kernel, meta, [prev, prev_other, x, x_other, og, og_other, mine, got],
        [shape((2, 2 * rows, C), BF16), shape((2 * rows, C), BF16), shape((2 * rows, Hh), F32)],
    )
    taps, following, fars[1] = lax.optimization_barrier((taps, following, fars[1]))
    following_other = send(following, partner)
    spread = (2 * Cq, 2 * rows)
    tap2, *x_parts = run(
        spread_kernel, meta, [taps, following, following_other, order(Cq, Cq // 64, 1)],
        [shape((2 * rows, C), BF16)] + [shape(spread, BF16)] * 4,
    )
    hg, hidden_t, wfar, message, *sends = run(
        forward_kernel, meta,
        [taps, tap2, ogs, near, mine, got, point_weight, *fars, order(Hh, Hq // 64, 2), *x_parts],
        [shape((2 * rows, Hh), BF16), shape((Hh, 2 * rows), BF16), shape((3, 16, piece, Hh), BF16)]
        + [shape((2 * Cq + Hh, 2 * rows), BF16)] * 4,
        [pltpu.VMEM((4, 2, 4, Hq // 4, Hh), BF16)],
    )
    messages = [message] + [send_a(part, k + 1) for k, part in enumerate(sends)]
    block = (4, Hh // 4, Hh)
    p_own, *sends = run(point_kernel, meta, [ogs, hidden_t], [shape(block, F32)] + [shape(block, BF16)] * 3)
    p_all = [p_own] + [send_a(part, k + 1) for k, part in enumerate(sends)]
    later, earlier = shifted(hg, -hops), shifted(hg, hops)
    later, earlier, *messages = lax.optimization_barrier((later, earlier, *messages))
    conv, = run(gradient_kernel, meta, [*centres, *messages], [shape((3 * Cq, Hh), F32)])
    n = 12 * (Cq // 16)
    big = (n + Hh // 4, Hh)
    total, *sends = run(pack_kernel, meta, [conv, *p_all], [shape(big, F32)] + [shape(big, BF16)] * 3)
    hg_late, _ = lax.optimization_barrier((hg, total))

    kept, other = run(
        input_kernel, meta, [hg_late, later, earlier, mine, got, wfar.reshape(3, 2 * Cq, Hh)],
        [shape((rows, C), F32)] * 2,
    )
    in_grad = (og.astype(F32) + kept + send(other, partner)).astype(BF16)

    for k, part in enumerate(sends):
        total = total + send_b(part, k + 1).astype(F32)
    conv = total[:n].reshape(3, 2, 2, 4, Cq // 64, Hh).transpose(3, 1, 0, 2, 4, 5).reshape(4, 2, -1, Hh)
    point = total[n:].reshape(C // Hh, 2, 4, Hq // 64, Hh).transpose(2, 1, 0, 3, 4).reshape(4, 2, -1, Hh)
    by_z = jnp.concatenate([conv, point], 2)
    last = by_z[0]
    for t in (1, 2, 3):
        got_z = send(by_z[t].astype(BF16), lambda x, y, z, c: (x, y, z // 4 * 4 + (z + t) % 4, c))
        last = last + got_z.astype(F32)
    last = last[0] + send(last[1].astype(BF16), lambda x, y, z, c: (x, y, z + 4, c)).astype(F32)
    n = conv.shape[2]
    conv = last[:n].reshape(3, 2, Cq // 64, Hh)
    point_mine = last[n:].reshape(C // Hh, Hq // 64, Hh).transpose(1, 0, 2).reshape(Hq // 64, C)
    kept, swapped = conv[:, 0], send(conv[:, 1], partner)
    kept, swapped = (part.reshape(3, Cq // 64, 2, 1, Hq) for part in (kept, swapped))
    conv_mine = jnp.where(
        core == 0, jnp.concatenate([kept, swapped], 3), jnp.concatenate([swapped, kept], 3)
    ).reshape(3, Cq // 64, H)
    return in_grad[None], conv_mine, point_mine


def solution(mesh):
    placed = (P("dp", "seq", None), P("dp", "seq", None), P(None, "dp", None), P("dp", None))
    return jax.shard_map(
        local,
        mesh=mesh,
        in_specs=placed,
        out_specs=(P("dp", "seq", None), P(None, ("dp", "seq"), None), P(("dp", "seq"), None)),
        check_vma=False,
    )
```

```python
import jax
import jax.numpy as jnp
from jax import lax
from jax.experimental import pallas as pl
from jax.experimental.pallas import tpu as pltpu
from jax.sharding import PartitionSpec as P

DILATION_STEP = 1024
BF16 = jnp.bfloat16
F32 = jnp.float32


def coords(index):
    dp, seq = divmod(index, 64)
    return seq // 16, seq % 4, (dp // 2) * 4 + (seq // 4) % 4, dp % 2


def index_of(x, y, z, core):
    return ((z % 8) // 4 * 2 + core % 2) * 64 + (x % 4) * 16 + (z % 4) * 4 + y % 4


def send(value, target, sources=range(256)):
    pairs = [(device, index_of(*target(*coords(device)))) for device in sources]
    return lax.ppermute(value, ("dp", "seq"), pairs)


def send_a(value, steps):
    return send(value, lambda x, y, z, c: (x + steps * (1 - c), y + steps * c, z, c))


def send_b(value, steps):
    return send(value, lambda x, y, z, c: (x + steps * c, y + steps * (1 - c), z, c))


def shifted(value, steps):
    first, last = (max(0, -steps), min(64, 64 - steps))
    return lax.ppermute(value, "seq", [(source, source + steps) for source in range(first, last)])


def dot(left, right, dims):
    return lax.dot_general(left, right, ((dims[:1], dims[1:]), ((), ())), preferred_element_type=F32)


def pick(value, axis, index):
    return lax.dynamic_index_in_dim(value, index, axis, keepdims=False)


def run(kernel, scalars, arrays, outs, scratch=()):
    vmem = pl.BlockSpec(memory_space=pltpu.VMEM)
    return pl.pallas_call(
        kernel,
        out_shape=outs,
        in_specs=[pl.BlockSpec(memory_space=pltpu.SMEM)] + [vmem] * len(arrays),
        out_specs=[vmem] * len(outs),
        scratch_shapes=scratch,
        compiler_params=pltpu.CompilerParams(vmem_limit_bytes=48 * 1024 * 1024),
        cost_estimate=pl.CostEstimate(flops=1, bytes_accessed=1, transcendentals=0),
    )(scalars, *arrays)


def shape(dims, dtype):
    return jax.ShapeDtypeStruct(tuple(dims), dtype)


def lanes(start, size):
    return pl.ds(pl.multiple_of(start * size, size), size)


def split_kernel(meta, weight, mine, theirs):
    size = weight.shape[2] // 4
    for t in range(3):
        value = weight[t]
        parts = [value[:, k * size:(k + 1) * size] for k in range(4)]
        even, odd = jnp.concatenate(parts[::2], 1), jnp.concatenate(parts[1::2], 1)
        first = meta[0] == 0
        mine[t] = jnp.where(first, even, odd)
        theirs[t] = jnp.where(first, odd, even)


def spread_block(meta, block, order, outs, first):
    core, zh = meta[0], meta[1]
    quarter = order.shape[0]
    unit = quarter // 4
    for u in range(2):
        for v in range(2):
            columns = lanes(lax.rem(zh + u, 2) * 2 + lax.rem(core + v, 2), quarter)
            moved = dot(order[...], block[:, columns], (1, 1)).astype(BF16)
            at = first + (u * 2 + v) * unit
            for r, out in enumerate(outs):
                out[at:at + unit] = moved[r * unit:(r + 1) * unit]


def near_kernel(meta, x0, x0o, x1, x1o, og, ogo, mine, got, pw, order, taps, ogs, pre, arriving,
                keep, send1, send2, send3):
    core, zh = meta[0], meta[1]
    rows, quarter = x0.shape[0], mine.shape[1]
    ogs[:rows] = og[...]
    ogs[rows:] = ogo[...]
    total = jnp.zeros(pre.shape, F32)
    for k, (own, other) in enumerate(((x0, x0o), (x1, x1o))):
        taps[k, :rows] = own[...]
        taps[k, rows:] = other[...]
        total += dot(taps[k, :, lanes(zh * 2 + core, quarter)], mine[k], (1, 0))
        total += dot(taps[k, :, lanes(zh * 2 + 1 - core, quarter)], got[k], (1, 0))
    pre[...] = total
    arriving[...] = dot(ogs[...], pw[...], (1, 1))
    outs = (keep, send1, send2, send3)
    for k in range(2):
        spread_block(meta, taps.at[k], order, outs, k * quarter)


def late_kernel(meta, x2, x2o, near, mine, got, order, tap, pre, own, send1, send2, send3):
    core, zh = meta[0], meta[1]
    rows, quarter = x2.shape[0], order.shape[0]
    tap[:rows] = x2[...]
    tap[rows:] = x2o[...]
    total = near[...] + dot(tap[:, lanes(zh * 2 + core, quarter)], mine[2], (1, 0))
    pre[...] = total + dot(tap[:, lanes(zh * 2 + 1 - core, quarter)], got[2], (1, 0))
    spread_block(meta, tap, order, (own, send1, send2, send3), 0)


def forward_kernel(meta, taps, tap2, ogs, near, arriving, far0, far1, far2, far3, order,
                   x0, x1, x2, x3, hg, hidden_t, wfar, m0, m1, m2, m3, pws):
    core, zh, a, b = (meta[i] for i in range(4))
    piece, width = far0.shape[2:]
    half = 16 * piece
    for j, far in enumerate((far0, far1, far2, far3)):
        for k in range(4):
            ak, bj = lax.rem(a + k, 4), lax.rem(b + j, 4)
            x, y = jnp.where(core == 0, ak, bj), jnp.where(core == 0, bj, ak)
            for t in range(3):
                wfar[t, x * 4 + y] = far[k, t]
            pws[y, x] = far[k, 3]
    pre = near[...]
    for t in range(3):
        columns = lanes(1 - zh, half)
        block = tap2[:, columns] if t == 2 else taps[t, :, columns]
        pre += dot(block, wfar[t].reshape(half, width), (1, 0))
    other = jnp.zeros(arriving.shape, F32)
    for y in range(4):
        other += dot(ogs[:, y * width:(y + 1) * width], pws[y].reshape(4 * piece, width), (1, 1))
    pair = (arriving[...], other)
    grads = jnp.where(zh == 0, jnp.concatenate(pair, 1), jnp.concatenate(pair[::-1], 1))
    scale, cubic = 0.7978845608028654, 0.044715
    square = pre * pre
    tanh = jnp.tanh(scale * (pre + cubic * (square * pre)))
    gate = 0.5 * (1.0 + tanh)
    slope = gate + 0.5 * pre * (1.0 - tanh * tanh) * (scale * (1.0 + 3.0 * cubic * square))
    grads = (grads * slope).astype(BF16)
    hg[...] = grads
    count = x0.shape[0]
    place = [lax.broadcasted_iota(jnp.int32, (width, width), axis) for axis in (0, 1)]
    turned = dot((place[0] == place[1]).astype(BF16), grads, (1, 1)).astype(BF16)
    for x, message in ((x0, m0), (x1, m1), (x2, m2), (x3, m3)):
        message[:count] = x[...]
        message[count:] = turned
    hidden_t[...] = dot(order[...], (pre * gate).astype(BF16), (1, 1)).astype(BF16)


def point_kernel(meta, ogs, hidden_t, own, send1, send2, send3):
    width = own.shape[2]
    unit = hidden_t.shape[0] // 4
    small = unit // 4
    for h in range(ogs.shape[1] // (2 * width)):
        parts = [dot(hidden_t[...], ogs[:, (2 * h + p) * width:(2 * h + p + 1) * width], (1, 0)) for p in range(2)]
        for r, out in enumerate((own, send1, send2, send3)):
            for q in range(4):
                at = r * unit + q * small
                pair = jnp.concatenate([p[at:at + small] for p in parts], 0)
                out[q, h * 2 * small:(h + 1) * 2 * small] = pair.astype(out.dtype)


def gradient_kernel(meta, x0, x1, x2, x3, m0, m1, m2, m3, conv):
    early, width = x0.shape[0], conv.shape[1]
    last = conv.shape[0] - early
    total = [jnp.zeros((size, width), F32) for size in (early, last)]
    for x, m in ((x0, m0), (x1, m1), (x2, m2), (x3, m3)):
        turned = m[last:]
        total[0] += dot(x[...], turned, (1, 1))
        total[1] += dot(m[:last], turned, (1, 1))
    conv[:early] = total[0]
    conv[early:] = total[1]


def pack_kernel(meta, conv, p0, p1, p2, p3, own, send1, send2, send3):
    unit = conv.shape[0] // 12
    piece = unit // 4
    for q, out in enumerate((own, send1, send2, send3)):
        for g in range(6):
            at = 2 * g * unit + q * piece
            pair = jnp.concatenate([conv[at:at + piece], conv[at + unit:at + unit + piece]], 0)
            out[g * 2 * piece:(g + 1) * 2 * piece] = pair.astype(out.dtype)
        point = p0[q] + p1[q].astype(F32) + p2[q].astype(F32) + p3[q].astype(F32)
        out[12 * piece:] = point.astype(out.dtype)


def slice_kernel(meta, own, got1, got2, got3, kept, send1, send2, send3):
    total = own[...] + got1[...].astype(F32) + got2[...].astype(F32) + got3[...].astype(F32)
    piece = total.shape[0] // 16
    row, thin = piece // 4, piece // 8
    for t, out in enumerate((kept, send1, send2, send3)):
        parts = []
        for u in range(2):
            for g in range(3):
                at = (2 * g + u) * 2 * piece + t * row
                parts += [total[at:at + row], total[at + piece:at + piece + row]]
            for p in range(4):
                at = (12 + p) * piece + u * piece // 2 + t * thin
                parts.append(total[at:at + thin])
        out[...] = jnp.concatenate(parts, 0).astype(out.dtype)


def input_kernel(meta, hg, later, earlier, mine, got, wfar, kept, other):
    core, zh = meta[0], meta[1]
    quarter = mine.shape[1]
    rows = kept.shape[0]
    grads = (later[...], hg[...], earlier[...])
    for weights, at, size in ((mine, zh * 2 + core, quarter), (got, zh * 2 + 1 - core, quarter), (wfar, 1 - zh, 2 * quarter)):
        total = sum(dot(grads[t], weights[t], (1, 1)) for t in range(3))
        kept[:, lanes(at, size)] = total[:rows]
        other[:, lanes(at, size)] = total[rows:]


def local(inputs, out_grad, conv_weight, point_weight):
    x, og = inputs[0], out_grad[0]
    rows, C = x.shape
    H = conv_weight.shape[2]
    Cq, Hq, Hh = C // 4, H // 4, H // 2
    piece = C // 32
    hops = DILATION_STEP // rows
    dp, seq = lax.axis_index("dp"), lax.axis_index("seq")
    zh, core = dp // 2, dp % 2
    xi, zl, yi = seq // 16, seq // 4 % 4, seq % 4
    a, b = jnp.where(core == 0, xi, yi), jnp.where(core == 0, yi, xi)
    meta = jnp.stack([core, zh, a, b]).astype(jnp.int32)

    def columns(value, c):
        return jnp.concatenate(
            [lax.dynamic_slice_in_dim(value, half * 2 * Hq + c * Hq, Hq, 2) for half in (0, 1)], axis=2
        )

    def mirror(x, y, z, c):
        return x, y, 7 - z, c

    def partner(x, y, z, c):
        return x, y, z, 1 - c

    def order(width, unit, count):
        new = jnp.arange(width)
        inner = new % (4 * unit)
        u = new // (4 * unit) % count
        r, q = new // (16 * unit * count), new // (4 * unit * count) % 4
        an, bn = (a + r) % 4, (b + q) % 4
        xn, yn = jnp.where(core == 0, an, bn), jnp.where(core == 0, bn, an)
        half = (zh + u) % 2 if count == 2 else 0
        old = half * (64 * unit) + xn * (16 * unit) + (zl + inner // unit) % 4 * (4 * unit) + yn * unit + inner % unit
        return (old[:, None] == jnp.arange(width)[None, :]).astype(BF16)

    def mirror(x, y, z, c):
        return x, y, 7 - z, c

    def partner(x, y, z, c):
        return x, y, z, 1 - c

    def beside(first, second, axis):
        return jnp.where(core == 0, jnp.concatenate([first, second], axis), jnp.concatenate([second, first], axis))

    conv_piece = lax.dynamic_slice_in_dim(conv_weight, (xi * 4 + yi) % 8 * piece, piece, 1)
    point_piece = lax.dynamic_slice(point_weight, (xi * (Hq // 4), yi * Hh), (Hq // 4, Hh))
    holders = [d for d in range(256) if coords(d)[3] == coords(d)[0] // 2]
    conv_piece = send(conv_piece, mirror, holders)
    point_piece = send(point_piece, mirror)
    prev = shifted(x[:rows // 2], hops)
    x_other = send(x, partner)
    og_other = send(og, partner)
    conv_weight, _ = lax.optimization_barrier((conv_weight, x_other))
    mine, theirs = run(split_kernel, meta, [conv_weight], [shape((3, Cq, Hh), BF16)] * 2)
    conv_piece, point_piece, x_late, x_other, og_other, theirs, prev, mine = lax.optimization_barrier(
        (conv_piece, point_piece, x, x_other, og_other, theirs, prev, mine)
    )
    got = send(theirs, partner)
    handed = send(columns(conv_piece, 1 - core), partner, holders)
    conv_piece = jnp.where(core == xi // 2, columns(conv_piece, core), handed)
    far = jnp.concatenate([conv_piece, point_piece[None]])
    prev = jnp.concatenate([prev, shifted(x_late[rows // 2:], hops)])
    fars = [send_a(far, -k) for k in (1, 2, 3)]
    far, prev, x_late, got, *fars = lax.optimization_barrier((far, prev, x_late, got, *fars))
    following = shifted(x_late, -hops)
    far = jnp.stack([far, *fars])
    fars = [far] + [send_b(far, -k) for k in (1, 2, 3)]
    prev_other = send(prev, partner)
    spread = order(Cq, Cq // 64, 1)
    taps, ogs, near, arriving, *early = run(
        near_kernel, meta, [prev, prev_other, x, x_other, og, og_other, mine, got, point_weight, spread],
        [shape((2, 2 * rows, C), BF16), shape((2 * rows, C), BF16), shape((2 * rows, Hh), F32),
         shape((2 * rows, Hq), F32)] + [shape((2 * Cq, 2 * rows), BF16)] * 4,
    )
    following_other = send(following, partner)
    tap, near, *late = run(
        late_kernel, meta, [following, following_other, near, mine, got, spread],
        [shape((2 * rows, C), BF16), shape((2 * rows, Hh), F32)] + [shape((Cq, 2 * rows), BF16)] * 4,
    )
    rest = lax.optimization_barrier((*fars, *early))
    fars, early = rest[:4], rest[4:]
    early = [early[0]] + [send_a(part, k + 1) for k, part in enumerate(early[1:])]
    hg, hidden_t, wfar, *messages = run(
        forward_kernel, meta, [taps, tap, ogs, near, arriving, *fars, order(Hh, Hq // 64, 2), *late],
        [shape((2 * rows, Hh), BF16), shape((Hh, 2 * rows), BF16), shape((3, 16, piece, Hh), BF16)]
        + [shape((Cq + Hh, 2 * rows), BF16)] * 4,
        [pltpu.VMEM((4, 4, Hq // 4, Hh), BF16)],
    )
    messages = [messages[0]] + [send_a(part, k + 1) for k, part in enumerate(messages[1:])]
    block = (4, Hh // 4, Hh)
    p_own, *sends = run(point_kernel, meta, [ogs, hidden_t], [shape(block, F32)] + [shape(block, BF16)] * 3)
    p_all = [p_own] + [send_a(part, k + 1) for k, part in enumerate(sends)]
    conv, = run(gradient_kernel, meta, [*early, *messages], [shape((3 * Cq, Hh), F32)])
    hg_late, _ = lax.optimization_barrier((hg, messages[1]))
    earlier = shifted(hg_late, hops)
    earlier, conv, *p_all = lax.optimization_barrier((earlier, conv, *p_all))
    n = 12 * (Cq // 16)
    big = (n + Hh // 4, Hh)
    total, *sends = run(pack_kernel, meta, [conv, *p_all], [shape(big, F32)] + [shape(big, BF16)] * 3)
    hg_late, _ = lax.optimization_barrier((hg, total))
    later = shifted(hg_late, -hops)
    later, *got_b = lax.optimization_barrier((later, *[send_b(part, k + 1) for k, part in enumerate(sends)]))
    small = (big[0] // 4, Hh)
    last, *sends = run(
        slice_kernel, meta, [total, *got_b],
        [shape(small, F32)] + [shape(small, BF16)] * 3,
    )
    hg_late, last = lax.optimization_barrier((hg, last))
    kept, other = run(
        input_kernel, meta, [hg_late, later, earlier, mine, got, wfar.reshape(3, 2 * Cq, Hh)],
        [shape((rows, C), F32)] * 2,
    )
    in_grad = (og.astype(F32) + kept + send(other, partner)).astype(BF16)

    for t, part in enumerate(sends):
        got_z = send(part, lambda x, y, z, c: (x, y, z // 4 * 4 + (z + t + 1) % 4, c))
        last = last + got_z.astype(F32)
    last = last.reshape(2, small[0] // 2, Hh)
    last = last[0] + send(last[1].astype(BF16), lambda x, y, z, c: (x, y, z + 4, c)).astype(F32)
    n = 6 * (Cq // 64)
    conv = last[:n].reshape(3, 2, Cq // 64, Hh)
    point_mine = last[n:].reshape(C // Hh, Hq // 64, Hh).transpose(1, 0, 2).reshape(Hq // 64, C)
    kept, swapped = conv[:, 0], send(conv[:, 1], partner)
    kept, swapped = (part.reshape(3, Cq // 64, 2, 1, Hq) for part in (kept, swapped))
    conv_mine = jnp.where(
        core == 0, jnp.concatenate([kept, swapped], 3), jnp.concatenate([swapped, kept], 3)
    ).reshape(3, Cq // 64, H)
    return in_grad[None], conv_mine, point_mine


def solution(mesh):
    placed = (P("dp", "seq", None), P("dp", "seq", None), P(None, "dp", None), P("dp", None))
    return jax.shard_map(
        local,
        mesh=mesh,
        in_specs=placed,
        out_specs=(P("dp", "seq", None), P(None, ("dp", "seq"), None), P(("dp", "seq"), None)),
        check_vma=False,
    )
```

```python
import jax
import jax.numpy as jnp
from jax import lax
from jax.experimental import pallas as pl
from jax.experimental.pallas import tpu as pltpu
from jax.sharding import PartitionSpec as P

DILATION_STEP = 1024
BF16 = jnp.bfloat16
F32 = jnp.float32


def coords(index):
    dp, seq = divmod(index, 64)
    return seq // 16, seq % 4, (dp // 2) * 4 + (seq // 4) % 4, dp % 2


def index_of(x, y, z, core):
    return ((z % 8) // 4 * 2 + core % 2) * 64 + (x % 4) * 16 + (z % 4) * 4 + y % 4


def send(value, target, sources=range(256)):
    pairs = [(device, index_of(*target(*coords(device)))) for device in sources]
    return lax.ppermute(value, ("dp", "seq"), pairs)


def send_a(value, steps):
    return send(value, lambda x, y, z, c: (x + steps * (1 - c), y + steps * c, z, c))


def send_b(value, steps):
    return send(value, lambda x, y, z, c: (x + steps * c, y + steps * (1 - c), z, c))


def shifted(value, steps):
    first, last = (max(0, -steps), min(64, 64 - steps))
    return lax.ppermute(value, "seq", [(source, source + steps) for source in range(first, last)])


def dot(left, right, dims):
    return lax.dot_general(left, right, ((dims[:1], dims[1:]), ((), ())), preferred_element_type=F32)


def pick(value, axis, index):
    return lax.dynamic_index_in_dim(value, index, axis, keepdims=False)


def run(kernel, scalars, arrays, outs, scratch=()):
    vmem = pl.BlockSpec(memory_space=pltpu.VMEM)
    return pl.pallas_call(
        kernel,
        out_shape=outs,
        in_specs=[pl.BlockSpec(memory_space=pltpu.SMEM)] + [vmem] * len(arrays),
        out_specs=[vmem] * len(outs),
        scratch_shapes=scratch,
        compiler_params=pltpu.CompilerParams(vmem_limit_bytes=48 * 1024 * 1024),
        cost_estimate=pl.CostEstimate(flops=1, bytes_accessed=1, transcendentals=0),
    )(scalars, *arrays)


def shape(dims, dtype):
    return jax.ShapeDtypeStruct(tuple(dims), dtype)


def lanes(start, size):
    return pl.ds(pl.multiple_of(start * size, size), size)


def split_kernel(meta, weight, mine, theirs):
    size = weight.shape[2] // 4
    for t in range(3):
        value = weight[t]
        parts = [value[:, k * size:(k + 1) * size] for k in range(4)]
        even, odd = jnp.concatenate(parts[::2], 1), jnp.concatenate(parts[1::2], 1)
        first = meta[0] == 0
        mine[t] = jnp.where(first, even, odd)
        theirs[t] = jnp.where(first, odd, even)


def spread_block(meta, block, order, outs, first):
    core, zh = meta[0], meta[1]
    quarter = order.shape[0]
    unit = quarter // 4
    for u in range(2):
        for v in range(2):
            columns = lanes(lax.rem(zh + u, 2) * 2 + lax.rem(core + v, 2), quarter)
            moved = dot(order[...], block[:, columns], (1, 1)).astype(BF16)
            at = first + (u * 2 + v) * unit
            for r, out in enumerate(outs):
                out[at:at + unit] = moved[r * unit:(r + 1) * unit]


def near_kernel(meta, x0, x0o, x1, x1o, og, ogo, mine, got, pw, order, taps, ogs, pre, arriving,
                keep, send1, send2, send3):
    core, zh = meta[0], meta[1]
    rows, quarter = x0.shape[0], mine.shape[1]
    ogs[:rows] = og[...]
    ogs[rows:] = ogo[...]
    total = jnp.zeros(pre.shape, F32)
    for k, (own, other) in enumerate(((x0, x0o), (x1, x1o))):
        taps[k, :rows] = own[...]
        taps[k, rows:] = other[...]
        total += dot(taps[k, :, lanes(zh * 2 + core, quarter)], mine[k], (1, 0))
        total += dot(taps[k, :, lanes(zh * 2 + 1 - core, quarter)], got[k], (1, 0))
    pre[...] = total
    arriving[...] = dot(ogs[...], pw[...], (1, 1))
    outs = (keep, send1, send2, send3)
    for k in range(2):
        spread_block(meta, taps.at[k], order, outs, k * quarter)


def late_kernel(meta, x2, x2o, near, mine, got, order, tap, pre, own, send1, send2, send3):
    core, zh = meta[0], meta[1]
    rows, quarter = x2.shape[0], order.shape[0]
    tap[:rows] = x2[...]
    tap[rows:] = x2o[...]
    total = near[...] + dot(tap[:, lanes(zh * 2 + core, quarter)], mine[2], (1, 0))
    pre[...] = total + dot(tap[:, lanes(zh * 2 + 1 - core, quarter)], got[2], (1, 0))
    spread_block(meta, tap, order, (own, send1, send2, send3), 0)


def forward_kernel(meta, taps, tap2, ogs, near, arriving, far0, far1, far2, far3, order,
                   x0, x1, x2, x3, hg, hidden_t, wfar, m0, m1, m2, m3, pws):
    core, zh, a, b = (meta[i] for i in range(4))
    piece, width = far0.shape[2:]
    half = 16 * piece
    for j, far in enumerate((far0, far1, far2, far3)):
        for k in range(4):
            ak, bj = lax.rem(a + k, 4), lax.rem(b + j, 4)
            x, y = jnp.where(core == 0, ak, bj), jnp.where(core == 0, bj, ak)
            for t in range(3):
                wfar[t, x * 4 + y] = far[k, t]
            pws[y, x] = far[k, 3]
    pre = near[...]
    for t in range(3):
        columns = lanes(1 - zh, half)
        block = tap2[:, columns] if t == 2 else taps[t, :, columns]
        pre += dot(block, wfar[t].reshape(half, width), (1, 0))
    other = jnp.zeros(arriving.shape, F32)
    for y in range(4):
        other += dot(ogs[:, y * width:(y + 1) * width], pws[y].reshape(4 * piece, width), (1, 1))
    pair = (arriving[...], other)
    grads = jnp.where(zh == 0, jnp.concatenate(pair, 1), jnp.concatenate(pair[::-1], 1))
    scale, cubic = 0.7978845608028654, 0.044715
    square = pre * pre
    tanh = jnp.tanh(scale * (pre + cubic * (square * pre)))
    gate = 0.5 * (1.0 + tanh)
    slope = gate + 0.5 * pre * (1.0 - tanh * tanh) * (scale * (1.0 + 3.0 * cubic * square))
    grads = (grads * slope).astype(BF16)
    hg[...] = grads
    count = x0.shape[0]
    place = [lax.broadcasted_iota(jnp.int32, (width, width), axis) for axis in (0, 1)]
    turned = dot((place[0] == place[1]).astype(BF16), grads, (1, 1)).astype(BF16)
    for x, message in ((x0, m0), (x1, m1), (x2, m2), (x3, m3)):
        message[:count] = x[...]
        message[count:] = turned
    hidden_t[...] = dot(order[...], (pre * gate).astype(BF16), (1, 1)).astype(BF16)


def point_kernel(meta, ogs, hidden_t, own, send1, send2, send3):
    width = own.shape[2]
    unit = hidden_t.shape[0] // 4
    small = unit // 4
    for h in range(ogs.shape[1] // (2 * width)):
        parts = [dot(hidden_t[...], ogs[:, (2 * h + p) * width:(2 * h + p + 1) * width], (1, 0)) for p in range(2)]
        for r, out in enumerate((own, send1, send2, send3)):
            for q in range(4):
                at = r * unit + q * small
                pair = jnp.concatenate([p[at:at + small] for p in parts], 0)
                out[q, h * 2 * small:(h + 1) * 2 * small] = pair.astype(out.dtype)


def gradient_kernel(meta, x0, x1, x2, x3, m0, m1, m2, m3, conv):
    early, width = x0.shape[0], conv.shape[1]
    last = conv.shape[0] - early
    total = [jnp.zeros((size, width), F32) for size in (early, last)]
    for x, m in ((x0, m0), (x1, m1), (x2, m2), (x3, m3)):
        turned = m[last:]
        total[0] += dot(x[...], turned, (1, 1))
        total[1] += dot(m[:last], turned, (1, 1))
    conv[:early] = total[0]
    conv[early:] = total[1]


def pack_kernel(meta, conv, p0, p1, p2, p3, own, send1, send2, send3):
    unit = conv.shape[0] // 12
    piece = unit // 4
    for q, out in enumerate((own, send1, send2, send3)):
        for g in range(6):
            at = 2 * g * unit + q * piece
            pair = jnp.concatenate([conv[at:at + piece], conv[at + unit:at + unit + piece]], 0)
            out[g * 2 * piece:(g + 1) * 2 * piece] = pair.astype(out.dtype)
        point = p0[q] + p1[q].astype(F32) + p2[q].astype(F32) + p3[q].astype(F32)
        out[12 * piece:] = point.astype(out.dtype)


def slice_kernel(meta, own, got1, got2, got3, kept, send1, send2, send3):
    total = own[...] + got1[...].astype(F32) + got2[...].astype(F32) + got3[...].astype(F32)
    piece = total.shape[0] // 16
    row, thin = piece // 4, piece // 8
    for t, out in enumerate((kept, send1, send2, send3)):
        parts = []
        for u in range(2):
            for g in range(3):
                at = (2 * g + u) * 2 * piece + t * row
                parts += [total[at:at + row], total[at + piece:at + piece + row]]
            for p in range(4):
                at = (12 + p) * piece + u * piece // 2 + t * thin
                parts.append(total[at:at + thin])
        out[...] = jnp.concatenate(parts, 0).astype(out.dtype)


def input_kernel(meta, hg, later, earlier, mine, got, wfar, kept, other):
    core, zh = meta[0], meta[1]
    quarter = mine.shape[1]
    rows = kept.shape[0]
    grads = (later[...], hg[...], earlier[...])
    for weights, at, size in ((mine, zh * 2 + core, quarter), (got, zh * 2 + 1 - core, quarter), (wfar, 1 - zh, 2 * quarter)):
        total = sum(dot(grads[t], weights[t], (1, 1)) for t in range(3))
        kept[:, lanes(at, size)] = total[:rows]
        other[:, lanes(at, size)] = total[rows:]


def local(inputs, out_grad, conv_weight, point_weight):
    x, og = inputs[0], out_grad[0]
    rows, C = x.shape
    H = conv_weight.shape[2]
    Cq, Hq, Hh = C // 4, H // 4, H // 2
    piece = C // 32
    hops = DILATION_STEP // rows
    dp, seq = lax.axis_index("dp"), lax.axis_index("seq")
    zh, core = dp // 2, dp % 2
    xi, zl, yi = seq // 16, seq // 4 % 4, seq % 4
    a, b = jnp.where(core == 0, xi, yi), jnp.where(core == 0, yi, xi)
    meta = jnp.stack([core, zh, a, b]).astype(jnp.int32)

    def columns(value, c):
        return jnp.concatenate(
            [lax.dynamic_slice_in_dim(value, half * 2 * Hq + c * Hq, Hq, 2) for half in (0, 1)], axis=2
        )

    def mirror(x, y, z, c):
        return x, y, 7 - z, c

    def partner(x, y, z, c):
        return x, y, z, 1 - c

    def order(width, unit, count):
        new = jnp.arange(width)
        inner = new % (4 * unit)
        u = new // (4 * unit) % count
        r, q = new // (16 * unit * count), new // (4 * unit * count) % 4
        an, bn = (a + r) % 4, (b + q) % 4
        xn, yn = jnp.where(core == 0, an, bn), jnp.where(core == 0, bn, an)
        half = (zh + u) % 2 if count == 2 else 0
        old = half * (64 * unit) + xn * (16 * unit) + (zl + inner // unit) % 4 * (4 * unit) + yn * unit + inner % unit
        return (old[:, None] == jnp.arange(width)[None, :]).astype(BF16)

    def mirror(x, y, z, c):
        return x, y, 7 - z, c

    def partner(x, y, z, c):
        return x, y, z, 1 - c

    def beside(first, second, axis):
        return jnp.where(core == 0, jnp.concatenate([first, second], axis), jnp.concatenate([second, first], axis))

    conv_piece = lax.dynamic_slice_in_dim(conv_weight, (xi * 4 + yi) % 8 * piece, piece, 1)
    point_piece = lax.dynamic_slice(point_weight, (xi * (Hq // 4), yi * Hh), (Hq // 4, Hh))
    holders = [d for d in range(256) if coords(d)[3] == coords(d)[0] // 2]
    conv_piece = send(conv_piece, mirror, holders)
    point_piece = send(point_piece, mirror)
    first = rows * 3 // 8
    prev = shifted(x[:first], hops)
    x_other = send(x, partner)
    og_other = send(og, partner)
    conv_weight, _ = lax.optimization_barrier((conv_weight, x_other))
    mine, theirs = run(split_kernel, meta, [conv_weight], [shape((3, Cq, Hh), BF16)] * 2)
    conv_piece, point_piece, x_late, x_other, og_other, theirs, prev, mine = lax.optimization_barrier(
        (conv_piece, point_piece, x, x_other, og_other, theirs, prev, mine)
    )
    got = send(theirs, partner)
    handed = send(columns(conv_piece, 1 - core), partner, holders)
    conv_piece = jnp.where(core == xi // 2, columns(conv_piece, core), handed)
    far = jnp.concatenate([conv_piece, point_piece[None]])
    prev = jnp.concatenate([prev, shifted(x_late[first:], hops)])
    fars = [send_a(far, -k) for k in (1, 2, 3)]
    far, prev, x_late, got, *fars = lax.optimization_barrier((far, prev, x_late, got, *fars))
    following = shifted(x_late, -hops)
    far = jnp.stack([far, *fars])
    fars = [far] + [send_b(far, -k) for k in (1, 2, 3)]
    prev_other = send(prev, partner)
    spread = order(Cq, Cq // 64, 1)
    taps, ogs, near, arriving, *early = run(
        near_kernel, meta, [prev, prev_other, x, x_other, og, og_other, mine, got, point_weight, spread],
        [shape((2, 2 * rows, C), BF16), shape((2 * rows, C), BF16), shape((2 * rows, Hh), F32),
         shape((2 * rows, Hq), F32)] + [shape((2 * Cq, 2 * rows), BF16)] * 4,
    )
    following, taps = lax.optimization_barrier((following, taps))
    following_other = send(following, partner)
    tap, near, *late = run(
        late_kernel, meta, [following, following_other, near, mine, got, spread],
        [shape((2 * rows, C), BF16), shape((2 * rows, Hh), F32)] + [shape((Cq, 2 * rows), BF16)] * 4,
    )
    rest = lax.optimization_barrier((*fars, *early))
    fars, early = rest[:4], rest[4:]
    early = [early[0]] + [send_a(part, k + 1) for k, part in enumerate(early[1:])]
    hg, hidden_t, wfar, *messages = run(
        forward_kernel, meta, [taps, tap, ogs, near, arriving, *fars, order(Hh, Hq // 64, 2), *late],
        [shape((2 * rows, Hh), BF16), shape((Hh, 2 * rows), BF16), shape((3, 16, piece, Hh), BF16)]
        + [shape((Cq + Hh, 2 * rows), BF16)] * 4,
        [pltpu.VMEM((4, 4, Hq // 4, Hh), BF16)],
    )
    hg, *rest = lax.optimization_barrier((hg, *early, *messages))
    early, messages = rest[:4], rest[4:]
    messages = [messages[0]] + [send_a(part, k + 1) for k, part in enumerate(messages[1:])]
    block = (4, Hh // 4, Hh)
    p_own, *sends = run(point_kernel, meta, [ogs, hidden_t], [shape(block, F32)] + [shape(block, BF16)] * 3)
    p_all = [p_own] + [send_a(part, k + 1) for k, part in enumerate(sends)]
    earlier = shifted(hg, hops)
    earlier, hg_late, *messages = lax.optimization_barrier((earlier, hg, *messages))
    later = shifted(hg_late, -hops)
    conv, = run(gradient_kernel, meta, [*early, *messages], [shape((3 * Cq, Hh), F32)])
    later, conv, *p_all = lax.optimization_barrier((later, conv, *p_all))
    n = 12 * (Cq // 16)
    big = (n + Hh // 4, Hh)
    total, *sends = run(pack_kernel, meta, [conv, *p_all], [shape(big, F32)] + [shape(big, BF16)] * 3)
    got_b = [send_b(part, k + 1) for k, part in enumerate(sends)]
    small = (big[0] // 4, Hh)
    last, *sends = run(
        slice_kernel, meta, [total, *got_b],
        [shape(small, F32)] + [shape(small, BF16)] * 3,
    )
    hg_late, last = lax.optimization_barrier((hg, last))
    kept, other = run(
        input_kernel, meta, [hg_late, later, earlier, mine, got, wfar.reshape(3, 2 * Cq, Hh)],
        [shape((rows, C), F32)] * 2,
    )
    in_grad = (og.astype(F32) + kept + send(other, partner)).astype(BF16)

    got_z = [
        send(part, lambda x, y, z, c: (x, y, z // 4 * 4 + (z + t + 1) % 4, c)) for t, part in enumerate(sends)
    ]
    for part in got_z:
        last = last + part.astype(F32)
    last = last.reshape(2, small[0] // 2, Hh)
    got_z = send(last[1].astype(BF16), lambda x, y, z, c: (x, y, z + 4, c))
    last = last[0] + got_z.astype(F32)
    n = 6 * (Cq // 64)
    conv = last[:n].reshape(3, 2, Cq // 64, Hh)
    point_mine = last[n:].reshape(C // Hh, Hq // 64, Hh).transpose(1, 0, 2).reshape(Hq // 64, C)
    kept, swapped = conv[:, 0], send(conv[:, 1], partner)
    in_grad, swapped = lax.optimization_barrier((in_grad, swapped))
    kept, swapped = (part.reshape(3, Cq // 64, 2, 1, Hq) for part in (kept, swapped))
    conv_mine = jnp.where(
        core == 0, jnp.concatenate([kept, swapped], 3), jnp.concatenate([swapped, kept], 3)
    ).reshape(3, Cq // 64, H)
    return in_grad[None], conv_mine, point_mine


def solution(mesh):
    placed = (P("dp", "seq", None), P("dp", "seq", None), P(None, "dp", None), P("dp", None))
    return jax.shard_map(
        local,
        mesh=mesh,
        in_specs=placed,
        out_specs=(P("dp", "seq", None), P(None, ("dp", "seq"), None), P(("dp", "seq"), None)),
        check_vma=False,
    )
```

```python
import jax
import jax.numpy as jnp
from jax import lax
from jax.experimental import pallas as pl
from jax.experimental.pallas import tpu as pltpu
from jax.sharding import PartitionSpec as P

DILATION_STEP = 1024
BF16 = jnp.bfloat16
F32 = jnp.float32


def coords(index):
    dp, seq = divmod(index, 64)
    return seq // 16, seq % 4, (dp // 2) * 4 + (seq // 4) % 4, dp % 2


def index_of(x, y, z, core):
    return ((z % 8) // 4 * 2 + core % 2) * 64 + (x % 4) * 16 + (z % 4) * 4 + y % 4


def send(value, target, sources=range(256)):
    pairs = [(device, index_of(*target(*coords(device)))) for device in sources]
    return lax.ppermute(value, ("dp", "seq"), pairs)


def send_a(value, steps):
    return send(value, lambda x, y, z, c: (x + steps * (1 - c), y + steps * c, z, c))


def send_b(value, steps):
    return send(value, lambda x, y, z, c: (x + steps * c, y + steps * (1 - c), z, c))


def flip(value):
    return send(value, lambda x, y, z, c: (x, y, z // 4 * 4 + (z + 2) % 4, c))


def hop(value):
    up = [d for d in range(256) if coords(d)[2] % 4 < 2 and coords(d)[0] < 3]
    down = [d for d in range(256) if coords(d)[2] % 4 >= 2 and coords(d)[0] > 0]
    return send(value, lambda x, y, z, c: (x + 1 if z % 4 < 2 else x - 1, y, z, c), up + down)


def dot(left, right, dims):
    return lax.dot_general(left, right, ((dims[:1], dims[1:]), ((), ())), preferred_element_type=F32)


def pick(value, axis, index):
    return lax.dynamic_index_in_dim(value, index, axis, keepdims=False)


def run(kernel, scalars, arrays, outs, scratch=()):
    vmem = pl.BlockSpec(memory_space=pltpu.VMEM)
    return pl.pallas_call(
        kernel,
        out_shape=outs,
        in_specs=[pl.BlockSpec(memory_space=pltpu.SMEM)] + [vmem] * len(arrays),
        out_specs=[vmem] * len(outs),
        scratch_shapes=scratch,
        compiler_params=pltpu.CompilerParams(vmem_limit_bytes=48 * 1024 * 1024),
        cost_estimate=pl.CostEstimate(flops=1, bytes_accessed=1, transcendentals=0),
    )(scalars, *arrays)


def shape(dims, dtype):
    return jax.ShapeDtypeStruct(tuple(dims), dtype)


def lanes(start, size):
    return pl.ds(pl.multiple_of(start * size, size), size)


def split_kernel(meta, weight, mine, theirs):
    size = weight.shape[2] // 4
    for t in range(3):
        value = weight[t]
        parts = [value[:, k * size:(k + 1) * size] for k in range(4)]
        even, odd = jnp.concatenate(parts[::2], 1), jnp.concatenate(parts[1::2], 1)
        first = meta[0] == 0
        mine[t] = jnp.where(first, even, odd)
        theirs[t] = jnp.where(first, odd, even)


def spread_block(meta, block, order, outs, first):
    core, zh = meta[0], meta[1]
    quarter = order.shape[0]
    unit = quarter // 4
    for u in range(2):
        for v in range(2):
            columns = lanes(lax.rem(zh + u, 2) * 2 + lax.rem(core + v, 2), quarter)
            moved = dot(order[...], block[:, columns], (1, 1)).astype(BF16)
            at = first + (u * 2 + v) * unit
            for r, out in enumerate(outs):
                out[at:at + unit] = moved[r * unit:(r + 1) * unit]


def near_kernel(meta, x0, x0o, x1, x1o, og, ogo, mine, got, pw, order, taps, ogs, pre, arriving,
                keep, send1, send2, send3):
    core, zh = meta[0], meta[1]
    rows, quarter = x0.shape[0], mine.shape[1]
    ogs[:rows] = og[...]
    ogs[rows:] = ogo[...]
    total = jnp.zeros(pre.shape, F32)
    for k, (own, other) in enumerate(((x0, x0o), (x1, x1o))):
        taps[k, :rows] = own[...]
        taps[k, rows:] = other[...]
        t = meta[4] if k == 0 else 1
        total += dot(taps[k, :, lanes(zh * 2 + core, quarter)], mine[t], (1, 0))
        total += dot(taps[k, :, lanes(zh * 2 + 1 - core, quarter)], got[t], (1, 0))
    pre[...] = total
    arriving[...] = dot(ogs[...], pw[...], (1, 1))
    outs = (keep, send1, send2, send3)
    for k in range(2):
        spread_block(meta, taps.at[k], order, outs, k * quarter)


def late_kernel(meta, x2, x2o, near, mine, got, order, tap, pre, own, send1, send2, send3):
    core, zh = meta[0], meta[1]
    rows, quarter = x2.shape[0], order.shape[0]
    tap[:rows] = x2[...]
    tap[rows:] = x2o[...]
    t = 2 - meta[4]
    total = near[...] + dot(tap[:, lanes(zh * 2 + core, quarter)], mine[t], (1, 0))
    pre[...] = total + dot(tap[:, lanes(zh * 2 + 1 - core, quarter)], got[t], (1, 0))
    spread_block(meta, tap, order, (own, send1, send2, send3), 0)


def forward_kernel(meta, taps, tap2, ogs, near, arriving, far0, far1, far2, far3, order,
                   x0, x1, x2, x3, hg, hidden_t, wfar, m0, m1, m2, m3, pws):
    core, zh, a, b = (meta[i] for i in range(4))
    piece, width = far0.shape[2:]
    half = 16 * piece
    for j, far in enumerate((far0, far1, far2, far3)):
        for k in range(4):
            ak, bj = lax.rem(a + k, 4), lax.rem(b + j, 4)
            x, y = jnp.where(core == 0, ak, bj), jnp.where(core == 0, bj, ak)
            for t in range(3):
                wfar[t, x * 4 + y] = far[k, t]
            pws[y, x] = far[k, 3]
    pre = near[...]
    for k, t in enumerate((meta[4], 1, 2 - meta[4])):
        columns = lanes(1 - zh, half)
        block = tap2[:, columns] if k == 2 else taps[k, :, columns]
        pre += dot(block, wfar[t].reshape(half, width), (1, 0))
    other = jnp.zeros(arriving.shape, F32)
    for y in range(4):
        other += dot(ogs[:, y * width:(y + 1) * width], pws[y].reshape(4 * piece, width), (1, 1))
    pair = (arriving[...], other)
    grads = jnp.where(zh == 0, jnp.concatenate(pair, 1), jnp.concatenate(pair[::-1], 1))
    scale, cubic = 0.7978845608028654, 0.044715
    square = pre * pre
    tanh = jnp.tanh(scale * (pre + cubic * (square * pre)))
    gate = 0.5 * (1.0 + tanh)
    slope = gate + 0.5 * pre * (1.0 - tanh * tanh) * (scale * (1.0 + 3.0 * cubic * square))
    grads = (grads * slope).astype(BF16)
    hg[...] = grads
    count = x0.shape[0]
    place = [lax.broadcasted_iota(jnp.int32, (width, width), axis) for axis in (0, 1)]
    turned = dot((place[0] == place[1]).astype(BF16), grads, (1, 1)).astype(BF16)
    for x, message in ((x0, m0), (x1, m1), (x2, m2), (x3, m3)):
        message[:count] = x[...]
        message[count:] = turned
    hidden_t[...] = dot(order[...], (pre * gate).astype(BF16), (1, 1)).astype(BF16)


def point_kernel(meta, ogs, hidden_t, own, send1, send2, send3):
    width = own.shape[2]
    unit = hidden_t.shape[0] // 4
    small = unit // 4
    for h in range(ogs.shape[1] // (2 * width)):
        parts = [dot(hidden_t[...], ogs[:, (2 * h + p) * width:(2 * h + p + 1) * width], (1, 0)) for p in range(2)]
        for r, out in enumerate((own, send1, send2, send3)):
            for q in range(4):
                at = r * unit + q * small
                pair = jnp.concatenate([p[at:at + small] for p in parts], 0)
                out[q, h * 2 * small:(h + 1) * 2 * small] = pair.astype(out.dtype)


def gradient_kernel(meta, x0, x1, x2, x3, m0, m1, m2, m3, conv):
    early, width = x0.shape[0], conv.shape[1]
    last = conv.shape[0] - early
    total = [jnp.zeros((size, width), F32) for size in (early, last)]
    for x, m in ((x0, m0), (x1, m1), (x2, m2), (x3, m3)):
        turned = m[last:]
        total[0] += dot(x[...], turned, (1, 1))
        total[1] += dot(m[:last], turned, (1, 1))
    conv[pl.ds(pl.multiple_of(meta[4] * last, last), last)] = total[0][:last]
    conv[last:2 * last] = total[0][last:]
    conv[pl.ds(pl.multiple_of((2 - meta[4]) * last, last), last)] = total[1]


def pack_kernel(meta, conv, p0, p1, p2, p3, own, send1, send2, send3):
    unit = conv.shape[0] // 12
    piece = unit // 4
    for q, out in enumerate((own, send1, send2, send3)):
        for g in range(6):
            at = 2 * g * unit + q * piece
            pair = jnp.concatenate([conv[at:at + piece], conv[at + unit:at + unit + piece]], 0)
            out[g * 2 * piece:(g + 1) * 2 * piece] = pair.astype(out.dtype)
        point = p0[q] + p1[q].astype(F32) + p2[q].astype(F32) + p3[q].astype(F32)
        out[12 * piece:] = point.astype(out.dtype)


def slice_kernel(meta, own, got1, got2, got3, kept, send1, send2, send3):
    total = own[...] + got1[...].astype(F32) + got2[...].astype(F32) + got3[...].astype(F32)
    piece = total.shape[0] // 16
    row, thin = piece // 4, piece // 8
    for t, out in enumerate((kept, send1, send2, send3)):
        parts = []
        for u in range(2):
            for g in range(3):
                at = (2 * g + u) * 2 * piece + t * row
                parts += [total[at:at + row], total[at + piece:at + piece + row]]
            for p in range(4):
                at = (12 + p) * piece + u * piece // 2 + t * thin
                parts.append(total[at:at + thin])
        out[...] = jnp.concatenate(parts, 0).astype(out.dtype)


def input_kernel(meta, hg, flipped, hopped, mine, got, wfar, kept, other):
    core, zh = meta[0], meta[1]
    quarter = mine.shape[1]
    rows = kept.shape[0]
    grads = ((flipped[...], 2 - meta[4]), (hg[...], 1), (hopped[...], meta[4]))
    for weights, at, size in ((mine, zh * 2 + core, quarter), (got, zh * 2 + 1 - core, quarter), (wfar, 1 - zh, 2 * quarter)):
        total = sum(dot(grad, weights[t], (1, 1)) for grad, t in grads)
        kept[:, lanes(at, size)] = total[:rows]
        other[:, lanes(at, size)] = total[rows:]


def local(inputs, out_grad, conv_weight, point_weight):
    x, og = inputs[0], out_grad[0]
    rows, C = x.shape
    H = conv_weight.shape[2]
    Cq, Hq, Hh = C // 4, H // 4, H // 2
    piece = C // 32
    assert DILATION_STEP == 8 * rows
    dp, seq = lax.axis_index("dp"), lax.axis_index("seq")
    zh, core = dp // 2, dp % 2
    xi, zl, yi = seq // 16, seq // 4 % 4, seq % 4
    a, b = jnp.where(core == 0, xi, yi), jnp.where(core == 0, yi, xi)
    meta = jnp.stack([core, zh, a, b, jnp.where(zl < 2, 2, 0)]).astype(jnp.int32)

    def columns(value, c):
        return jnp.concatenate(
            [lax.dynamic_slice_in_dim(value, half * 2 * Hq + c * Hq, Hq, 2) for half in (0, 1)], axis=2
        )

    def mirror(x, y, z, c):
        return x, y, 7 - z, c

    def partner(x, y, z, c):
        return x, y, z, 1 - c

    def order(width, unit, count):
        new = jnp.arange(width)
        inner = new % (4 * unit)
        u = new // (4 * unit) % count
        r, q = new // (16 * unit * count), new // (4 * unit * count) % 4
        an, bn = (a + r) % 4, (b + q) % 4
        xn, yn = jnp.where(core == 0, an, bn), jnp.where(core == 0, bn, an)
        half = (zh + u) % 2 if count == 2 else 0
        old = half * (64 * unit) + xn * (16 * unit) + (zl + inner // unit) % 4 * (4 * unit) + yn * unit + inner % unit
        return (old[:, None] == jnp.arange(width)[None, :]).astype(BF16)

    def mirror(x, y, z, c):
        return x, y, 7 - z, c

    def partner(x, y, z, c):
        return x, y, z, 1 - c

    def beside(first, second, axis):
        return jnp.where(core == 0, jnp.concatenate([first, second], axis), jnp.concatenate([second, first], axis))

    conv_piece = lax.dynamic_slice_in_dim(conv_weight, (xi * 4 + yi) % 8 * piece, piece, 1)
    point_piece = lax.dynamic_slice(point_weight, (xi * (Hq // 4), yi * Hh), (Hq // 4, Hh))
    holders = [d for d in range(256) if coords(d)[3] == coords(d)[0] // 2]
    conv_piece = send(conv_piece, mirror, holders)
    point_piece = send(point_piece, mirror)
    first = rows // 2
    flipped = flip(x[:first])
    x_other = send(x, partner)
    og_other = send(og, partner)
    conv_weight, _ = lax.optimization_barrier((conv_weight, x_other))
    mine, theirs = run(split_kernel, meta, [conv_weight], [shape((3, Cq, Hh), BF16)] * 2)
    conv_piece, point_piece, x_late, x_other, og_other, theirs, flipped, mine = lax.optimization_barrier(
        (conv_piece, point_piece, x, x_other, og_other, theirs, flipped, mine)
    )
    got = send(theirs, partner)
    handed = send(columns(conv_piece, 1 - core), partner, holders)
    conv_piece = jnp.where(core == xi // 2, columns(conv_piece, core), handed)
    far = jnp.concatenate([conv_piece, point_piece[None]])
    flipped = jnp.concatenate([flipped, flip(x_late[first:])])
    fars = [send_a(far, -k) for k in (1, 2, 3)]
    far, flipped, got, *fars = lax.optimization_barrier((far, flipped, got, *fars))
    hopped = hop(flipped)
    far = jnp.stack([far, *fars])
    fars = [far] + [send_b(far, -k) for k in (1, 2, 3)]
    flipped_other = send(flipped, partner)
    spread = order(Cq, Cq // 64, 1)
    taps, ogs, near, arriving, *early = run(
        near_kernel, meta, [flipped, flipped_other, x, x_other, og, og_other, mine, got, point_weight, spread],
        [shape((2, 2 * rows, C), BF16), shape((2 * rows, C), BF16), shape((2 * rows, Hh), F32),
         shape((2 * rows, Hq), F32)] + [shape((2 * Cq, 2 * rows), BF16)] * 4,
    )
    hopped, taps = lax.optimization_barrier((hopped, taps))
    hopped_other = send(hopped, partner)
    tap, near, *late = run(
        late_kernel, meta, [hopped, hopped_other, near, mine, got, spread],
        [shape((2 * rows, C), BF16), shape((2 * rows, Hh), F32)] + [shape((Cq, 2 * rows), BF16)] * 4,
    )
    rest = lax.optimization_barrier((*fars, *early, *late))
    fars, early, late = rest[:4], rest[4:8], rest[8:]
    early = [early[0]] + [send_a(part, k + 1) for k, part in enumerate(early[1:])]
    hg, hidden_t, wfar, *messages = run(
        forward_kernel, meta, [taps, tap, ogs, near, arriving, *fars, order(Hh, Hq // 64, 2), *late],
        [shape((2 * rows, Hh), BF16), shape((Hh, 2 * rows), BF16), shape((3, 16, piece, Hh), BF16)]
        + [shape((Cq + Hh, 2 * rows), BF16)] * 4,
        [pltpu.VMEM((4, 4, Hq // 4, Hh), BF16)],
    )
    hg, *rest = lax.optimization_barrier((hg, *early, *messages))
    early, messages = rest[:4], rest[4:]
    messages = [messages[0]] + [send_a(part, k + 1) for k, part in enumerate(messages[1:])]
    block = (4, Hh // 4, Hh)
    p_own, *sends = run(point_kernel, meta, [ogs, hidden_t], [shape(block, F32)] + [shape(block, BF16)] * 3)
    p_all = [p_own] + [send_a(part, k + 1) for k, part in enumerate(sends)]
    hg_flipped = flip(hg)
    hg_flipped, *messages = lax.optimization_barrier((hg_flipped, *messages))
    hg_hopped = hop(hg_flipped)
    conv, = run(gradient_kernel, meta, [*early, *messages], [shape((3 * Cq, Hh), F32)])
    hg_hopped, conv, *p_all = lax.optimization_barrier((hg_hopped, conv, *p_all))
    n = 12 * (Cq // 16)
    big = (n + Hh // 4, Hh)
    total, *sends = run(pack_kernel, meta, [conv, *p_all], [shape(big, F32)] + [shape(big, BF16)] * 3)
    got_b = [send_b(part, k + 1) for k, part in enumerate(sends)]
    small = (big[0] // 4, Hh)
    last, *sends = run(
        slice_kernel, meta, [total, *got_b],
        [shape(small, F32)] + [shape(small, BF16)] * 3,
    )
    hg_late, last = lax.optimization_barrier((hg, last))
    kept, other = run(
        input_kernel, meta, [hg_late, hg_flipped, hg_hopped, mine, got, wfar.reshape(3, 2 * Cq, Hh)],
        [shape((rows, C), F32)] * 2,
    )
    in_grad = (og.astype(F32) + kept + send(other, partner)).astype(BF16)

    got_z = [
        send(part, lambda x, y, z, c: (x, y, z // 4 * 4 + (z + t + 1) % 4, c)) for t, part in enumerate(sends)
    ]
    for part in got_z:
        last = last + part.astype(F32)
    last = last.reshape(2, small[0] // 2, Hh)
    got_z = send(last[1].astype(BF16), lambda x, y, z, c: (x, y, z + 4, c))
    last = last[0] + got_z.astype(F32)
    n = 6 * (Cq // 64)
    conv = last[:n].reshape(3, 2, Cq // 64, Hh)
    point_mine = last[n:].reshape(C // Hh, Hq // 64, Hh).transpose(1, 0, 2).reshape(Hq // 64, C)
    kept, swapped = conv[:, 0], send(conv[:, 1], partner)
    in_grad, swapped = lax.optimization_barrier((in_grad, swapped))
    kept, swapped = (part.reshape(3, Cq // 64, 2, 1, Hq) for part in (kept, swapped))
    conv_mine = jnp.where(
        core == 0, jnp.concatenate([kept, swapped], 3), jnp.concatenate([swapped, kept], 3)
    ).reshape(3, Cq // 64, H)
    return in_grad[None], conv_mine, point_mine


def solution(mesh):
    placed = (P("dp", "seq", None), P("dp", "seq", None), P(None, "dp", None), P("dp", None))
    return jax.shard_map(
        local,
        mesh=mesh,
        in_specs=placed,
        out_specs=(P("dp", "seq", None), P(None, ("dp", "seq"), None), P(("dp", "seq"), None)),
        check_vma=False,
    )
```

```python
import jax
import jax.numpy as jnp
from jax import lax
from jax.experimental import pallas as pl
from jax.experimental.pallas import tpu as pltpu
from jax.sharding import PartitionSpec as P

DILATION_STEP = 1024
BF16 = jnp.bfloat16
F32 = jnp.float32


def coords(index):
    dp, seq = divmod(index, 64)
    return seq // 16, seq % 4, (dp // 2) * 4 + (seq // 4) % 4, dp % 2


def index_of(x, y, z, core):
    return ((z % 8) // 4 * 2 + core % 2) * 64 + (x % 4) * 16 + (z % 4) * 4 + y % 4


def send(value, target, sources=range(256)):
    pairs = [(device, index_of(*target(*coords(device)))) for device in sources]
    return lax.ppermute(value, ("dp", "seq"), pairs)


def send_a(value, steps):
    return send(value, lambda x, y, z, c: (x + steps * (1 - c), y + steps * c, z, c))


def send_b(value, steps):
    return send(value, lambda x, y, z, c: (x + steps * c, y + steps * (1 - c), z, c))


def flip(value):
    return send(value, lambda x, y, z, c: (x, y, z // 4 * 4 + (z + 2) % 4, c))


def hop(value):
    up = [d for d in range(256) if coords(d)[2] % 4 < 2 and coords(d)[0] < 3]
    down = [d for d in range(256) if coords(d)[2] % 4 >= 2 and coords(d)[0] > 0]
    return send(value, lambda x, y, z, c: (x + 1 if z % 4 < 2 else x - 1, y, z, c), up + down)


def dot(left, right, dims):
    return lax.dot_general(left, right, ((dims[:1], dims[1:]), ((), ())), preferred_element_type=F32)


def pick(value, axis, index):
    return lax.dynamic_index_in_dim(value, index, axis, keepdims=False)


def run(kernel, scalars, arrays, outs, scratch=()):
    vmem = pl.BlockSpec(memory_space=pltpu.VMEM)
    return pl.pallas_call(
        kernel,
        out_shape=outs,
        in_specs=[pl.BlockSpec(memory_space=pltpu.SMEM)] + [vmem] * len(arrays),
        out_specs=[vmem] * len(outs),
        scratch_shapes=scratch,
        compiler_params=pltpu.CompilerParams(vmem_limit_bytes=48 * 1024 * 1024),
        cost_estimate=pl.CostEstimate(flops=1, bytes_accessed=1, transcendentals=0),
    )(scalars, *arrays)


def shape(dims, dtype):
    return jax.ShapeDtypeStruct(tuple(dims), dtype)


def lanes(start, size):
    return pl.ds(pl.multiple_of(start * size, size), size)


def split_kernel(meta, weight, mine, theirs):
    size = weight.shape[2] // 4
    for t in range(3):
        value = weight[t]
        parts = [value[:, k * size:(k + 1) * size] for k in range(4)]
        even, odd = jnp.concatenate(parts[::2], 1), jnp.concatenate(parts[1::2], 1)
        first = meta[0] == 0
        mine[t] = jnp.where(first, even, odd)
        theirs[t] = jnp.where(first, odd, even)


def spread_block(meta, block, order, outs, first):
    core, zh = meta[0], meta[1]
    quarter = order.shape[0]
    unit = quarter // 4
    for u in range(2):
        for v in range(2):
            columns = lanes(lax.rem(zh + u, 2) * 2 + lax.rem(core + v, 2), quarter)
            moved = dot(order[...], block[:, columns], (1, 1)).astype(BF16)
            at = first + (u * 2 + v) * unit
            for r, out in enumerate(outs):
                out[at:at + unit] = moved[r * unit:(r + 1) * unit]


def near_kernel(meta, x0, x0o, x1, x1o, og, ogo, mine, got, pw, order, taps, ogs, pre, arriving,
                keep, send1, send2, send3):
    core, zh = meta[0], meta[1]
    rows, quarter = x0.shape[0], mine.shape[1]
    ogs[:rows] = og[...]
    ogs[rows:] = ogo[...]
    total = jnp.zeros(pre.shape, F32)
    for k, (own, other) in enumerate(((x0, x0o), (x1, x1o))):
        taps[k, :rows] = own[...]
        taps[k, rows:] = other[...]
        t = meta[4] if k == 0 else 1
        total += dot(taps[k, :, lanes(zh * 2 + core, quarter)], mine[t], (1, 0))
        total += dot(taps[k, :, lanes(zh * 2 + 1 - core, quarter)], got[t], (1, 0))
    pre[...] = total
    arriving[...] = dot(ogs[...], pw[...], (1, 1))
    outs = (keep, send1, send2, send3)
    for k in range(2):
        spread_block(meta, taps.at[k], order, outs, k * quarter)


def late_kernel(meta, x2, x2o, near, mine, got, order, tap, pre, own, send1, send2, send3):
    core, zh = meta[0], meta[1]
    rows, quarter = x2.shape[0], order.shape[0]
    tap[:rows] = x2[...]
    tap[rows:] = x2o[...]
    t = 2 - meta[4]
    total = near[...] + dot(tap[:, lanes(zh * 2 + core, quarter)], mine[t], (1, 0))
    pre[...] = total + dot(tap[:, lanes(zh * 2 + 1 - core, quarter)], got[t], (1, 0))
    spread_block(meta, tap, order, (own, send1, send2, send3), 0)


def forward_kernel(meta, taps, tap2, ogs, near, arriving, far0, far1, far2, far3, order,
                   x0, x1, x2, x3, hg, hidden_t, wfar, m0, m1, m2, m3, pws):
    core, zh, a, b = (meta[i] for i in range(4))
    piece, width = far0.shape[2:]
    half = 16 * piece
    for j, far in enumerate((far0, far1, far2, far3)):
        for k in range(4):
            ak, bj = lax.rem(a + k, 4), lax.rem(b + j, 4)
            x, y = jnp.where(core == 0, ak, bj), jnp.where(core == 0, bj, ak)
            for t in range(3):
                wfar[t, x * 4 + y] = far[k, t]
            pws[y, x] = far[k, 3]
    pre = near[...]
    for k, t in enumerate((meta[4], 1, 2 - meta[4])):
        columns = lanes(1 - zh, half)
        block = tap2[:, columns] if k == 2 else taps[k, :, columns]
        pre += dot(block, wfar[t].reshape(half, width), (1, 0))
    other = jnp.zeros(arriving.shape, F32)
    for y in range(4):
        other += dot(ogs[:, y * width:(y + 1) * width], pws[y].reshape(4 * piece, width), (1, 1))
    pair = (arriving[...], other)
    grads = jnp.where(zh == 0, jnp.concatenate(pair, 1), jnp.concatenate(pair[::-1], 1))
    scale, cubic = 0.7978845608028654, 0.044715
    square = pre * pre
    tanh = jnp.tanh(scale * (pre + cubic * (square * pre)))
    gate = 0.5 * (1.0 + tanh)
    slope = gate + 0.5 * pre * (1.0 - tanh * tanh) * (scale * (1.0 + 3.0 * cubic * square))
    grads = (grads * slope).astype(BF16)
    hg[...] = grads
    count = x0.shape[0]
    place = [lax.broadcasted_iota(jnp.int32, (width, width), axis) for axis in (0, 1)]
    turned = dot((place[0] == place[1]).astype(BF16), grads, (1, 1)).astype(BF16)
    for x, message in ((x0, m0), (x1, m1), (x2, m2), (x3, m3)):
        message[:count] = x[...]
        message[count:] = turned
    hidden_t[...] = dot(order[...], (pre * gate).astype(BF16), (1, 1)).astype(BF16)


def point_kernel(meta, ogs, hidden_t, own, send1, send2, send3):
    width = own.shape[2]
    unit = hidden_t.shape[0] // 4
    small = unit // 4
    for h in range(ogs.shape[1] // (2 * width)):
        parts = [dot(hidden_t[...], ogs[:, (2 * h + p) * width:(2 * h + p + 1) * width], (1, 0)) for p in range(2)]
        for r, out in enumerate((own, send1, send2, send3)):
            for q in range(4):
                at = r * unit + q * small
                pair = jnp.concatenate([p[at:at + small] for p in parts], 0)
                out[q, h * 2 * small:(h + 1) * 2 * small] = pair.astype(out.dtype)


def gradient_kernel(meta, x0, x1, x2, x3, m0, m1, m2, m3, conv):
    early, width = x0.shape[0], conv.shape[1]
    last = conv.shape[0] - early
    total = [jnp.zeros((size, width), F32) for size in (early, last)]
    for x, m in ((x0, m0), (x1, m1), (x2, m2), (x3, m3)):
        turned = m[last:]
        total[0] += dot(x[...], turned, (1, 1))
        total[1] += dot(m[:last], turned, (1, 1))
    conv[pl.ds(pl.multiple_of(meta[4] * last, last), last)] = total[0][:last]
    conv[last:2 * last] = total[0][last:]
    conv[pl.ds(pl.multiple_of((2 - meta[4]) * last, last), last)] = total[1]


def pack_kernel(meta, conv, p0, p1, p2, p3, own, send1, send2, send3):
    unit = conv.shape[0] // 12
    piece = unit // 4
    for q, out in enumerate((own, send1, send2, send3)):
        for g in range(6):
            at = 2 * g * unit + q * piece
            pair = jnp.concatenate([conv[at:at + piece], conv[at + unit:at + unit + piece]], 0)
            out[g * 2 * piece:(g + 1) * 2 * piece] = pair.astype(out.dtype)
        point = p0[q] + p1[q].astype(F32) + p2[q].astype(F32) + p3[q].astype(F32)
        out[12 * piece:] = point.astype(out.dtype)


def slice_kernel(meta, own, got1, got2, got3, kept, send1, send2, send3):
    total = own[...] + got1[...].astype(F32) + got2[...].astype(F32) + got3[...].astype(F32)
    piece = total.shape[0] // 16
    row, thin = piece // 4, piece // 8
    for t, out in enumerate((kept, send1, send2, send3)):
        parts = []
        for u in range(2):
            first = [(2 * g + u) * 2 * piece + t * row for g in range(3)]
            parts += [total[at:at + row] for at in first]
            for p in range(4):
                at = (12 + p) * piece + u * piece // 2 + t * thin
                parts.append(total[at:at + thin])
            parts += [total[at + piece:at + piece + row] for at in first]
        out[...] = jnp.concatenate(parts, 0).astype(out.dtype)


def split_sum_kernel(meta, own, got1, got2, got3, kept, to_z, to_core, to_both):
    total = own[...] + got1[...].astype(F32) + got2[...].astype(F32) + got3[...].astype(F32)
    half, size = total.shape[0] // 2, kept.shape[0]
    kept[...] = total[:size]
    to_core[...] = total[size:half]
    to_z[...] = total[half:half + size]
    to_both[...] = total[half + size:]


def output_kernel(meta, kept, from_z, from_core, from_both, conv, point):
    here, there = kept[...] + from_z[...], from_core[...] + from_both[...]
    taps, row = conv.shape[:2]
    width = here.shape[1]
    half = width // 2
    first = meta[0] == 0
    for t in range(taps):
        a, b = here[t * row:(t + 1) * row], there[t * row:(t + 1) * row]
        even, odd = jnp.where(first, a, b), jnp.where(first, b, a)
        conv[t] = jnp.concatenate([even[:, :half], odd[:, :half], even[:, half:], odd[:, half:]], 1)
    thin = point.shape[0]
    for p in range(point.shape[1] // width):
        at = taps * row + p * thin
        point[:, p * width:(p + 1) * width] = here[at:at + thin]


def input_kernel(meta, hg, flipped, hopped, mine, got, wfar, kept, other):
    core, zh = meta[0], meta[1]
    quarter = mine.shape[1]
    rows = kept.shape[0]
    grads = ((flipped[...], 2 - meta[4]), (hg[...], 1), (hopped[...], meta[4]))
    for weights, at, size in ((mine, zh * 2 + core, quarter), (got, zh * 2 + 1 - core, quarter), (wfar, 1 - zh, 2 * quarter)):
        total = sum(dot(grad, weights[t], (1, 1)) for grad, t in grads)
        kept[:, lanes(at, size)] = total[:rows]
        other[:, lanes(at, size)] = total[rows:]


def local(inputs, out_grad, conv_weight, point_weight):
    x, og = inputs[0], out_grad[0]
    rows, C = x.shape
    H = conv_weight.shape[2]
    Cq, Hq, Hh = C // 4, H // 4, H // 2
    piece = C // 32
    assert DILATION_STEP == 8 * rows
    dp, seq = lax.axis_index("dp"), lax.axis_index("seq")
    zh, core = dp // 2, dp % 2
    xi, zl, yi = seq // 16, seq // 4 % 4, seq % 4
    a, b = jnp.where(core == 0, xi, yi), jnp.where(core == 0, yi, xi)
    meta = jnp.stack([core, zh, a, b, jnp.where(zl < 2, 2, 0)]).astype(jnp.int32)

    def columns(value, c):
        return jnp.concatenate(
            [lax.dynamic_slice_in_dim(value, half * 2 * Hq + c * Hq, Hq, 2) for half in (0, 1)], axis=2
        )

    def mirror(x, y, z, c):
        return x, y, 7 - z, c

    def partner(x, y, z, c):
        return x, y, z, 1 - c

    def order(width, unit, count):
        new = jnp.arange(width)
        inner = new % (4 * unit)
        u = new // (4 * unit) % count
        r, q = new // (16 * unit * count), new // (4 * unit * count) % 4
        an, bn = (a + r) % 4, (b + q) % 4
        xn, yn = jnp.where(core == 0, an, bn), jnp.where(core == 0, bn, an)
        half = (zh + u) % 2 if count == 2 else 0
        old = half * (64 * unit) + xn * (16 * unit) + (zl + inner // unit) % 4 * (4 * unit) + yn * unit + inner % unit
        return (old[:, None] == jnp.arange(width)[None, :]).astype(BF16)

    def mirror(x, y, z, c):
        return x, y, 7 - z, c

    def partner(x, y, z, c):
        return x, y, z, 1 - c

    conv_piece = lax.dynamic_slice_in_dim(conv_weight, (xi * 4 + yi) % 8 * piece, piece, 1)
    point_piece = lax.dynamic_slice(point_weight, (xi * (Hq // 4), yi * Hh), (Hq // 4, Hh))
    holders = [d for d in range(256) if coords(d)[3] == coords(d)[0] // 2]
    conv_piece = send(conv_piece, mirror, holders)
    point_piece = send(point_piece, mirror)
    first = rows * 3 // 8
    flipped = flip(x[:first])
    x_other = send(x, partner)
    og_other = send(og, partner)
    conv_piece, point_piece, x_late, x_other, og_other, flipped, conv_weight = lax.optimization_barrier(
        (conv_piece, point_piece, x, x_other, og_other, flipped, conv_weight)
    )
    mine, theirs = run(split_kernel, meta, [conv_weight], [shape((3, Cq, Hh), BF16)] * 2)
    handed = send(columns(conv_piece, 1 - core), partner, holders)
    conv_piece = jnp.where(core == xi // 2, columns(conv_piece, core), handed)
    far = jnp.concatenate([conv_piece, point_piece[None]])
    flipped = jnp.concatenate([flipped, flip(x_late[first:])])
    fars = [send_a(far, -k) for k in (1, 2, 3)]
    far, flipped, mine, theirs, *fars = lax.optimization_barrier((far, flipped, mine, theirs, *fars))
    got = send(theirs, partner)
    hopped = hop(flipped)
    far = jnp.stack([far, *fars])
    fars = [far] + [send_b(far, -k) for k in (1, 2, 3)]
    flipped_other = send(flipped, partner)
    spread = order(Cq, Cq // 64, 1)
    taps, ogs, near, arriving, *early = run(
        near_kernel, meta, [flipped, flipped_other, x, x_other, og, og_other, mine, got, point_weight, spread],
        [shape((2, 2 * rows, C), BF16), shape((2 * rows, C), BF16), shape((2 * rows, Hh), F32),
         shape((2 * rows, Hq), F32)] + [shape((2 * Cq, 2 * rows), BF16)] * 4,
    )
    hopped, taps = lax.optimization_barrier((hopped, taps))
    hopped_other = send(hopped, partner)
    tap, near, *late = run(
        late_kernel, meta, [hopped, hopped_other, near, mine, got, spread],
        [shape((2 * rows, C), BF16), shape((2 * rows, Hh), F32)] + [shape((Cq, 2 * rows), BF16)] * 4,
    )
    rest = lax.optimization_barrier((*fars, *early, *late))
    fars, early, late = rest[:4], rest[4:8], rest[8:]
    early = [early[0]] + [send_a(part, k + 1) for k, part in enumerate(early[1:])]
    hg, hidden_t, wfar, *messages = run(
        forward_kernel, meta, [taps, tap, ogs, near, arriving, *fars, order(Hh, Hq // 64, 2), *late],
        [shape((2 * rows, Hh), BF16), shape((Hh, 2 * rows), BF16), shape((3, 16, piece, Hh), BF16)]
        + [shape((Cq + Hh, 2 * rows), BF16)] * 4,
        [pltpu.VMEM((4, 4, Hq // 4, Hh), BF16)],
    )
    for k in (1, 2, 3):
        early[k], messages[k] = lax.optimization_barrier((early[k], messages[k]))
    messages = [messages[0]] + [send_a(part, k + 1) for k, part in enumerate(messages[1:])]
    block = (4, Hh // 4, Hh)
    p_own, *sends = run(point_kernel, meta, [ogs, hidden_t], [shape(block, F32)] + [shape(block, BF16)] * 3)
    p_all = [p_own] + [send_a(part, k + 1) for k, part in enumerate(sends)]
    hg_flipped = flip(hg)
    conv, = run(gradient_kernel, meta, [*early, *messages], [shape((3 * Cq, Hh), F32)])
    hg_flipped, conv, *p_all = lax.optimization_barrier((hg_flipped, conv, *p_all))
    hg_hopped = hop(hg_flipped)
    n = 12 * (Cq // 16)
    big = (n + Hh // 4, Hh)
    total, *sends = run(pack_kernel, meta, [conv, *p_all], [shape(big, F32)] + [shape(big, BF16)] * 3)
    got_b = [send_b(part, k + 1) for k, part in enumerate(sends)]
    *got_b, hg_hopped = lax.optimization_barrier((*got_b, hg_hopped))
    small = (big[0] // 4, Hh)
    last, *sends = run(
        slice_kernel, meta, [total, *got_b],
        [shape(small, F32)] + [shape(small, BF16)] * 3,
    )
    hg_late, last = lax.optimization_barrier((hg, last))
    mine_rows, other_rows = run(
        input_kernel, meta, [hg_late, hg_flipped, hg_hopped, mine, got, wfar.reshape(3, 2 * Cq, Hh)],
        [shape((rows, C), F32)] * 2,
    )
    in_grad = (og.astype(F32) + mine_rows + send(other_rows, partner)).astype(BF16)
    got_z = [
        send(part, lambda x, y, z, c: (x, y, z // 4 * 4 + (z + t + 1) % 4, c)) for t, part in enumerate(sends)
    ]
    conv_rows = 3 * (Cq // 64)
    point_rows = small[0] // 2 - 2 * conv_rows
    halves = (conv_rows + point_rows, Hh), (conv_rows, Hh)
    kept, to_z, to_core, to_both = run(
        split_sum_kernel, meta, [last, *got_z], [shape(halves[k], F32) for k in (0, 0, 1, 1)]
    )
    from_z = send(to_z, lambda x, y, z, c: (x, y, z + 4, c))
    from_both = send(to_both, lambda x, y, z, c: (x, y, z + 4, 1 - c))
    in_grad, from_core = lax.optimization_barrier((in_grad, send(to_core, partner)))
    conv_mine, point_mine = run(
        output_kernel, meta, [kept, from_z, from_core, from_both],
        [shape((3, Cq // 64, H), F32), shape((Hq // 64, C), F32)],
    )
    return in_grad[None], conv_mine, point_mine


def solution(mesh):
    placed = (P("dp", "seq", None), P("dp", "seq", None), P(None, "dp", None), P("dp", None))
    return jax.shard_map(
        local,
        mesh=mesh,
        in_specs=placed,
        out_specs=(P("dp", "seq", None), P(None, ("dp", "seq"), None), P(("dp", "seq"), None)),
        check_vma=False,
    )
```

```python
import jax
import jax.numpy as jnp
from jax import lax
from jax.experimental import pallas as pl
from jax.experimental.pallas import tpu as pltpu
from jax.sharding import PartitionSpec as P

DILATION_STEP = 1024
BF16 = jnp.bfloat16
F32 = jnp.float32


def coords(index):
    dp, seq = divmod(index, 64)
    return seq // 16, seq % 4, (dp // 2) * 4 + (seq // 4) % 4, dp % 2


def index_of(x, y, z, core):
    return ((z % 8) // 4 * 2 + core % 2) * 64 + (x % 4) * 16 + (z % 4) * 4 + y % 4


def send(value, target, sources=range(256)):
    pairs = [(device, index_of(*target(*coords(device)))) for device in sources]
    return lax.ppermute(value, ("dp", "seq"), pairs)


def send_a(value, steps):
    return send(value, lambda x, y, z, c: (x + steps * (1 - c), y + steps * c, z, c))


def send_b(value, steps):
    return send(value, lambda x, y, z, c: (x + steps * c, y + steps * (1 - c), z, c))


def flip(value):
    return send(value, lambda x, y, z, c: (x, y, z // 4 * 4 + (z + 2) % 4, c))


def hop(value):
    up = [d for d in range(256) if coords(d)[2] % 4 < 2 and coords(d)[0] < 3]
    down = [d for d in range(256) if coords(d)[2] % 4 >= 2 and coords(d)[0] > 0]
    return send(value, lambda x, y, z, c: (x + 1 if z % 4 < 2 else x - 1, y, z, c), up + down)


def dot(left, right, dims):
    return lax.dot_general(left, right, ((dims[:1], dims[1:]), ((), ())), preferred_element_type=F32)


def pick(value, axis, index):
    return lax.dynamic_index_in_dim(value, index, axis, keepdims=False)


def run(kernel, scalars, arrays, outs, scratch=()):
    vmem = pl.BlockSpec(memory_space=pltpu.VMEM)
    return pl.pallas_call(
        kernel,
        out_shape=outs,
        in_specs=[pl.BlockSpec(memory_space=pltpu.SMEM)] + [vmem] * len(arrays),
        out_specs=[vmem] * len(outs),
        scratch_shapes=scratch,
        compiler_params=pltpu.CompilerParams(vmem_limit_bytes=48 * 1024 * 1024),
        cost_estimate=pl.CostEstimate(flops=1, bytes_accessed=1, transcendentals=0),
    )(scalars, *arrays)


def shape(dims, dtype):
    return jax.ShapeDtypeStruct(tuple(dims), dtype)


def lanes(start, size):
    return pl.ds(pl.multiple_of(start * size, size), size)


def split_kernel(meta, weight, mine, theirs):
    size = weight.shape[2] // 4
    for t in range(3):
        value = weight[t]
        parts = [value[:, k * size:(k + 1) * size] for k in range(4)]
        even, odd = jnp.concatenate(parts[::2], 1), jnp.concatenate(parts[1::2], 1)
        first = meta[0] == 0
        mine[t] = jnp.where(first, even, odd)
        theirs[t] = jnp.where(first, odd, even)


def spread_block(meta, block, order, outs, first):
    core, zh = meta[0], meta[1]
    quarter = order.shape[0]
    unit = quarter // 4
    for u in range(2):
        for v in range(2):
            columns = lanes(lax.rem(zh + u, 2) * 2 + lax.rem(core + v, 2), quarter)
            moved = dot(order[...], block[:, columns], (1, 1)).astype(BF16)
            at = first + (u * 2 + v) * unit
            for r, out in enumerate(outs):
                out[at:at + unit] = moved[r * unit:(r + 1) * unit]


def near_kernel(meta, x0, x0o, x1, x1o, og, ogo, mine, got, pw, order, taps, ogs, pre, arriving,
                keep, send1, send2, send3):
    core, zh = meta[0], meta[1]
    rows, quarter = x0.shape[0], mine.shape[1]
    ogs[:rows] = og[...]
    ogs[rows:] = ogo[...]
    total = jnp.zeros(pre.shape, F32)
    for k, (own, other) in enumerate(((x0, x0o), (x1, x1o))):
        taps[k, :rows] = own[...]
        taps[k, rows:] = other[...]
        t = meta[4] if k == 0 else 1
        total += dot(taps[k, :, lanes(zh * 2 + core, quarter)], mine[t], (1, 0))
        total += dot(taps[k, :, lanes(zh * 2 + 1 - core, quarter)], got[t], (1, 0))
    pre[...] = total
    arriving[...] = dot(ogs[...], pw[...], (1, 1))
    outs = (keep, send1, send2, send3)
    for k in range(2):
        spread_block(meta, taps.at[k], order, outs, k * quarter)


def late_kernel(meta, x2, x2o, near, mine, got, order, tap, pre, own, send1, send2, send3):
    core, zh = meta[0], meta[1]
    rows, quarter = x2.shape[0], order.shape[0]
    tap[:rows] = x2[...]
    tap[rows:] = x2o[...]
    t = 2 - meta[4]
    total = near[...] + dot(tap[:, lanes(zh * 2 + core, quarter)], mine[t], (1, 0))
    pre[...] = total + dot(tap[:, lanes(zh * 2 + 1 - core, quarter)], got[t], (1, 0))
    spread_block(meta, tap, order, (own, send1, send2, send3), 0)


def forward_kernel(meta, taps, tap2, ogs, near, arriving, far0, far1, far2, far3, order,
                   x0, x1, x2, x3, hg, hidden_t, wfar, m0, m1, m2, m3, pws):
    core, zh, a, b = (meta[i] for i in range(4))
    piece, width = far0.shape[2:]
    half = 16 * piece
    for j, far in enumerate((far0, far1, far2, far3)):
        for k in range(4):
            ak, bj = lax.rem(a + k, 4), lax.rem(b + j, 4)
            x, y = jnp.where(core == 0, ak, bj), jnp.where(core == 0, bj, ak)
            for t in range(3):
                wfar[t, x * 4 + y] = far[k, t]
            pws[y, x] = far[k, 3]
    pre = near[...]
    for k, t in enumerate((meta[4], 1, 2 - meta[4])):
        columns = lanes(1 - zh, half)
        block = tap2[:, columns] if k == 2 else taps[k, :, columns]
        pre += dot(block, wfar[t].reshape(half, width), (1, 0))
    other = jnp.zeros(arriving.shape, F32)
    for y in range(4):
        other += dot(ogs[:, y * width:(y + 1) * width], pws[y].reshape(4 * piece, width), (1, 1))
    pair = (arriving[...], other)
    grads = jnp.where(zh == 0, jnp.concatenate(pair, 1), jnp.concatenate(pair[::-1], 1))
    scale, cubic = 0.7978845608028654, 0.044715
    square = pre * pre
    tanh = jnp.tanh(scale * (pre + cubic * (square * pre)))
    gate = 0.5 * (1.0 + tanh)
    slope = gate + 0.5 * pre * (1.0 - tanh * tanh) * (scale * (1.0 + 3.0 * cubic * square))
    grads = (grads * slope).astype(BF16)
    hg[...] = grads
    count = x0.shape[0]
    place = [lax.broadcasted_iota(jnp.int32, (width, width), axis) for axis in (0, 1)]
    turned = dot((place[0] == place[1]).astype(BF16), grads, (1, 1)).astype(BF16)
    for x, message in ((x0, m0), (x1, m1), (x2, m2), (x3, m3)):
        message[:count] = x[...]
        message[count:] = turned
    hidden_t[...] = dot(order[...], (pre * gate).astype(BF16), (1, 1)).astype(BF16)


def point_kernel(meta, ogs, hidden_t, own, send1, send2, send3):
    width = own.shape[2]
    unit = hidden_t.shape[0] // 4
    small = unit // 4
    for h in range(ogs.shape[1] // (2 * width)):
        parts = [dot(hidden_t[...], ogs[:, (2 * h + p) * width:(2 * h + p + 1) * width], (1, 0)) for p in range(2)]
        for r, out in enumerate((own, send1, send2, send3)):
            for q in range(4):
                at = r * unit + q * small
                pair = jnp.concatenate([p[at:at + small] for p in parts], 0)
                out[q, h * 2 * small:(h + 1) * 2 * small] = pair.astype(out.dtype)


def gradient_kernel(meta, x0, x1, x2, x3, m0, m1, m2, m3, conv):
    early, width = x0.shape[0], conv.shape[1]
    last = conv.shape[0] - early
    total = [jnp.zeros((size, width), F32) for size in (early, last)]
    for x, m in ((x0, m0), (x1, m1), (x2, m2), (x3, m3)):
        turned = m[last:]
        total[0] += dot(x[...], turned, (1, 1))
        total[1] += dot(m[:last], turned, (1, 1))
    conv[pl.ds(pl.multiple_of(meta[4] * last, last), last)] = total[0][:last]
    conv[last:2 * last] = total[0][last:]
    conv[pl.ds(pl.multiple_of((2 - meta[4]) * last, last), last)] = total[1]


def pack_kernel(meta, conv, p0, p1, p2, p3, own, send1, send2, send3):
    unit = conv.shape[0] // 12
    piece = unit // 4
    for q, out in enumerate((own, send1, send2, send3)):
        for g in range(6):
            at = 2 * g * unit + q * piece
            pair = jnp.concatenate([conv[at:at + piece], conv[at + unit:at + unit + piece]], 0)
            out[g * 2 * piece:(g + 1) * 2 * piece] = pair.astype(out.dtype)
        point = p0[q] + p1[q].astype(F32) + p2[q].astype(F32) + p3[q].astype(F32)
        out[12 * piece:] = point.astype(out.dtype)


def slice_kernel(meta, own, got1, got2, got3, out):
    total = own[...] + got1[...].astype(F32) + got2[...].astype(F32) + got3[...].astype(F32)
    piece = total.shape[0] // 16
    row, thin = piece // 4, piece // 8
    for t in range(4):
        for u in range(2):
            first = [(2 * g + u) * 2 * piece + t * row for g in range(3)]
            parts = [total[at:at + row] for at in first]
            for p in range(4):
                at = (12 + p) * piece + u * piece // 2 + t * thin
                parts.append(total[at:at + thin])
            parts += [total[at + piece:at + piece + row] for at in first]
            z = lax.rem(meta[1] + u, 2) * 4 + lax.rem(meta[5] + t, 4)
            out[z] = jnp.concatenate(parts, 0).astype(out.dtype)


def split_sum_kernel(meta, parts, kept, to_core):
    total = sum(parts[z].astype(F32) for z in range(parts.shape[0]))
    size = kept.shape[0]
    kept[...] = total[:size]
    to_core[...] = total[size:]


def output_kernel(meta, kept, from_core, conv, point):
    here, there = kept[...], from_core[...]
    taps, row = conv.shape[:2]
    width = here.shape[1]
    half = width // 2
    first = meta[0] == 0
    for t in range(taps):
        a, b = here[t * row:(t + 1) * row], there[t * row:(t + 1) * row]
        even, odd = jnp.where(first, a, b), jnp.where(first, b, a)
        conv[t] = jnp.concatenate([even[:, :half], odd[:, :half], even[:, half:], odd[:, half:]], 1)
    thin = point.shape[0]
    for p in range(point.shape[1] // width):
        at = taps * row + p * thin
        point[:, p * width:(p + 1) * width] = here[at:at + thin]


def input_kernel(meta, hg, flipped, hopped, mine, got, wfar, kept, other):
    core, zh = meta[0], meta[1]
    quarter = mine.shape[1]
    rows = kept.shape[0]
    grads = ((flipped[...], 2 - meta[4]), (hg[...], 1), (hopped[...], meta[4]))
    for weights, at, size in ((mine, zh * 2 + core, quarter), (got, zh * 2 + 1 - core, quarter), (wfar, 1 - zh, 2 * quarter)):
        total = sum(dot(grad, weights[t], (1, 1)) for grad, t in grads)
        kept[:, lanes(at, size)] = total[:rows]
        other[:, lanes(at, size)] = total[rows:]


def local(inputs, out_grad, conv_weight, point_weight):
    x, og = inputs[0], out_grad[0]
    rows, C = x.shape
    H = conv_weight.shape[2]
    Cq, Hq, Hh = C // 4, H // 4, H // 2
    piece = C // 32
    assert DILATION_STEP == 8 * rows
    dp, seq = lax.axis_index("dp"), lax.axis_index("seq")
    zh, core = dp // 2, dp % 2
    xi, zl, yi = seq // 16, seq // 4 % 4, seq % 4
    a, b = jnp.where(core == 0, xi, yi), jnp.where(core == 0, yi, xi)
    meta = jnp.stack([core, zh, a, b, jnp.where(zl < 2, 2, 0), zl]).astype(jnp.int32)

    def columns(value, c):
        return jnp.concatenate(
            [lax.dynamic_slice_in_dim(value, half * 2 * Hq + c * Hq, Hq, 2) for half in (0, 1)], axis=2
        )

    def mirror(x, y, z, c):
        return x, y, 7 - z, c

    def partner(x, y, z, c):
        return x, y, z, 1 - c

    def order(width, unit, count):
        new = jnp.arange(width)
        inner = new % (4 * unit)
        u = new // (4 * unit) % count
        r, q = new // (16 * unit * count), new // (4 * unit * count) % 4
        an, bn = (a + r) % 4, (b + q) % 4
        xn, yn = jnp.where(core == 0, an, bn), jnp.where(core == 0, bn, an)
        half = (zh + u) % 2 if count == 2 else 0
        old = half * (64 * unit) + xn * (16 * unit) + (zl + inner // unit) % 4 * (4 * unit) + yn * unit + inner % unit
        return (old[:, None] == jnp.arange(width)[None, :]).astype(BF16)

    def mirror(x, y, z, c):
        return x, y, 7 - z, c

    def partner(x, y, z, c):
        return x, y, z, 1 - c

    conv_piece = lax.dynamic_slice_in_dim(conv_weight, (xi * 4 + yi) % 8 * piece, piece, 1)
    point_piece = lax.dynamic_slice(point_weight, (xi * (Hq // 4), yi * Hh), (Hq // 4, Hh))
    holders = [d for d in range(256) if coords(d)[3] == coords(d)[0] // 2]
    conv_piece = send(conv_piece, mirror, holders)
    point_piece = send(point_piece, mirror)
    first, tail = flip(x[:rows // 2]), x[rows // 2:]
    x_other = send(x, partner)
    og_other = send(og, partner)
    conv_piece, point_piece, tail, x_other, og_other, first, conv_weight = lax.optimization_barrier(
        (conv_piece, point_piece, tail, x_other, og_other, first, conv_weight)
    )
    mine, theirs = run(split_kernel, meta, [conv_weight], [shape((3, Cq, Hh), BF16)] * 2)
    handed = send(columns(conv_piece, 1 - core), partner, holders)
    conv_piece = jnp.where(core == xi // 2, columns(conv_piece, core), handed)
    far = jnp.concatenate([conv_piece, point_piece[None]])
    tail, hopped = flip(tail), hop(first)
    fars = [send_a(far, -k) for k in (1, 2, 3)]
    far, first, tail, hopped, mine, theirs, *fars = lax.optimization_barrier(
        (far, first, tail, hopped, mine, theirs, *fars)
    )
    flipped = jnp.concatenate([first, tail])
    got = send(theirs, partner)
    hopped = jnp.concatenate([hopped, hop(tail)])
    far = jnp.stack([far, *fars])
    fars = [far] + [send_b(far, -k) for k in (1, 2, 3)]
    flipped, got = lax.optimization_barrier((flipped, got))
    flipped_other = send(flipped, partner)
    spread = order(Cq, Cq // 64, 1)
    taps, ogs, near, arriving, *early = run(
        near_kernel, meta, [flipped, flipped_other, x, x_other, og, og_other, mine, got, point_weight, spread],
        [shape((2, 2 * rows, C), BF16), shape((2 * rows, C), BF16), shape((2 * rows, Hh), F32),
         shape((2 * rows, Hq), F32)] + [shape((2 * Cq, 2 * rows), BF16)] * 4,
    )
    hopped, taps = lax.optimization_barrier((hopped, taps))
    hopped_other = send(hopped, partner)
    tap, near, *late = run(
        late_kernel, meta, [hopped, hopped_other, near, mine, got, spread],
        [shape((2 * rows, C), BF16), shape((2 * rows, Hh), F32)] + [shape((Cq, 2 * rows), BF16)] * 4,
    )
    rest = lax.optimization_barrier((*fars, *early, *late))
    fars, early, late = rest[:4], rest[4:8], rest[8:]
    early = [early[0]] + [send_a(part, k + 1) for k, part in enumerate(early[1:])]
    hg, hidden_t, wfar, *messages = run(
        forward_kernel, meta, [taps, tap, ogs, near, arriving, *fars, order(Hh, Hq // 64, 2), *late],
        [shape((2 * rows, Hh), BF16), shape((Hh, 2 * rows), BF16), shape((3, 16, piece, Hh), BF16)]
        + [shape((Cq + Hh, 2 * rows), BF16)] * 4,
        [pltpu.VMEM((4, 4, Hq // 4, Hh), BF16)],
    )
    for k in (1, 2, 3):
        early[k], messages[k] = lax.optimization_barrier((early[k], messages[k]))
    messages = [messages[0]] + [send_a(part, k + 1) for k, part in enumerate(messages[1:])]
    block = (4, Hh // 4, Hh)
    p_own, *sends = run(point_kernel, meta, [ogs, hidden_t], [shape(block, F32)] + [shape(block, BF16)] * 3)
    hg_flipped, *sends = lax.optimization_barrier((flip(hg), *sends))
    p_all = [p_own] + [send_a(part, k + 1) for k, part in enumerate(sends)]
    conv, = run(gradient_kernel, meta, [*early, *messages], [shape((3 * Cq, Hh), F32)])
    hg_late, conv = lax.optimization_barrier((hg_flipped, conv))
    hg_hopped = hop(hg_late)
    n = 12 * (Cq // 16)
    big = (n + Hh // 4, Hh)
    total, *sends = run(pack_kernel, meta, [conv, *p_all], [shape(big, F32)] + [shape(big, BF16)] * 3)
    got_b = [send_b(part, k + 1) for k, part in enumerate(sends)]
    half = big[0] // 8
    by_z, = run(slice_kernel, meta, [total, *got_b], [shape((8, half, Hh), BF16)])
    hg_late, by_z = lax.optimization_barrier((hg, by_z))
    mine_rows, other_rows = run(
        input_kernel, meta, [hg_late, hg_flipped, hg_hopped, mine, got, wfar.reshape(3, 2 * Cq, Hh)],
        [shape((rows, C), F32)] * 2,
    )
    in_grad = (og.astype(F32) + mine_rows + send(other_rows, partner)).astype(BF16)
    rings = [[index_of(x, y, z, c) for z in range(8)] for x in range(4) for y in range(4) for c in range(2)]
    by_z = lax.all_to_all(by_z, ("dp", "seq"), 0, 0, axis_index_groups=rings)
    conv_rows = 3 * (Cq // 64)
    kept, to_core = run(
        split_sum_kernel, meta, [by_z], [shape((half - conv_rows, Hh), F32), shape((conv_rows, Hh), F32)]
    )
    in_grad, from_core = lax.optimization_barrier((in_grad, send(to_core, partner)))
    conv_mine, point_mine = run(
        output_kernel, meta, [kept, from_core], [shape((3, Cq // 64, H), F32), shape((Hq // 64, C), F32)]
    )
    return in_grad[None], conv_mine, point_mine


def solution(mesh):
    placed = (P("dp", "seq", None), P("dp", "seq", None), P(None, "dp", None), P("dp", None))
    return jax.shard_map(
        local,
        mesh=mesh,
        in_specs=placed,
        out_specs=(P("dp", "seq", None), P(None, ("dp", "seq"), None), P(("dp", "seq"), None)),
        check_vma=False,
    )
```

```python
import jax
import jax.numpy as jnp
from jax import lax
from jax.experimental import pallas as pl
from jax.experimental.pallas import tpu as pltpu
from jax.sharding import PartitionSpec as P

DILATION_STEP = 1024
BF16 = jnp.bfloat16
F32 = jnp.float32


def coords(index):
    dp, seq = divmod(index, 64)
    return seq // 16, seq % 4, (dp // 2) * 4 + (seq // 4) % 4, dp % 2


def index_of(x, y, z, core):
    return ((z % 8) // 4 * 2 + core % 2) * 64 + (x % 4) * 16 + (z % 4) * 4 + y % 4


def send(value, target, sources=range(256)):
    pairs = [(device, index_of(*target(*coords(device)))) for device in sources]
    return lax.ppermute(value, ("dp", "seq"), pairs)


def send_a(value, steps):
    return send(value, lambda x, y, z, c: (x + steps * (1 - c), y + steps * c, z, c))


def send_b(value, steps):
    return send(value, lambda x, y, z, c: (x + steps * c, y + steps * (1 - c), z, c))


def flip(value):
    return send(value, lambda x, y, z, c: (x, y, z // 4 * 4 + (z + 2) % 4, c))


def hop(value):
    up = [d for d in range(256) if coords(d)[2] % 4 < 2 and coords(d)[0] < 3]
    down = [d for d in range(256) if coords(d)[2] % 4 >= 2 and coords(d)[0] > 0]
    return send(value, lambda x, y, z, c: (x + 1 if z % 4 < 2 else x - 1, y, z, c), up + down)


def dot(left, right, dims):
    return lax.dot_general(left, right, ((dims[:1], dims[1:]), ((), ())), preferred_element_type=F32)


def pick(value, axis, index):
    return lax.dynamic_index_in_dim(value, index, axis, keepdims=False)


def run(kernel, scalars, arrays, outs, scratch=()):
    vmem = pl.BlockSpec(memory_space=pltpu.VMEM)
    return pl.pallas_call(
        kernel,
        out_shape=outs,
        in_specs=[pl.BlockSpec(memory_space=pltpu.SMEM)] + [vmem] * len(arrays),
        out_specs=[vmem] * len(outs),
        scratch_shapes=scratch,
        compiler_params=pltpu.CompilerParams(vmem_limit_bytes=48 * 1024 * 1024),
        cost_estimate=pl.CostEstimate(flops=1, bytes_accessed=1, transcendentals=0),
    )(scalars, *arrays)


def shape(dims, dtype):
    return jax.ShapeDtypeStruct(tuple(dims), dtype)


def lanes(start, size):
    return pl.ds(pl.multiple_of(start * size, size), size)


def split_kernel(meta, weight, mine, theirs):
    size = weight.shape[2] // 4
    for t in range(3):
        value = weight[t]
        parts = [value[:, k * size:(k + 1) * size] for k in range(4)]
        even, odd = jnp.concatenate(parts[::2], 1), jnp.concatenate(parts[1::2], 1)
        first = meta[0] == 0
        mine[t] = jnp.where(first, even, odd)
        theirs[t] = jnp.where(first, odd, even)


def spread_block(meta, block, order, outs, first):
    core, zh = meta[0], meta[1]
    quarter = order.shape[0]
    unit = quarter // 4
    for u in range(2):
        for v in range(2):
            columns = lanes(lax.rem(zh + u, 2) * 2 + lax.rem(core + v, 2), quarter)
            moved = dot(order[...], block[:, columns], (1, 1)).astype(BF16)
            at = first + (u * 2 + v) * unit
            for r, out in enumerate(outs):
                out[at:at + unit] = moved[r * unit:(r + 1) * unit]


def near_kernel(meta, x0, x0o, x1, x1o, og, ogo, mine, got, pw, order, taps, ogs, pre, arriving,
                keep, send1, send2, send3):
    core, zh = meta[0], meta[1]
    rows, quarter = x0.shape[0], mine.shape[1]
    ogs[:rows] = og[...]
    ogs[rows:] = ogo[...]
    total = jnp.zeros(pre.shape, F32)
    for k, (own, other) in enumerate(((x0, x0o), (x1, x1o))):
        taps[k, :rows] = own[...]
        taps[k, rows:] = other[...]
        t = meta[4] if k == 0 else 1
        total += dot(taps[k, :, lanes(zh * 2 + core, quarter)], mine[t], (1, 0))
        total += dot(taps[k, :, lanes(zh * 2 + 1 - core, quarter)], got[t], (1, 0))
    pre[...] = total
    arriving[...] = dot(ogs[...], pw[...], (1, 1))
    outs = (keep, send1, send2, send3)
    for k in range(2):
        spread_block(meta, taps.at[k], order, outs, k * quarter)


def late_kernel(meta, x2, x2o, near, mine, got, order, tap, pre, own, send1, send2, send3):
    core, zh = meta[0], meta[1]
    rows, quarter = x2.shape[0], order.shape[0]
    tap[:rows] = x2[...]
    tap[rows:] = x2o[...]
    t = 2 - meta[4]
    total = near[...] + dot(tap[:, lanes(zh * 2 + core, quarter)], mine[t], (1, 0))
    pre[...] = total + dot(tap[:, lanes(zh * 2 + 1 - core, quarter)], got[t], (1, 0))
    spread_block(meta, tap, order, (own, send1, send2, send3), 0)


def forward_kernel(meta, taps, tap2, ogs, near, arriving, far0, far1, far2, far3, order,
                   x0, x1, x2, x3, hg, hidden_t, wfar, m0, m1, m2, m3, pws):
    core, zh, a, b = (meta[i] for i in range(4))
    piece, width = far0.shape[2:]
    half = 16 * piece
    for j, far in enumerate((far0, far1, far2, far3)):
        for k in range(4):
            ak, bj = lax.rem(a + k, 4), lax.rem(b + j, 4)
            x, y = jnp.where(core == 0, ak, bj), jnp.where(core == 0, bj, ak)
            for t in range(3):
                wfar[t, x * 4 + y] = far[k, t]
            pws[y, x] = far[k, 3]
    pre = near[...]
    for k, t in enumerate((meta[4], 1, 2 - meta[4])):
        columns = lanes(1 - zh, half)
        block = tap2[:, columns] if k == 2 else taps[k, :, columns]
        pre += dot(block, wfar[t].reshape(half, width), (1, 0))
    other = jnp.zeros(arriving.shape, F32)
    for y in range(4):
        other += dot(ogs[:, y * width:(y + 1) * width], pws[y].reshape(4 * piece, width), (1, 1))
    pair = (arriving[...], other)
    grads = jnp.where(zh == 0, jnp.concatenate(pair, 1), jnp.concatenate(pair[::-1], 1))
    scale, cubic = 0.7978845608028654, 0.044715
    square = pre * pre
    tanh = jnp.tanh(scale * (pre + cubic * (square * pre)))
    gate = 0.5 * (1.0 + tanh)
    slope = gate + 0.5 * pre * (1.0 - tanh * tanh) * (scale * (1.0 + 3.0 * cubic * square))
    grads = (grads * slope).astype(BF16)
    hg[...] = grads
    count = x0.shape[0]
    place = [lax.broadcasted_iota(jnp.int32, (width, width), axis) for axis in (0, 1)]
    turned = dot((place[0] == place[1]).astype(BF16), grads, (1, 1)).astype(BF16)
    for x, message in ((x0, m0), (x1, m1), (x2, m2), (x3, m3)):
        message[:count] = x[...]
        message[count:] = turned
    hidden_t[...] = dot(order[...], (pre * gate).astype(BF16), (1, 1)).astype(BF16)


def point_kernel(meta, ogs, hidden_t, own, send1, send2, send3):
    width = own.shape[2]
    unit = hidden_t.shape[0] // 4
    small = unit // 4
    for h in range(ogs.shape[1] // (2 * width)):
        parts = [dot(hidden_t[...], ogs[:, (2 * h + p) * width:(2 * h + p + 1) * width], (1, 0)) for p in range(2)]
        for r, out in enumerate((own, send1, send2, send3)):
            for q in range(4):
                at = r * unit + q * small
                pair = jnp.concatenate([p[at:at + small] for p in parts], 0)
                out[q, h * 2 * small:(h + 1) * 2 * small] = pair.astype(out.dtype)


def gradient_kernel(meta, x0, x1, x2, x3, m0, m1, m2, m3, conv):
    early, width = x0.shape[0], conv.shape[1]
    last = conv.shape[0] - early
    total = [jnp.zeros((size, width), F32) for size in (early, last)]
    for x, m in ((x0, m0), (x1, m1), (x2, m2), (x3, m3)):
        turned = m[last:]
        total[0] += dot(x[...], turned, (1, 1))
        total[1] += dot(m[:last], turned, (1, 1))
    conv[pl.ds(pl.multiple_of(meta[4] * last, last), last)] = total[0][:last]
    conv[last:2 * last] = total[0][last:]
    conv[pl.ds(pl.multiple_of((2 - meta[4]) * last, last), last)] = total[1]


def pack_kernel(meta, conv, p0, p1, p2, p3, own, send1, send2, send3):
    unit = conv.shape[0] // 12
    piece = unit // 4
    for q, out in enumerate((own, send1, send2, send3)):
        for g in range(6):
            at = 2 * g * unit + q * piece
            pair = jnp.concatenate([conv[at:at + piece], conv[at + unit:at + unit + piece]], 0)
            out[g * 2 * piece:(g + 1) * 2 * piece] = pair.astype(out.dtype)
        point = p0[q] + p1[q].astype(F32) + p2[q].astype(F32) + p3[q].astype(F32)
        out[12 * piece:] = point.astype(out.dtype)


def slice_kernel(meta, own, got1, got2, got3, out):
    total = own[...] + got1[...].astype(F32) + got2[...].astype(F32) + got3[...].astype(F32)
    piece = total.shape[0] // 16
    row, thin = piece // 4, piece // 8
    for t in range(4):
        for u in range(2):
            first = [(2 * g + u) * 2 * piece + t * row for g in range(3)]
            parts = [total[at:at + row] for at in first]
            for p in range(4):
                at = (12 + p) * piece + u * piece // 2 + t * thin
                parts.append(total[at:at + thin])
            parts += [total[at + piece:at + piece + row] for at in first]
            z = lax.rem(meta[1] + u, 2) * 4 + lax.rem(meta[5] + t, 4)
            out[z] = jnp.concatenate(parts, 0).astype(out.dtype)


def split_sum_kernel(meta, parts, kept, to_core):
    total = sum(parts[z].astype(F32) for z in range(parts.shape[0]))
    size = kept.shape[0]
    kept[...] = total[:size]
    to_core[...] = total[size:]


def output_kernel(meta, kept, from_core, conv, point):
    here, there = kept[...], from_core[...]
    taps, row = conv.shape[:2]
    width = here.shape[1]
    half = width // 2
    first = meta[0] == 0
    for t in range(taps):
        a, b = here[t * row:(t + 1) * row], there[t * row:(t + 1) * row]
        even, odd = jnp.where(first, a, b), jnp.where(first, b, a)
        conv[t] = jnp.concatenate([even[:, :half], odd[:, :half], even[:, half:], odd[:, half:]], 1)
    thin = point.shape[0]
    for p in range(point.shape[1] // width):
        at = taps * row + p * thin
        point[:, p * width:(p + 1) * width] = here[at:at + thin]


def input_kernel(meta, hg, flipped, hopped, mine, got, wfar, kept, other):
    core, zh = meta[0], meta[1]
    quarter = mine.shape[1]
    rows = kept.shape[0]
    grads = ((flipped[...], 2 - meta[4]), (hg[...], 1), (hopped[...], meta[4]))
    for weights, at, size in ((mine, zh * 2 + core, quarter), (got, zh * 2 + 1 - core, quarter), (wfar, 1 - zh, 2 * quarter)):
        total = sum(dot(grad, weights[t], (1, 1)) for grad, t in grads)
        kept[:, lanes(at, size)] = total[:rows]
        other[:, lanes(at, size)] = total[rows:]


def local(inputs, out_grad, conv_weight, point_weight):
    x, og = inputs[0], out_grad[0]
    rows, C = x.shape
    H = conv_weight.shape[2]
    Cq, Hq, Hh = C // 4, H // 4, H // 2
    piece = C // 32
    assert DILATION_STEP == 8 * rows
    dp, seq = lax.axis_index("dp"), lax.axis_index("seq")
    zh, core = dp // 2, dp % 2
    xi, zl, yi = seq // 16, seq // 4 % 4, seq % 4
    a, b = jnp.where(core == 0, xi, yi), jnp.where(core == 0, yi, xi)
    meta = jnp.stack([core, zh, a, b, jnp.where(zl < 2, 2, 0), zl]).astype(jnp.int32)

    def columns(value, c):
        return jnp.concatenate(
            [lax.dynamic_slice_in_dim(value, half * 2 * Hq + c * Hq, Hq, 2) for half in (0, 1)], axis=2
        )

    def mirror(x, y, z, c):
        return x, y, 7 - z, c

    def partner(x, y, z, c):
        return x, y, z, 1 - c

    def order(width, unit, count):
        new = jnp.arange(width)
        inner = new % (4 * unit)
        u = new // (4 * unit) % count
        r, q = new // (16 * unit * count), new // (4 * unit * count) % 4
        an, bn = (a + r) % 4, (b + q) % 4
        xn, yn = jnp.where(core == 0, an, bn), jnp.where(core == 0, bn, an)
        half = (zh + u) % 2 if count == 2 else 0
        old = half * (64 * unit) + xn * (16 * unit) + (zl + inner // unit) % 4 * (4 * unit) + yn * unit + inner % unit
        return (old[:, None] == jnp.arange(width)[None, :]).astype(BF16)

    def mirror(x, y, z, c):
        return x, y, 7 - z, c

    def partner(x, y, z, c):
        return x, y, z, 1 - c

    conv_piece = lax.dynamic_slice_in_dim(conv_weight, (xi * 4 + yi) % 8 * piece, piece, 1)
    point_piece = lax.dynamic_slice(point_weight, (xi * (Hq // 4), yi * Hh), (Hq // 4, Hh))
    holders = [d for d in range(256) if coords(d)[3] == coords(d)[0] // 2]
    conv_piece = send(conv_piece, mirror, holders)
    point_piece = send(point_piece, mirror)
    first, tail = flip(x[:rows * 3 // 8]), x[rows * 3 // 8:]
    x_other = send(x, partner)
    og_other = send(og, partner)
    conv_weight, _ = lax.optimization_barrier((conv_weight, x_other))
    mine, theirs = run(split_kernel, meta, [conv_weight], [shape((3, Cq, Hh), BF16)] * 2)
    conv_piece, point_piece, tail, x_other, og_other, first, mine, theirs = lax.optimization_barrier(
        (conv_piece, point_piece, tail, x_other, og_other, first, mine, theirs)
    )
    got = send(theirs, partner)
    handed = send(columns(conv_piece, 1 - core), partner, holders)
    handed, got = lax.optimization_barrier((handed, got))
    conv_piece = jnp.where(core == xi // 2, columns(conv_piece, core), handed)
    far = jnp.concatenate([conv_piece, point_piece[None]])
    tail, hopped = flip(tail), hop(first)
    fars = [send_a(far, -k) for k in (1, 2, 3)]
    far, first, tail, hopped, *fars = lax.optimization_barrier((far, first, tail, hopped, *fars))
    flipped = jnp.concatenate([first, tail])
    hopped = jnp.concatenate([hopped, hop(tail)])
    far = jnp.stack([far, *fars])
    fars = [far] + [send_b(far, -k) for k in (1, 2, 3)]
    flipped_other = send(flipped, partner)
    spread = order(Cq, Cq // 64, 1)
    taps, ogs, near, arriving, *early = run(
        near_kernel, meta, [flipped, flipped_other, x, x_other, og, og_other, mine, got, point_weight, spread],
        [shape((2, 2 * rows, C), BF16), shape((2 * rows, C), BF16), shape((2 * rows, Hh), F32),
         shape((2 * rows, Hq), F32)] + [shape((2 * Cq, 2 * rows), BF16)] * 4,
    )
    hopped, taps = lax.optimization_barrier((hopped, taps))
    hopped_other = send(hopped, partner)
    tap, near, *late = run(
        late_kernel, meta, [hopped, hopped_other, near, mine, got, spread],
        [shape((2 * rows, C), BF16), shape((2 * rows, Hh), F32)] + [shape((Cq, 2 * rows), BF16)] * 4,
    )
    rest = lax.optimization_barrier((*fars, *early, *late))
    fars, early, late = rest[:4], rest[4:8], rest[8:]
    early = [early[0]] + [send_a(part, k + 1) for k, part in enumerate(early[1:])]
    hg, hidden_t, wfar, *messages = run(
        forward_kernel, meta, [taps, tap, ogs, near, arriving, *fars, order(Hh, Hq // 64, 2), *late],
        [shape((2 * rows, Hh), BF16), shape((Hh, 2 * rows), BF16), shape((3, 16, piece, Hh), BF16)]
        + [shape((Cq + Hh, 2 * rows), BF16)] * 4,
        [pltpu.VMEM((4, 4, Hq // 4, Hh), BF16)],
    )
    for k in (1, 2, 3):
        early[k], messages[k] = lax.optimization_barrier((early[k], messages[k]))
    messages = [messages[0]] + [send_a(part, k + 1) for k, part in enumerate(messages[1:])]
    block = (4, Hh // 4, Hh)
    p_own, *sends = run(point_kernel, meta, [ogs, hidden_t], [shape(block, F32)] + [shape(block, BF16)] * 3)
    hg_flipped, sends[2] = lax.optimization_barrier((flip(hg), sends[2]))
    hg_hopped = hop(hg_flipped)
    p_all = [p_own] + [send_a(part, k + 1) for k, part in enumerate(sends)]
    conv, = run(gradient_kernel, meta, [*early, *messages], [shape((3 * Cq, Hh), F32)])
    n = 12 * (Cq // 16)
    big = (n + Hh // 4, Hh)
    total, *sends = run(pack_kernel, meta, [conv, *p_all], [shape(big, F32)] + [shape(big, BF16)] * 3)
    got_b = [send_b(part, k + 1) for k, part in enumerate(sends)]
    half = big[0] // 8
    by_z, = run(slice_kernel, meta, [total, *got_b], [shape((8, half, Hh), BF16)])
    rings = [[index_of(x, y, z, c) for z in range(8)] for x in range(4) for y in range(4) for c in range(2)]
    by_z = lax.all_to_all(by_z, ("dp", "seq"), 0, 0, axis_index_groups=rings)
    hg_late, by_z = lax.optimization_barrier((hg, by_z))
    mine_rows, other_rows = run(
        input_kernel, meta, [hg_late, hg_flipped, hg_hopped, mine, got, wfar.reshape(3, 2 * Cq, Hh)],
        [shape((rows, C), F32)] * 2,
    )
    in_grad = (og.astype(F32) + mine_rows + send(other_rows, partner)).astype(BF16)
    conv_rows = 3 * (Cq // 64)
    kept, to_core = run(
        split_sum_kernel, meta, [by_z], [shape((half - conv_rows, Hh), F32), shape((conv_rows, Hh), F32)]
    )
    from_core = send(to_core, partner)
    conv_mine, point_mine = run(
        output_kernel, meta, [kept, from_core], [shape((3, Cq // 64, H), F32), shape((Hq // 64, C), F32)]
    )
    return in_grad[None], conv_mine, point_mine


def solution(mesh):
    placed = (P("dp", "seq", None), P("dp", "seq", None), P(None, "dp", None), P("dp", None))
    return jax.shard_map(
        local,
        mesh=mesh,
        in_specs=placed,
        out_specs=(P("dp", "seq", None), P(None, ("dp", "seq"), None), P(("dp", "seq"), None)),
        check_vma=False,
    )
```

```python
import jax
import jax.numpy as jnp
from jax import lax
from jax.experimental import pallas as pl
from jax.experimental.pallas import tpu as pltpu
from jax.sharding import PartitionSpec as P

DILATION_STEP = 1024
BF16 = jnp.bfloat16
F32 = jnp.float32


def coords(index):
    dp, seq = divmod(index, 64)
    return seq // 16, seq % 4, (dp // 2) * 4 + (seq // 4) % 4, dp % 2


def index_of(x, y, z, core):
    return ((z % 8) // 4 * 2 + core % 2) * 64 + (x % 4) * 16 + (z % 4) * 4 + y % 4


def send(value, target, sources=range(256)):
    pairs = [(device, index_of(*target(*coords(device)))) for device in sources]
    return lax.ppermute(value, ("dp", "seq"), pairs)


def send_a(value, steps):
    return send(value, lambda x, y, z, c: (x + steps * (1 - c), y + steps * c, z, c))


def send_b(value, steps):
    return send(value, lambda x, y, z, c: (x + steps * c, y + steps * (1 - c), z, c))


def flip(value):
    return send(value, lambda x, y, z, c: (x, y, z // 4 * 4 + (z + 2) % 4, c))


def hop(value):
    up = [d for d in range(256) if coords(d)[2] % 4 < 2 and coords(d)[0] < 3]
    down = [d for d in range(256) if coords(d)[2] % 4 >= 2 and coords(d)[0] > 0]
    return send(value, lambda x, y, z, c: (x + 1 if z % 4 < 2 else x - 1, y, z, c), up + down)


def dot(left, right, dims):
    return lax.dot_general(left, right, ((dims[:1], dims[1:]), ((), ())), preferred_element_type=F32)


def pick(value, axis, index):
    return lax.dynamic_index_in_dim(value, index, axis, keepdims=False)


def run(kernel, scalars, arrays, outs, scratch=()):
    vmem = pl.BlockSpec(memory_space=pltpu.VMEM)
    return pl.pallas_call(
        kernel,
        out_shape=outs,
        in_specs=[pl.BlockSpec(memory_space=pltpu.SMEM)] + [vmem] * len(arrays),
        out_specs=[vmem] * len(outs),
        scratch_shapes=scratch,
        compiler_params=pltpu.CompilerParams(vmem_limit_bytes=48 * 1024 * 1024),
        cost_estimate=pl.CostEstimate(flops=1, bytes_accessed=1, transcendentals=0),
    )(scalars, *arrays)


def shape(dims, dtype):
    return jax.ShapeDtypeStruct(tuple(dims), dtype)


def lanes(start, size):
    return pl.ds(pl.multiple_of(start * size, size), size)


def split_kernel(meta, weight, mine, theirs):
    size = weight.shape[2] // 4
    for t in range(3):
        value = weight[t]
        parts = [value[:, k * size:(k + 1) * size] for k in range(4)]
        even, odd = jnp.concatenate(parts[::2], 1), jnp.concatenate(parts[1::2], 1)
        first = meta[0] == 0
        mine[t] = jnp.where(first, even, odd)
        theirs[t] = jnp.where(first, odd, even)


def spread_block(meta, block, order, outs, first):
    core, zh = meta[0], meta[1]
    quarter = order.shape[0]
    unit = quarter // 4
    for u in range(2):
        for v in range(2):
            columns = lanes(lax.rem(zh + u, 2) * 2 + lax.rem(core + v, 2), quarter)
            moved = dot(order[...], block[:, columns], (1, 1)).astype(BF16)
            at = first + (u * 2 + v) * unit
            for r, out in enumerate(outs):
                out[at:at + unit] = moved[r * unit:(r + 1) * unit]


def near_kernel(meta, x0, x0o, x1, x1o, og, ogo, mine, got, pw, order, taps, ogs, pre, arriving,
                keep, send1, send2, send3):
    core, zh = meta[0], meta[1]
    rows, quarter = x0.shape[0], mine.shape[1]
    ogs[:rows] = og[...]
    ogs[rows:] = ogo[...]
    total = jnp.zeros(pre.shape, F32)
    for k, (own, other) in enumerate(((x0, x0o), (x1, x1o))):
        taps[k, :rows] = own[...]
        taps[k, rows:] = other[...]
        t = meta[4] if k == 0 else 1
        total += dot(taps[k, :, lanes(zh * 2 + core, quarter)], mine[t], (1, 0))
        total += dot(taps[k, :, lanes(zh * 2 + 1 - core, quarter)], got[t], (1, 0))
    pre[...] = total
    arriving[...] = dot(ogs[...], pw[...], (1, 1))
    outs = (keep, send1, send2, send3)
    for k in range(2):
        spread_block(meta, taps.at[k], order, outs, k * quarter)


def late_kernel(meta, x2, x2o, near, mine, got, order, tap, pre, own, send1, send2, send3):
    core, zh = meta[0], meta[1]
    rows, quarter = x2.shape[0], order.shape[0]
    tap[:rows] = x2[...]
    tap[rows:] = x2o[...]
    t = 2 - meta[4]
    total = near[...] + dot(tap[:, lanes(zh * 2 + core, quarter)], mine[t], (1, 0))
    pre[...] = total + dot(tap[:, lanes(zh * 2 + 1 - core, quarter)], got[t], (1, 0))
    spread_block(meta, tap, order, (own, send1, send2, send3), 0)


def forward_kernel(meta, taps, tap2, ogs, near, arriving, far0, far1, far2, far3, order,
                   x0, x1, x2, x3, hg, hidden_t, wfar, m0, m1, m2, m3, pws):
    core, zh, a, b = (meta[i] for i in range(4))
    piece, width = far0.shape[2:]
    half = 16 * piece
    for j, far in enumerate((far0, far1, far2, far3)):
        for k in range(4):
            ak, bj = lax.rem(a + k, 4), lax.rem(b + j, 4)
            x, y = jnp.where(core == 0, ak, bj), jnp.where(core == 0, bj, ak)
            for t in range(3):
                wfar[t, x * 4 + y] = far[k, t]
            pws[y, x] = far[k, 3]
    pre = near[...]
    for k, t in enumerate((meta[4], 1, 2 - meta[4])):
        columns = lanes(1 - zh, half)
        block = tap2[:, columns] if k == 2 else taps[k, :, columns]
        pre += dot(block, wfar[t].reshape(half, width), (1, 0))
    other = jnp.zeros(arriving.shape, F32)
    for y in range(4):
        other += dot(ogs[:, y * width:(y + 1) * width], pws[y].reshape(4 * piece, width), (1, 1))
    pair = (arriving[...], other)
    grads = jnp.where(zh == 0, jnp.concatenate(pair, 1), jnp.concatenate(pair[::-1], 1))
    scale, cubic = 0.7978845608028654, 0.044715
    square = pre * pre
    tanh = jnp.tanh(scale * (pre + cubic * (square * pre)))
    gate = 0.5 * (1.0 + tanh)
    slope = gate + 0.5 * pre * (1.0 - tanh * tanh) * (scale * (1.0 + 3.0 * cubic * square))
    grads = (grads * slope).astype(BF16)
    hg[...] = grads
    count = x0.shape[0]
    place = [lax.broadcasted_iota(jnp.int32, (width, width), axis) for axis in (0, 1)]
    turned = dot((place[0] == place[1]).astype(BF16), grads, (1, 1)).astype(BF16)
    for x, message in ((x0, m0), (x1, m1), (x2, m2), (x3, m3)):
        message[:count] = x[...]
        message[count:] = turned
    hidden_t[...] = dot(order[...], (pre * gate).astype(BF16), (1, 1)).astype(BF16)


def point_kernel(meta, ogs, hidden_t, own, send1, send2, send3):
    width = own.shape[2]
    unit = hidden_t.shape[0] // 4
    small = unit // 4
    for h in range(ogs.shape[1] // (2 * width)):
        parts = [dot(hidden_t[...], ogs[:, (2 * h + p) * width:(2 * h + p + 1) * width], (1, 0)) for p in range(2)]
        for r, out in enumerate((own, send1, send2, send3)):
            for q in range(4):
                at = r * unit + q * small
                pair = jnp.concatenate([p[at:at + small] for p in parts], 0)
                out[q, h * 2 * small:(h + 1) * 2 * small] = pair.astype(out.dtype)


def gradient_kernel(meta, x0, x1, x2, x3, m0, m1, m2, m3, conv):
    early, width = x0.shape[0], conv.shape[1]
    last = conv.shape[0] - early
    total = [jnp.zeros((size, width), F32) for size in (early, last)]
    for x, m in ((x0, m0), (x1, m1), (x2, m2), (x3, m3)):
        turned = m[last:]
        total[0] += dot(x[...], turned, (1, 1))
        total[1] += dot(m[:last], turned, (1, 1))
    conv[pl.ds(pl.multiple_of(meta[4] * last, last), last)] = total[0][:last]
    conv[last:2 * last] = total[0][last:]
    conv[pl.ds(pl.multiple_of((2 - meta[4]) * last, last), last)] = total[1]


def pack_kernel(meta, conv, p0, p1, p2, p3, own, send1, send2, send3):
    unit = conv.shape[0] // 12
    piece = unit // 4
    for q, out in enumerate((own, send1, send2, send3)):
        for g in range(6):
            at = 2 * g * unit + q * piece
            pair = jnp.concatenate([conv[at:at + piece], conv[at + unit:at + unit + piece]], 0)
            out[g * 2 * piece:(g + 1) * 2 * piece] = pair.astype(out.dtype)
        point = p0[q] + p1[q].astype(F32) + p2[q].astype(F32) + p3[q].astype(F32)
        out[12 * piece:] = point.astype(out.dtype)


def slice_kernel(meta, own, got1, got2, got3, out):
    total = own[...] + got1[...].astype(F32) + got2[...].astype(F32) + got3[...].astype(F32)
    piece = total.shape[0] // 16
    row, thin = piece // 4, piece // 8
    for t in range(4):
        for u in range(2):
            first = [(2 * g + u) * 2 * piece + t * row for g in range(3)]
            parts = [total[at:at + row] for at in first]
            for p in range(4):
                at = (12 + p) * piece + u * piece // 2 + t * thin
                parts.append(total[at:at + thin])
            parts += [total[at + piece:at + piece + row] for at in first]
            z = lax.rem(meta[1] + u, 2) * 4 + lax.rem(meta[5] + t, 4)
            out[z] = jnp.concatenate(parts, 0).astype(out.dtype)


def split_sum_kernel(meta, parts, kept, to_core):
    total = sum(parts[z].astype(F32) for z in range(parts.shape[0]))
    size = kept.shape[0]
    kept[...] = total[:size]
    to_core[...] = total[size:]


def output_kernel(meta, kept, from_core, conv, point):
    here, there = kept[...], from_core[...]
    taps, row = conv.shape[:2]
    width = here.shape[1]
    half = width // 2
    first = meta[0] == 0
    for t in range(taps):
        a, b = here[t * row:(t + 1) * row], there[t * row:(t + 1) * row]
        even, odd = jnp.where(first, a, b), jnp.where(first, b, a)
        conv[t] = jnp.concatenate([even[:, :half], odd[:, :half], even[:, half:], odd[:, half:]], 1)
    thin = point.shape[0]
    for p in range(point.shape[1] // width):
        at = taps * row + p * thin
        point[:, p * width:(p + 1) * width] = here[at:at + thin]


def input_kernel(meta, hg, flipped, hopped, mine, got, wfar, kept, other):
    core, zh = meta[0], meta[1]
    quarter = mine.shape[1]
    rows = kept.shape[0]
    grads = ((flipped[...], 2 - meta[4]), (hg[...], 1), (hopped[...], meta[4]))
    for weights, at, size in ((mine, zh * 2 + core, quarter), (got, zh * 2 + 1 - core, quarter), (wfar, 1 - zh, 2 * quarter)):
        total = sum(dot(grad, weights[t], (1, 1)) for grad, t in grads)
        kept[:, lanes(at, size)] = total[:rows]
        other[:, lanes(at, size)] = total[rows:]


def local(inputs, out_grad, conv_weight, point_weight):
    x, og = inputs[0], out_grad[0]
    rows, C = x.shape
    H = conv_weight.shape[2]
    Cq, Hq, Hh = C // 4, H // 4, H // 2
    piece = C // 32
    assert DILATION_STEP == 8 * rows
    dp, seq = lax.axis_index("dp"), lax.axis_index("seq")
    zh, core = dp // 2, dp % 2
    xi, zl, yi = seq // 16, seq // 4 % 4, seq % 4
    a, b = jnp.where(core == 0, xi, yi), jnp.where(core == 0, yi, xi)
    meta = jnp.stack([core, zh, a, b, jnp.where(zl < 2, 2, 0), zl]).astype(jnp.int32)

    def columns(value, c):
        return jnp.concatenate(
            [lax.dynamic_slice_in_dim(value, half * 2 * Hq + c * Hq, Hq, 2) for half in (0, 1)], axis=2
        )

    def mirror(x, y, z, c):
        return x, y, 7 - z, c

    def partner(x, y, z, c):
        return x, y, z, 1 - c

    def order(width, unit, count):
        new = jnp.arange(width)
        inner = new % (4 * unit)
        u = new // (4 * unit) % count
        r, q = new // (16 * unit * count), new // (4 * unit * count) % 4
        an, bn = (a + r) % 4, (b + q) % 4
        xn, yn = jnp.where(core == 0, an, bn), jnp.where(core == 0, bn, an)
        half = (zh + u) % 2 if count == 2 else 0
        old = half * (64 * unit) + xn * (16 * unit) + (zl + inner // unit) % 4 * (4 * unit) + yn * unit + inner % unit
        return (old[:, None] == jnp.arange(width)[None, :]).astype(BF16)

    def mirror(x, y, z, c):
        return x, y, 7 - z, c

    def partner(x, y, z, c):
        return x, y, z, 1 - c

    conv_piece = lax.dynamic_slice_in_dim(conv_weight, (xi * 4 + yi) % 8 * piece, piece, 1)
    point_piece = lax.dynamic_slice(point_weight, (xi * (Hq // 4), yi * Hh), (Hq // 4, Hh))
    holders = [d for d in range(256) if coords(d)[3] == coords(d)[0] // 2]
    conv_piece = send(conv_piece, mirror, holders)
    point_piece = send(point_piece, mirror)
    first = rows // 2
    flipped = flip(x[:first])
    x_other = send(x, partner)
    og_other = send(og, partner)
    conv_weight, _ = lax.optimization_barrier((conv_weight, x_other))
    mine, theirs = run(split_kernel, meta, [conv_weight], [shape((3, Cq, Hh), BF16)] * 2)
    conv_piece, point_piece, x_late, x_other, og_other, theirs, flipped, mine = lax.optimization_barrier(
        (conv_piece, point_piece, x, x_other, og_other, theirs, flipped, mine)
    )
    got = send(theirs, partner)
    handed = send(columns(conv_piece, 1 - core), partner, holders)
    conv_piece = jnp.where(core == xi // 2, columns(conv_piece, core), handed)
    far = jnp.concatenate([conv_piece, point_piece[None]])
    flipped = jnp.concatenate([flipped, flip(x_late[first:])])
    fars = [send_a(far, -k) for k in (1, 2, 3)]
    far, flipped, got, *fars = lax.optimization_barrier((far, flipped, got, *fars))
    hopped = hop(flipped)
    far = jnp.stack([far, *fars])
    fars = [far] + [send_b(far, -k) for k in (1, 2, 3)]
    flipped_other = send(flipped, partner)
    spread = order(Cq, Cq // 64, 1)
    taps, ogs, near, arriving, *early = run(
        near_kernel, meta, [flipped, flipped_other, x, x_other, og, og_other, mine, got, point_weight, spread],
        [shape((2, 2 * rows, C), BF16), shape((2 * rows, C), BF16), shape((2 * rows, Hh), F32),
         shape((2 * rows, Hq), F32)] + [shape((2 * Cq, 2 * rows), BF16)] * 4,
    )
    hopped, taps = lax.optimization_barrier((hopped, taps))
    hopped_other = send(hopped, partner)
    tap, near, *late = run(
        late_kernel, meta, [hopped, hopped_other, near, mine, got, spread],
        [shape((2 * rows, C), BF16), shape((2 * rows, Hh), F32)] + [shape((Cq, 2 * rows), BF16)] * 4,
    )
    rest = lax.optimization_barrier((*fars, *early, *late))
    fars, early, late = rest[:4], rest[4:8], rest[8:]
    early = [early[0]] + [send_a(part, k + 1) for k, part in enumerate(early[1:])]
    hg, hidden_t, wfar, *messages = run(
        forward_kernel, meta, [taps, tap, ogs, near, arriving, *fars, order(Hh, Hq // 64, 2), *late],
        [shape((2 * rows, Hh), BF16), shape((Hh, 2 * rows), BF16), shape((3, 16, piece, Hh), BF16)]
        + [shape((Cq + Hh, 2 * rows), BF16)] * 4,
        [pltpu.VMEM((4, 4, Hq // 4, Hh), BF16)],
    )
    for k in (1, 2, 3):
        early[k], messages[k] = lax.optimization_barrier((early[k], messages[k]))
    messages = [messages[0]] + [send_a(part, k + 1) for k, part in enumerate(messages[1:])]
    block = (4, Hh // 4, Hh)
    p_own, *sends = run(point_kernel, meta, [ogs, hidden_t], [shape(block, F32)] + [shape(block, BF16)] * 3)
    hg_flipped, sends[2] = lax.optimization_barrier((flip(hg), sends[2]))
    hg_hopped = hop(hg_flipped)
    p_all = [p_own] + [send_a(part, k + 1) for k, part in enumerate(sends)]
    conv, = run(gradient_kernel, meta, [*early, *messages], [shape((3 * Cq, Hh), F32)])
    n = 12 * (Cq // 16)
    big = (n + Hh // 4, Hh)
    total, *sends = run(pack_kernel, meta, [conv, *p_all], [shape(big, F32)] + [shape(big, BF16)] * 3)
    got_b = [send_b(part, k + 1) for k, part in enumerate(sends)]
    half = big[0] // 8
    by_z, = run(slice_kernel, meta, [total, *got_b], [shape((8, half, Hh), BF16)])
    hg_late, hg_hopped, by_z = lax.optimization_barrier((hg, hg_hopped, by_z))
    mine_rows, other_rows = run(
        input_kernel, meta, [hg_late, hg_flipped, hg_hopped, mine, got, wfar.reshape(3, 2 * Cq, Hh)],
        [shape((rows, C), F32)] * 2,
    )
    rings = [[index_of(x, y, z, c) for z in range(8)] for x in range(4) for y in range(4) for c in range(2)]
    by_z = lax.all_to_all(by_z, ("dp", "seq"), 0, 0, axis_index_groups=rings)
    by_z, mine_rows, other_rows = lax.optimization_barrier((by_z, mine_rows, other_rows))
    in_grad = (og.astype(F32) + mine_rows + send(other_rows, partner)).astype(BF16)
    conv_rows = 3 * (Cq // 64)
    kept, to_core = run(
        split_sum_kernel, meta, [by_z], [shape((half - conv_rows, Hh), F32), shape((conv_rows, Hh), F32)]
    )
    from_core = send(to_core, partner)
    conv_mine, point_mine = run(
        output_kernel, meta, [kept, from_core], [shape((3, Cq // 64, H), F32), shape((Hq // 64, C), F32)]
    )
    return in_grad[None], conv_mine, point_mine


def solution(mesh):
    placed = (P("dp", "seq", None), P("dp", "seq", None), P(None, "dp", None), P("dp", None))
    return jax.shard_map(
        local,
        mesh=mesh,
        in_specs=placed,
        out_specs=(P("dp", "seq", None), P(None, ("dp", "seq"), None), P(("dp", "seq"), None)),
        check_vma=False,
    )
```

```python
import jax
import jax.numpy as jnp
from jax import lax
from jax.experimental import pallas as pl
from jax.experimental.pallas import tpu as pltpu
from jax.sharding import PartitionSpec as P

DILATION_STEP = 1024
BF16 = jnp.bfloat16
F32 = jnp.float32


def coords(index):
    dp, seq = divmod(index, 64)
    return seq // 16, seq % 4, (dp // 2) * 4 + (seq // 4) % 4, dp % 2


def index_of(x, y, z, core):
    return ((z % 8) // 4 * 2 + core % 2) * 64 + (x % 4) * 16 + (z % 4) * 4 + y % 4


def send(value, target, sources=range(256)):
    pairs = [(device, index_of(*target(*coords(device)))) for device in sources]
    return lax.ppermute(value, ("dp", "seq"), pairs)


def send_a(value, steps):
    return send(value, lambda x, y, z, c: (x + steps * (1 - c), y + steps * c, z, c))


def send_b(value, steps):
    return send(value, lambda x, y, z, c: (x + steps * c, y + steps * (1 - c), z, c))


def flip(value):
    return send(value, lambda x, y, z, c: (x, y, z // 4 * 4 + (z + 2) % 4, c))


def hop(value):
    up = [d for d in range(256) if coords(d)[2] % 4 < 2 and coords(d)[0] < 3]
    down = [d for d in range(256) if coords(d)[2] % 4 >= 2 and coords(d)[0] > 0]
    return send(value, lambda x, y, z, c: (x + 1 if z % 4 < 2 else x - 1, y, z, c), up + down)


def dot(left, right, dims):
    return lax.dot_general(left, right, ((dims[:1], dims[1:]), ((), ())), preferred_element_type=F32)


def pick(value, axis, index):
    return lax.dynamic_index_in_dim(value, index, axis, keepdims=False)


def run(kernel, scalars, arrays, outs, scratch=()):
    vmem = pl.BlockSpec(memory_space=pltpu.VMEM)
    return pl.pallas_call(
        kernel,
        out_shape=outs,
        in_specs=[pl.BlockSpec(memory_space=pltpu.SMEM)] + [vmem] * len(arrays),
        out_specs=[vmem] * len(outs),
        scratch_shapes=scratch,
        compiler_params=pltpu.CompilerParams(vmem_limit_bytes=16 * 1024 * 1024),
        cost_estimate=pl.CostEstimate(flops=1, bytes_accessed=1, transcendentals=0),
    )(scalars, *arrays)


def shape(dims, dtype):
    return jax.ShapeDtypeStruct(tuple(dims), dtype)


def lanes(start, size):
    return pl.ds(pl.multiple_of(start * size, size), size)


def split_kernel(meta, weight, mine, theirs):
    size = weight.shape[2] // 4
    for t in range(3):
        value = weight[t]
        parts = [value[:, k * size:(k + 1) * size] for k in range(4)]
        even, odd = jnp.concatenate(parts[::2], 1), jnp.concatenate(parts[1::2], 1)
        first = meta[0] == 0
        mine[t] = jnp.where(first, even, odd)
        theirs[t] = jnp.where(first, odd, even)


def spread_block(meta, block, order, outs, first):
    core, zh = meta[0], meta[1]
    quarter = order.shape[0]
    unit = quarter // 4
    for u in range(2):
        for v in range(2):
            columns = lanes(lax.rem(zh + u, 2) * 2 + lax.rem(core + v, 2), quarter)
            moved = dot(order[...], block[:, columns], (1, 1)).astype(BF16)
            at = first + (u * 2 + v) * unit
            for r, out in enumerate(outs):
                out[at:at + unit] = moved[r * unit:(r + 1) * unit]


def near_kernel(meta, x0, x0o, x1, x1o, og, ogo, mine, got, pw, order, taps, ogs, pre, arriving,
                keep, send1, send2, send3):
    core, zh = meta[0], meta[1]
    rows, quarter = x0.shape[0], mine.shape[1]
    ogs[:rows] = og[...]
    ogs[rows:] = ogo[...]
    total = jnp.zeros(pre.shape, F32)
    for k, (own, other) in enumerate(((x0, x0o), (x1, x1o))):
        taps[k, :rows] = own[...]
        taps[k, rows:] = other[...]
        t = meta[4] if k == 0 else 1
        total += dot(taps[k, :, lanes(zh * 2 + core, quarter)], mine[t], (1, 0))
        total += dot(taps[k, :, lanes(zh * 2 + 1 - core, quarter)], got[t], (1, 0))
    pre[...] = total
    arriving[...] = dot(ogs[...], pw[...], (1, 1))
    outs = (keep, send1, send2, send3)
    for k in range(2):
        spread_block(meta, taps.at[k], order, outs, k * quarter)


def late_kernel(meta, x2, x2o, near, mine, got, order, tap, pre, own, send1, send2, send3):
    core, zh = meta[0], meta[1]
    rows, quarter = x2.shape[0], order.shape[0]
    tap[:rows] = x2[...]
    tap[rows:] = x2o[...]
    t = 2 - meta[4]
    total = near[...] + dot(tap[:, lanes(zh * 2 + core, quarter)], mine[t], (1, 0))
    pre[...] = total + dot(tap[:, lanes(zh * 2 + 1 - core, quarter)], got[t], (1, 0))
    spread_block(meta, tap, order, (own, send1, send2, send3), 0)


def forward_kernel(meta, taps, tap2, ogs, near, arriving, far0, far1, far2, far3, order,
                   x0, x1, x2, x3, hg, hidden_t, wfar, m0, m1, m2, m3, pws):
    core, zh, a, b = (meta[i] for i in range(4))
    piece, width = far0.shape[2:]
    half = 16 * piece
    for j, far in enumerate((far0, far1, far2, far3)):
        for k in range(4):
            ak, bj = lax.rem(a + k, 4), lax.rem(b + j, 4)
            x, y = jnp.where(core == 0, ak, bj), jnp.where(core == 0, bj, ak)
            for t in range(3):
                wfar[t, x * 4 + y] = far[k, t]
            pws[y, x] = far[k, 3]
    pre = near[...]
    for k, t in enumerate((meta[4], 1, 2 - meta[4])):
        columns = lanes(1 - zh, half)
        block = tap2[:, columns] if k == 2 else taps[k, :, columns]
        pre += dot(block, wfar[t].reshape(half, width), (1, 0))
    other = jnp.zeros(arriving.shape, F32)
    for y in range(4):
        other += dot(ogs[:, y * width:(y + 1) * width], pws[y].reshape(4 * piece, width), (1, 1))
    pair = (arriving[...], other)
    grads = jnp.where(zh == 0, jnp.concatenate(pair, 1), jnp.concatenate(pair[::-1], 1))
    scale, cubic = 0.7978845608028654, 0.044715
    square = pre * pre
    tanh = jnp.tanh(scale * (pre + cubic * (square * pre)))
    gate = 0.5 * (1.0 + tanh)
    slope = gate + 0.5 * pre * (1.0 - tanh * tanh) * (scale * (1.0 + 3.0 * cubic * square))
    grads = (grads * slope).astype(BF16)
    hg[...] = grads
    count = x0.shape[0]
    place = [lax.broadcasted_iota(jnp.int32, (width, width), axis) for axis in (0, 1)]
    turned = dot((place[0] == place[1]).astype(BF16), grads, (1, 1)).astype(BF16)
    for x, message in ((x0, m0), (x1, m1), (x2, m2), (x3, m3)):
        message[:count] = x[...]
        message[count:] = turned
    hidden_t[...] = dot(order[...], (pre * gate).astype(BF16), (1, 1)).astype(BF16)


def point_kernel(meta, ogs, hidden_t, own, send1, send2, send3):
    width = own.shape[2]
    unit = hidden_t.shape[0] // 4
    small = unit // 4
    for h in range(ogs.shape[1] // (2 * width)):
        parts = [dot(hidden_t[...], ogs[:, (2 * h + p) * width:(2 * h + p + 1) * width], (1, 0)) for p in range(2)]
        for r, out in enumerate((own, send1, send2, send3)):
            for q in range(4):
                at = r * unit + q * small
                pair = jnp.concatenate([p[at:at + small] for p in parts], 0)
                out[q, h * 2 * small:(h + 1) * 2 * small] = pair.astype(out.dtype)


def gradient_kernel(meta, x0, x1, x2, x3, m0, m1, m2, m3, conv):
    early, width = x0.shape[0], conv.shape[1]
    last = conv.shape[0] - early
    total = [jnp.zeros((size, width), F32) for size in (early, last)]
    for x, m in ((x0, m0), (x1, m1), (x2, m2), (x3, m3)):
        turned = m[last:]
        total[0] += dot(x[...], turned, (1, 1))
        total[1] += dot(m[:last], turned, (1, 1))
    conv[pl.ds(pl.multiple_of(meta[4] * last, last), last)] = total[0][:last]
    conv[last:2 * last] = total[0][last:]
    conv[pl.ds(pl.multiple_of((2 - meta[4]) * last, last), last)] = total[1]


def pack_kernel(meta, conv, p0, p1, p2, p3, own, send1, send2, send3):
    unit = conv.shape[0] // 12
    piece = unit // 4
    for q, out in enumerate((own, send1, send2, send3)):
        for g in range(6):
            at = 2 * g * unit + q * piece
            pair = jnp.concatenate([conv[at:at + piece], conv[at + unit:at + unit + piece]], 0)
            out[g * 2 * piece:(g + 1) * 2 * piece] = pair.astype(out.dtype)
        point = p0[q] + p1[q].astype(F32) + p2[q].astype(F32) + p3[q].astype(F32)
        out[12 * piece:] = point.astype(out.dtype)


def slice_kernel(meta, own, got1, got2, got3, out):
    total = own[...] + got1[...].astype(F32) + got2[...].astype(F32) + got3[...].astype(F32)
    piece = total.shape[0] // 16
    row, thin = piece // 4, piece // 8
    for t in range(4):
        for u in range(2):
            first = [(2 * g + u) * 2 * piece + t * row for g in range(3)]
            parts = [total[at:at + row] for at in first]
            for p in range(4):
                at = (12 + p) * piece + u * piece // 2 + t * thin
                parts.append(total[at:at + thin])
            parts += [total[at + piece:at + piece + row] for at in first]
            z = lax.rem(meta[1] + u, 2) * 4 + lax.rem(meta[5] + t, 4)
            out[z] = jnp.concatenate(parts, 0).astype(out.dtype)


def split_sum_kernel(meta, parts, kept, to_core):
    total = sum(parts[z].astype(F32) for z in range(parts.shape[0]))
    size = kept.shape[0]
    kept[...] = total[:size]
    to_core[...] = total[size:]


def output_kernel(meta, kept, from_core, conv, point):
    here, there = kept[...], from_core[...]
    taps, row = conv.shape[:2]
    width = here.shape[1]
    half = width // 2
    first = meta[0] == 0
    for t in range(taps):
        a, b = here[t * row:(t + 1) * row], there[t * row:(t + 1) * row]
        even, odd = jnp.where(first, a, b), jnp.where(first, b, a)
        conv[t] = jnp.concatenate([even[:, :half], odd[:, :half], even[:, half:], odd[:, half:]], 1)
    thin = point.shape[0]
    for p in range(point.shape[1] // width):
        at = taps * row + p * thin
        point[:, p * width:(p + 1) * width] = here[at:at + thin]


def input_kernel(meta, hg, flipped, hopped, mine, got, wfar, kept, other):
    core, zh = meta[0], meta[1]
    quarter = mine.shape[1]
    rows = kept.shape[0]
    grads = ((flipped[...], 2 - meta[4]), (hg[...], 1), (hopped[...], meta[4]))
    for weights, at, size in ((mine, zh * 2 + core, quarter), (got, zh * 2 + 1 - core, quarter), (wfar, 1 - zh, 2 * quarter)):
        total = sum(dot(grad, weights[t], (1, 1)) for grad, t in grads)
        kept[:, lanes(at, size)] = total[:rows]
        other[:, lanes(at, size)] = total[rows:]


def local(inputs, out_grad, conv_weight, point_weight):
    x, og = inputs[0], out_grad[0]
    rows, C = x.shape
    H = conv_weight.shape[2]
    Cq, Hq, Hh = C // 4, H // 4, H // 2
    piece = C // 32
    assert DILATION_STEP == 8 * rows
    dp, seq = lax.axis_index("dp"), lax.axis_index("seq")
    zh, core = dp // 2, dp % 2
    xi, zl, yi = seq // 16, seq // 4 % 4, seq % 4
    a, b = jnp.where(core == 0, xi, yi), jnp.where(core == 0, yi, xi)
    meta = jnp.stack([core, zh, a, b, jnp.where(zl < 2, 2, 0), zl]).astype(jnp.int32)

    def columns(value, c):
        return jnp.concatenate(
            [lax.dynamic_slice_in_dim(value, half * 2 * Hq + c * Hq, Hq, 2) for half in (0, 1)], axis=2
        )

    def mirror(x, y, z, c):
        return x, y, 7 - z, c

    def partner(x, y, z, c):
        return x, y, z, 1 - c

    def order(width, unit, count):
        new = jnp.arange(width)
        inner = new % (4 * unit)
        u = new // (4 * unit) % count
        r, q = new // (16 * unit * count), new // (4 * unit * count) % 4
        an, bn = (a + r) % 4, (b + q) % 4
        xn, yn = jnp.where(core == 0, an, bn), jnp.where(core == 0, bn, an)
        half = (zh + u) % 2 if count == 2 else 0
        old = half * (64 * unit) + xn * (16 * unit) + (zl + inner // unit) % 4 * (4 * unit) + yn * unit + inner % unit
        return (old[:, None] == jnp.arange(width)[None, :]).astype(BF16)

    def mirror(x, y, z, c):
        return x, y, 7 - z, c

    def partner(x, y, z, c):
        return x, y, z, 1 - c

    conv_piece = lax.dynamic_slice_in_dim(conv_weight, (xi * 4 + yi) % 8 * piece, piece, 1)
    point_piece = lax.dynamic_slice(point_weight, (xi * (Hq // 4), yi * Hh), (Hq // 4, Hh))
    holders = [d for d in range(256) if coords(d)[3] == coords(d)[0] // 2]
    conv_piece = send(conv_piece, mirror, holders)
    point_piece = send(point_piece, mirror)
    first = rows // 2
    flipped = flip(x[:first])
    x_other = send(x, partner)
    og_other = send(og, partner)
    conv_weight, _ = lax.optimization_barrier((conv_weight, x_other))
    mine, theirs = run(split_kernel, meta, [conv_weight], [shape((3, Cq, Hh), BF16)] * 2)
    conv_piece, point_piece, x_late, x_other, og_other, theirs, flipped, mine = lax.optimization_barrier(
        (conv_piece, point_piece, x, x_other, og_other, theirs, flipped, mine)
    )
    got = send(theirs, partner)
    handed = send(columns(conv_piece, 1 - core), partner, holders)
    conv_piece = jnp.where(core == xi // 2, columns(conv_piece, core), handed)
    far = jnp.concatenate([conv_piece, point_piece[None]])
    flipped = jnp.concatenate([flipped, flip(x_late[first:])])
    fars = [send_a(far, -k) for k in (1, 2, 3)]
    far, flipped, got, *fars = lax.optimization_barrier((far, flipped, got, *fars))
    hopped = hop(flipped)
    far = jnp.stack([far, *fars])
    fars = [far] + [send_b(far, -k) for k in (1, 2, 3)]
    flipped_other = send(flipped, partner)
    spread = order(Cq, Cq // 64, 1)
    taps, ogs, near, arriving, *early = run(
        near_kernel, meta, [flipped, flipped_other, x, x_other, og, og_other, mine, got, point_weight, spread],
        [shape((2, 2 * rows, C), BF16), shape((2 * rows, C), BF16), shape((2 * rows, Hh), F32),
         shape((2 * rows, Hq), F32)] + [shape((2 * Cq, 2 * rows), BF16)] * 4,
    )
    hopped, taps = lax.optimization_barrier((hopped, taps))
    hopped_other = send(hopped, partner)
    tap, near, *late = run(
        late_kernel, meta, [hopped, hopped_other, near, mine, got, spread],
        [shape((2 * rows, C), BF16), shape((2 * rows, Hh), F32)] + [shape((Cq, 2 * rows), BF16)] * 4,
    )
    rest = lax.optimization_barrier((*fars, *early, *late))
    fars, early, late = rest[:4], rest[4:8], rest[8:]
    early = [early[0]] + [send_a(part, k + 1) for k, part in enumerate(early[1:])]
    hg, hidden_t, wfar, *messages = run(
        forward_kernel, meta, [taps, tap, ogs, near, arriving, *fars, order(Hh, Hq // 64, 2), *late],
        [shape((2 * rows, Hh), BF16), shape((Hh, 2 * rows), BF16), shape((3, 16, piece, Hh), BF16)]
        + [shape((Cq + Hh, 2 * rows), BF16)] * 4,
        [pltpu.VMEM((4, 4, Hq // 4, Hh), BF16)],
    )
    for k in (1, 2, 3):
        early[k], messages[k] = lax.optimization_barrier((early[k], messages[k]))
    messages = [messages[0]] + [send_a(part, k + 1) for k, part in enumerate(messages[1:])]
    block = (4, Hh // 4, Hh)
    p_own, *sends = run(point_kernel, meta, [ogs, hidden_t], [shape(block, F32)] + [shape(block, BF16)] * 3)
    hg_flipped, sends[2] = lax.optimization_barrier((flip(hg), sends[2]))
    hg_hopped = hop(hg_flipped)
    p_all = [p_own] + [send_a(part, k + 1) for k, part in enumerate(sends)]
    conv, = run(gradient_kernel, meta, [*early, *messages], [shape((3 * Cq, Hh), F32)])
    n = 12 * (Cq // 16)
    big = (n + Hh // 4, Hh)
    total, *sends = run(pack_kernel, meta, [conv, *p_all], [shape(big, F32)] + [shape(big, BF16)] * 3)
    got_b = [send_b(part, k + 1) for k, part in enumerate(sends)]
    half = big[0] // 8
    by_z, = run(slice_kernel, meta, [total, *got_b], [shape((8, half, Hh), BF16)])
    hg_late, hg_hopped, by_z = lax.optimization_barrier((hg, hg_hopped, by_z))
    mine_rows, other_rows = run(
        input_kernel, meta, [hg_late, hg_flipped, hg_hopped, mine, got, wfar.reshape(3, 2 * Cq, Hh)],
        [shape((rows, C), F32)] * 2,
    )
    rings = [[index_of(x, y, z, c) for z in range(8)] for x in range(4) for y in range(4) for c in range(2)]
    by_z = lax.all_to_all(by_z, ("dp", "seq"), 0, 0, axis_index_groups=rings)
    by_z, mine_rows, other_rows = lax.optimization_barrier((by_z, mine_rows, other_rows))
    in_grad = (og.astype(F32) + mine_rows + send(other_rows, partner)).astype(BF16)
    conv_rows = 3 * (Cq // 64)
    kept, to_core = run(
        split_sum_kernel, meta, [by_z], [shape((half - conv_rows, Hh), F32), shape((conv_rows, Hh), F32)]
    )
    from_core = send(to_core, partner)
    conv_mine, point_mine = run(
        output_kernel, meta, [kept, from_core], [shape((3, Cq // 64, H), F32), shape((Hq // 64, C), F32)]
    )
    return in_grad[None], conv_mine, point_mine


def solution(mesh):
    placed = (P("dp", "seq", None), P("dp", "seq", None), P(None, "dp", None), P("dp", None))
    return jax.shard_map(
        local,
        mesh=mesh,
        in_specs=placed,
        out_specs=(P("dp", "seq", None), P(None, ("dp", "seq"), None), P(("dp", "seq"), None)),
        check_vma=False,
    )
```

```python
import jax
import jax.numpy as jnp
from jax import lax
from jax.experimental import pallas as pl
from jax.experimental.pallas import tpu as pltpu
from jax.sharding import PartitionSpec as P

DILATION_STEP = 1024
BF16 = jnp.bfloat16
F32 = jnp.float32


def coords(index):
    dp, seq = divmod(index, 64)
    return seq // 16, seq % 4, (dp // 2) * 4 + (seq // 4) % 4, dp % 2


def index_of(x, y, z, core):
    return ((z % 8) // 4 * 2 + core % 2) * 64 + (x % 4) * 16 + (z % 4) * 4 + y % 4


def send(value, target, sources=range(256)):
    pairs = [(device, index_of(*target(*coords(device)))) for device in sources]
    return lax.ppermute(value, ("dp", "seq"), pairs)


def send_a(value, steps):
    return send(value, lambda x, y, z, c: (x + steps * (1 - c), y + steps * c, z, c))


def send_b(value, steps):
    return send(value, lambda x, y, z, c: (x + steps * c, y + steps * (1 - c), z, c))


def flip(value):
    return send(value, lambda x, y, z, c: (x, y, z // 4 * 4 + (z + 2) % 4, c))


def hop(value):
    up = [d for d in range(256) if coords(d)[2] % 4 < 2 and coords(d)[0] < 3]
    down = [d for d in range(256) if coords(d)[2] % 4 >= 2 and coords(d)[0] > 0]
    return send(value, lambda x, y, z, c: (x + 1 if z % 4 < 2 else x - 1, y, z, c), up + down)


def dot(left, right, dims):
    return lax.dot_general(left, right, ((dims[:1], dims[1:]), ((), ())), preferred_element_type=F32)


def pick(value, axis, index):
    return lax.dynamic_index_in_dim(value, index, axis, keepdims=False)


def run(kernel, scalars, arrays, outs, scratch=()):
    vmem = pl.BlockSpec(memory_space=pltpu.VMEM)
    return pl.pallas_call(
        kernel,
        out_shape=outs,
        in_specs=[pl.BlockSpec(memory_space=pltpu.SMEM)] + [vmem] * len(arrays),
        out_specs=[vmem] * len(outs),
        scratch_shapes=scratch,
        compiler_params=pltpu.CompilerParams(vmem_limit_bytes=16 * 1024 * 1024),
        cost_estimate=pl.CostEstimate(flops=1, bytes_accessed=1, transcendentals=0),
    )(scalars, *arrays)


def shape(dims, dtype):
    return jax.ShapeDtypeStruct(tuple(dims), dtype)


def lanes(start, size):
    return pl.ds(pl.multiple_of(start * size, size), size)


def split_kernel(meta, weight, mine, theirs):
    size = weight.shape[2] // 4
    for t in range(3):
        value = weight[t]
        parts = [value[:, k * size:(k + 1) * size] for k in range(4)]
        even, odd = jnp.concatenate(parts[::2], 1), jnp.concatenate(parts[1::2], 1)
        first = meta[0] == 0
        mine[t] = jnp.where(first, even, odd)
        theirs[t] = jnp.where(first, odd, even)


def spread_block(meta, block, order, outs, first):
    core, zh = meta[0], meta[1]
    quarter = order.shape[0]
    unit = quarter // 4
    for u in range(2):
        for v in range(2):
            columns = lanes(lax.rem(zh + u, 2) * 2 + lax.rem(core + v, 2), quarter)
            moved = dot(order[...], block[:, columns], (1, 1)).astype(BF16)
            at = first + (u * 2 + v) * unit
            for r, out in enumerate(outs):
                out[at:at + unit] = moved[r * unit:(r + 1) * unit]


def near_kernel(meta, x0, x0o, x1, x1o, og, ogo, mine, got, pw, order, taps, ogs, pre, arriving,
                keep, send1, send2, send3):
    core, zh = meta[0], meta[1]
    rows, quarter = x0.shape[0], mine.shape[1]
    ogs[:rows] = og[...]
    ogs[rows:] = ogo[...]
    total = jnp.zeros(pre.shape, F32)
    for k, (own, other) in enumerate(((x0, x0o), (x1, x1o))):
        taps[k, :rows] = own[...]
        taps[k, rows:] = other[...]
        t = meta[4] if k == 0 else 1
        total += dot(taps[k, :, lanes(zh * 2 + core, quarter)], mine[t], (1, 0))
        total += dot(taps[k, :, lanes(zh * 2 + 1 - core, quarter)], got[t], (1, 0))
    pre[...] = total
    arriving[...] = dot(ogs[...], pw[...], (1, 1))
    outs = (keep, send1, send2, send3)
    for k in range(2):
        spread_block(meta, taps.at[k], order, outs, k * quarter)


def late_kernel(meta, x2, x2o, near, mine, got, order, tap, pre, own, send1, send2, send3):
    core, zh = meta[0], meta[1]
    rows, quarter = x2.shape[0], order.shape[0]
    tap[:rows] = x2[...]
    tap[rows:] = x2o[...]
    t = 2 - meta[4]
    total = near[...] + dot(tap[:, lanes(zh * 2 + core, quarter)], mine[t], (1, 0))
    pre[...] = total + dot(tap[:, lanes(zh * 2 + 1 - core, quarter)], got[t], (1, 0))
    spread_block(meta, tap, order, (own, send1, send2, send3), 0)


def forward_kernel(meta, taps, tap2, ogs, near, arriving, far0, far1, far2, far3, order,
                   x0, x1, x2, x3, hg, hidden_t, wfar, m0, m1, m2, m3, pws):
    core, zh, a, b = (meta[i] for i in range(4))
    piece, width = far0.shape[2:]
    half = 16 * piece
    for j, far in enumerate((far0, far1, far2, far3)):
        for k in range(4):
            ak, bj = lax.rem(a + k, 4), lax.rem(b + j, 4)
            x, y = jnp.where(core == 0, ak, bj), jnp.where(core == 0, bj, ak)
            for t in range(3):
                wfar[t, x * 4 + y] = far[k, t]
            pws[y, x] = far[k, 3]
    pre = near[...]
    for k, t in enumerate((meta[4], 1, 2 - meta[4])):
        columns = lanes(1 - zh, half)
        block = tap2[:, columns] if k == 2 else taps[k, :, columns]
        pre += dot(block, wfar[t].reshape(half, width), (1, 0))
    other = jnp.zeros(arriving.shape, F32)
    for y in range(4):
        other += dot(ogs[:, y * width:(y + 1) * width], pws[y].reshape(4 * piece, width), (1, 1))
    pair = (arriving[...], other)
    grads = jnp.where(zh == 0, jnp.concatenate(pair, 1), jnp.concatenate(pair[::-1], 1))
    scale, cubic = 0.7978845608028654, 0.044715
    square = pre * pre
    tanh = jnp.tanh(scale * (pre + cubic * (square * pre)))
    gate = 0.5 * (1.0 + tanh)
    slope = gate + 0.5 * pre * (1.0 - tanh * tanh) * (scale * (1.0 + 3.0 * cubic * square))
    grads = (grads * slope).astype(BF16)
    hg[...] = grads
    count = x0.shape[0]
    place = [lax.broadcasted_iota(jnp.int32, (width, width), axis) for axis in (0, 1)]
    turned = dot((place[0] == place[1]).astype(BF16), grads, (1, 1)).astype(BF16)
    for x, message in ((x0, m0), (x1, m1), (x2, m2), (x3, m3)):
        message[:count] = x[...]
        message[count:] = turned
    hidden_t[...] = dot(order[...], (pre * gate).astype(BF16), (1, 1)).astype(BF16)


def point_kernel(meta, ogs, hidden_t, own, send1, send2, send3):
    width = own.shape[2]
    unit = hidden_t.shape[0] // 4
    small = unit // 4
    for h in range(ogs.shape[1] // (2 * width)):
        parts = [dot(hidden_t[...], ogs[:, (2 * h + p) * width:(2 * h + p + 1) * width], (1, 0)) for p in range(2)]
        for r, out in enumerate((own, send1, send2, send3)):
            for q in range(4):
                at = r * unit + q * small
                pair = jnp.concatenate([p[at:at + small] for p in parts], 0)
                out[q, h * 2 * small:(h + 1) * 2 * small] = pair.astype(out.dtype)


def gradient_kernel(meta, x0, x1, x2, x3, m0, m1, m2, m3, conv):
    early, width = x0.shape[0], conv.shape[1]
    last = conv.shape[0] - early
    total = [jnp.zeros((size, width), F32) for size in (early, last)]
    for x, m in ((x0, m0), (x1, m1), (x2, m2), (x3, m3)):
        turned = m[last:]
        total[0] += dot(x[...], turned, (1, 1))
        total[1] += dot(m[:last], turned, (1, 1))
    conv[pl.ds(pl.multiple_of(meta[4] * last, last), last)] = total[0][:last]
    conv[last:2 * last] = total[0][last:]
    conv[pl.ds(pl.multiple_of((2 - meta[4]) * last, last), last)] = total[1]


def pack_kernel(meta, conv, p0, p1, p2, p3, own, send1, send2, send3):
    unit = conv.shape[0] // 12
    piece = unit // 4
    for q, out in enumerate((own, send1, send2, send3)):
        for g in range(6):
            at = 2 * g * unit + q * piece
            pair = jnp.concatenate([conv[at:at + piece], conv[at + unit:at + unit + piece]], 0)
            out[g * 2 * piece:(g + 1) * 2 * piece] = pair.astype(out.dtype)
        point = p0[q] + p1[q].astype(F32) + p2[q].astype(F32) + p3[q].astype(F32)
        out[12 * piece:] = point.astype(out.dtype)


def slice_kernel(meta, own, got1, got2, got3, out):
    total = own[...] + got1[...].astype(F32) + got2[...].astype(F32) + got3[...].astype(F32)
    piece = total.shape[0] // 16
    row, thin = piece // 4, piece // 8
    for t in range(4):
        for u in range(2):
            first = [(2 * g + u) * 2 * piece + t * row for g in range(3)]
            parts = [total[at:at + row] for at in first]
            for p in range(4):
                at = (12 + p) * piece + u * piece // 2 + t * thin
                parts.append(total[at:at + thin])
            parts += [total[at + piece:at + piece + row] for at in first]
            z = lax.rem(meta[1] + u, 2) * 4 + lax.rem(meta[5] + t, 4)
            out[z] = jnp.concatenate(parts, 0).astype(out.dtype)


def split_sum_kernel(meta, parts, kept, to_core):
    total = sum(parts[z].astype(F32) for z in range(parts.shape[0]))
    size = kept.shape[0]
    kept[...] = total[:size]
    to_core[...] = total[size:]


def output_kernel(meta, kept, from_core, conv, point):
    here, there = kept[...], from_core[...]
    taps, row = conv.shape[:2]
    width = here.shape[1]
    half = width // 2
    first = meta[0] == 0
    for t in range(taps):
        a, b = here[t * row:(t + 1) * row], there[t * row:(t + 1) * row]
        even, odd = jnp.where(first, a, b), jnp.where(first, b, a)
        conv[t] = jnp.concatenate([even[:, :half], odd[:, :half], even[:, half:], odd[:, half:]], 1)
    thin = point.shape[0]
    for p in range(point.shape[1] // width):
        at = taps * row + p * thin
        point[:, p * width:(p + 1) * width] = here[at:at + thin]


def input_kernel(meta, hg, flipped, hopped, mine, got, wfar, kept, other):
    core, zh = meta[0], meta[1]
    quarter = mine.shape[1]
    rows = kept.shape[0]
    grads = ((flipped[...], 2 - meta[4]), (hg[...], 1), (hopped[...], meta[4]))
    for weights, at, size in ((mine, zh * 2 + core, quarter), (got, zh * 2 + 1 - core, quarter), (wfar, 1 - zh, 2 * quarter)):
        total = sum(dot(grad, weights[t], (1, 1)) for grad, t in grads)
        kept[:, lanes(at, size)] = total[:rows]
        other[:, lanes(at, size)] = total[rows:]


def local(inputs, out_grad, conv_weight, point_weight):
    x, og = inputs[0], out_grad[0]
    rows, C = x.shape
    H = conv_weight.shape[2]
    Cq, Hq, Hh = C // 4, H // 4, H // 2
    piece = C // 32
    assert DILATION_STEP == 8 * rows
    dp, seq = lax.axis_index("dp"), lax.axis_index("seq")
    zh, core = dp // 2, dp % 2
    xi, zl, yi = seq // 16, seq // 4 % 4, seq % 4
    a, b = jnp.where(core == 0, xi, yi), jnp.where(core == 0, yi, xi)
    meta = jnp.stack([core, zh, a, b, jnp.where(zl < 2, 2, 0), zl]).astype(jnp.int32)

    def columns(value, c):
        return jnp.concatenate(
            [lax.dynamic_slice_in_dim(value, half * 2 * Hq + c * Hq, Hq, 2) for half in (0, 1)], axis=2
        )

    def mirror(x, y, z, c):
        return x, y, 7 - z, c

    def partner(x, y, z, c):
        return x, y, z, 1 - c

    def order(width, unit, count):
        new = jnp.arange(width)
        inner = new % (4 * unit)
        u = new // (4 * unit) % count
        r, q = new // (16 * unit * count), new // (4 * unit * count) % 4
        an, bn = (a + r) % 4, (b + q) % 4
        xn, yn = jnp.where(core == 0, an, bn), jnp.where(core == 0, bn, an)
        half = (zh + u) % 2 if count == 2 else 0
        old = half * (64 * unit) + xn * (16 * unit) + (zl + inner // unit) % 4 * (4 * unit) + yn * unit + inner % unit
        return (old[:, None] == jnp.arange(width)[None, :]).astype(BF16)

    def mirror(x, y, z, c):
        return x, y, 7 - z, c

    def partner(x, y, z, c):
        return x, y, z, 1 - c

    conv_piece = lax.dynamic_slice_in_dim(conv_weight, (xi * 4 + yi) % 8 * piece, piece, 1)
    point_piece = lax.dynamic_slice(point_weight, (xi * (Hq // 4), yi * Hh), (Hq // 4, Hh))
    holders = [d for d in range(256) if coords(d)[3] == coords(d)[0] // 2]
    conv_piece = send(conv_piece, mirror, holders)
    point_piece = send(point_piece, mirror)
    first, tail = flip(x[:rows // 2]), x[rows // 2:]
    x_other = send(x, partner)
    og_other = send(og, partner)
    conv_piece, point_piece, tail, x_other, og_other, first, conv_weight = lax.optimization_barrier(
        (conv_piece, point_piece, tail, x_other, og_other, first, conv_weight)
    )
    mine, theirs = run(split_kernel, meta, [conv_weight], [shape((3, Cq, Hh), BF16)] * 2)
    handed = send(columns(conv_piece, 1 - core), partner, holders)
    conv_piece = jnp.where(core == xi // 2, columns(conv_piece, core), handed)
    far = jnp.concatenate([conv_piece, point_piece[None]])
    tail, hopped = flip(tail), hop(first)
    fars = [send_a(far, -k) for k in (1, 2, 3)]
    far, first, tail, hopped, mine, theirs, *fars = lax.optimization_barrier(
        (far, first, tail, hopped, mine, theirs, *fars)
    )
    flipped = jnp.concatenate([first, tail])
    got = send(theirs, partner)
    hopped = jnp.concatenate([hopped, hop(tail)])
    far = jnp.stack([far, *fars])
    fars = [far] + [send_b(far, -k) for k in (1, 2, 3)]
    flipped, got = lax.optimization_barrier((flipped, got))
    flipped_other = send(flipped, partner)
    spread = order(Cq, Cq // 64, 1)
    taps, ogs, near, arriving, *early = run(
        near_kernel, meta, [flipped, flipped_other, x, x_other, og, og_other, mine, got, point_weight, spread],
        [shape((2, 2 * rows, C), BF16), shape((2 * rows, C), BF16), shape((2 * rows, Hh), F32),
         shape((2 * rows, Hq), F32)] + [shape((2 * Cq, 2 * rows), BF16)] * 4,
    )
    hopped, taps = lax.optimization_barrier((hopped, taps))
    hopped_other = send(hopped, partner)
    tap, near, *late = run(
        late_kernel, meta, [hopped, hopped_other, near, mine, got, spread],
        [shape((2 * rows, C), BF16), shape((2 * rows, Hh), F32)] + [shape((Cq, 2 * rows), BF16)] * 4,
    )
    rest = lax.optimization_barrier((*fars, *early, *late))
    fars, early, late = rest[:4], rest[4:8], rest[8:]
    early = [early[0]] + [send_a(part, k + 1) for k, part in enumerate(early[1:])]
    hg, hidden_t, wfar, *messages = run(
        forward_kernel, meta, [taps, tap, ogs, near, arriving, *fars, order(Hh, Hq // 64, 2), *late],
        [shape((2 * rows, Hh), BF16), shape((Hh, 2 * rows), BF16), shape((3, 16, piece, Hh), BF16)]
        + [shape((Cq + Hh, 2 * rows), BF16)] * 4,
        [pltpu.VMEM((4, 4, Hq // 4, Hh), BF16)],
    )
    for k in (1, 2, 3):
        early[k], messages[k] = lax.optimization_barrier((early[k], messages[k]))
    messages = [messages[0]] + [send_a(part, k + 1) for k, part in enumerate(messages[1:])]
    block = (4, Hh // 4, Hh)
    p_own, *sends = run(point_kernel, meta, [ogs, hidden_t], [shape(block, F32)] + [shape(block, BF16)] * 3)
    hg_flipped, sends[2] = lax.optimization_barrier((flip(hg), sends[2]))
    p_all = [p_own] + [send_a(part, k + 1) for k, part in enumerate(sends)]
    conv, = run(gradient_kernel, meta, [*early, *messages], [shape((3 * Cq, Hh), F32)])
    hg_late, conv = lax.optimization_barrier((hg_flipped, conv))
    hg_hopped = hop(hg_late)
    n = 12 * (Cq // 16)
    big = (n + Hh // 4, Hh)
    total, *sends = run(pack_kernel, meta, [conv, *p_all], [shape(big, F32)] + [shape(big, BF16)] * 3)
    got_b = [send_b(part, k + 1) for k, part in enumerate(sends)]
    half = big[0] // 8
    by_z, = run(slice_kernel, meta, [total, *got_b], [shape((8, half, Hh), BF16)])
    hg_late, by_z = lax.optimization_barrier((hg, by_z))
    mine_rows, other_rows = run(
        input_kernel, meta, [hg_late, hg_flipped, hg_hopped, mine, got, wfar.reshape(3, 2 * Cq, Hh)],
        [shape((rows, C), F32)] * 2,
    )
    in_grad = (og.astype(F32) + mine_rows + send(other_rows, partner)).astype(BF16)
    rings = [[index_of(x, y, z, c) for z in range(8)] for x in range(4) for y in range(4) for c in range(2)]
    by_z = lax.all_to_all(by_z, ("dp", "seq"), 0, 0, axis_index_groups=rings)
    conv_rows = 3 * (Cq // 64)
    kept, to_core = run(
        split_sum_kernel, meta, [by_z], [shape((half - conv_rows, Hh), F32), shape((conv_rows, Hh), F32)]
    )
    in_grad, from_core = lax.optimization_barrier((in_grad, send(to_core, partner)))
    conv_mine, point_mine = run(
        output_kernel, meta, [kept, from_core], [shape((3, Cq // 64, H), F32), shape((Hq // 64, C), F32)]
    )
    return in_grad[None], conv_mine, point_mine


def solution(mesh):
    placed = (P("dp", "seq", None), P("dp", "seq", None), P(None, "dp", None), P("dp", None))
    return jax.shard_map(
        local,
        mesh=mesh,
        in_specs=placed,
        out_specs=(P("dp", "seq", None), P(None, ("dp", "seq"), None), P(("dp", "seq"), None)),
        check_vma=False,
    )
```
